32 devices in a mesh: mol: 8 (over y, x, core), row: 4 (over z).
Axes of the slice: x: 2, y: 2, z: 4, core: 2. Of those that a mesh axis runs over, the one named last changes fastest.
Arguments:
- node_states: bfloat16 [3712, 128], P('mol'), may hold values from -6 to 6
- edge_feats: bfloat16 [65536, 16], P('mol'), may hold values from -6 to 6
- edge_src: int32 [65536], P('mol'), may hold values from 0 to 3711, as said below
- edge_dst: int32 [65536], P('mol'), may hold values from 0 to 3711, as said below
- atom_counts: int32 [128], P('mol'), may hold values from 9 to 29, as said below
- edge_counts: int32 [128], P('mol'), may hold values from 1 to 512, as said below
- mol_group: int32 [128], P('mol'), may hold values from 0 to 1
- col_mask: int32 [2, 16], replicated, may hold values 0 or 1
- cotangent: bfloat16 [3712, 128], P('mol'), may hold values from -6 to 6
- edge_in_state: float32 [3, 16, 128], replicated
- edge_in_bias_state: float32 [3, 128], replicated
- edge_out_state: float32 [3, 128, 16384], P(None, 'mol', 'row')
- edge_out_bias_state: float32 [3, 16384], P(None, 'row')
- gate_in_state: float32 [3, 128, 384], replicated
- gate_hidden_state: float32 [3, 128, 384], replicated
- gate_bias_state: float32 [3, 2, 384], replicated
Outputs:
- states: float32 [3712, 128], P('mol')
- state_grad: float32 [3712, 128], P('mol')
- edge_in_grad: float32 [16, 128], replicated
- edge_in_new: float32 [3, 16, 128], replicated
- edge_in_bias_grad: float32 [128], replicated
- edge_in_bias_new: float32 [3, 128], replicated
- edge_out_grad: float32 [128, 16384], P('mol', 'row')
- edge_out_new: float32 [3, 128, 16384], P(None, 'mol', 'row')
- edge_out_bias_grad: float32 [16384], P('row')
- edge_out_bias_new: float32 [3, 16384], P(None, 'row')
- gate_in_grad: float32 [128, 384], replicated
- gate_in_new: float32 [3, 128, 384], replicated
- gate_hidden_grad: float32 [128, 384], replicated
- gate_hidden_new: float32 [3, 128, 384], replicated
- gate_bias_grad: float32 [2, 384], replicated
- gate_bias_new: float32 [3, 2, 384], replicated
The draws below stay inside these ranges and needn't reach their ends.
Inputs may be any that keep to these rules, and one draw needn't show every extreme that they name: `atom_counts`: each index of mol holds 16 consecutive molecules, and the last of them has 29 atoms. `edge_counts`: molecule k has at most atom_counts[k] * (atom_counts[k] - 1) edges; on each index of mol the last of its molecules has 512 edges. `edge_src`: edge slot k * 512 + j names atom slot k * 29 + a with a < atom_counts[k] when j < edge_counts[k], and k * 29 otherwise. `edge_dst`: as edge_src; a live edge's destination differs from its source.
All inputs are finite; a program needn't handle non-finite values.
Results may differ from the reference program's by a relative error of at most 0.015.
The reference program's roundings to bfloat16 on the way count: a program that leaves them out, or rounds other values in their place, can miss the bound.
Values may be sent and summed in bfloat16 or wider, within the bound.
A program may use at most 64 MiB of HBM per device.

```python
import math
import jax
import jax.numpy as jnp
from jax import lax

F = 16
H = 128
EH = 128
ATOM_CAP = 29
EDGE_CAP = 512
LAYERS = 2
MOL_DEV = 16
MOLS = 128
NODES = 3712
EDGES = 65536
N_ROW = 4


def molecule_plan(key):
    subkeys = jax.random.split(jax.random.fold_in(key, 29), 5)
    atom_count = jax.random.randint(subkeys[0], (MOLS,), ATOM_CAP // 3, ATOM_CAP + 1)
    largest = jnp.arange(MOLS) % MOL_DEV == MOL_DEV - 1
    atom_count = jnp.where(largest, ATOM_CAP, atom_count)
    shortfall = jax.random.randint(subkeys[2], (MOLS,), 0, EDGE_CAP // 8 + 1)
    edge_total = jnp.minimum(jnp.minimum(EDGE_CAP, atom_count * (atom_count - 1)), jnp.maximum(1, atom_count * EDGE_CAP // ATOM_CAP - shortfall))
    edge_total = jnp.where(largest, EDGE_CAP, edge_total)
    source = jax.random.randint(subkeys[3], (MOLS, EDGE_CAP), 0, 1 << 20) % atom_count[:, None]
    slot_ids = jnp.arange(EDGE_CAP)[None, :]
    last_atom = (atom_count - 1)[:, None]
    source = jnp.where(slot_ids == 0, last_atom, source)
    source = jnp.where(slot_ids == 1, 0, source)
    step_on = jax.random.randint(subkeys[4], (MOLS, EDGE_CAP), 0, 1 << 20) % (atom_count[:, None] - 1)
    target = (source + 1 + step_on) % atom_count[:, None]
    target = jnp.where(slot_ids == 1, last_atom, target)
    in_use = slot_ids < edge_total[:, None]
    offset = (jnp.arange(MOLS) * ATOM_CAP)[:, None]
    source = jnp.where(in_use, source, 0) + offset
    target = jnp.where(in_use, target, 0) + offset
    return (atom_count.astype(jnp.int32), edge_total.astype(jnp.int32), source.reshape(-1).astype(jnp.int32), target.reshape(-1).astype(jnp.int32))


def draw_atom_counts(key, part):
    return molecule_plan(key)[0]


def draw_edge_counts(key, part):
    return molecule_plan(key)[1]


def draw_edge_src(key, part):
    return molecule_plan(key)[2]


def draw_edge_dst(key, part):
    return molecule_plan(key)[3]


def stacked_draw(key, shape, spread, moment_size):
    subkeys = jax.random.split(jax.random.fold_in(key, 101), 3)
    weight = jax.random.truncated_normal(subkeys[0], -3.0, 3.0, shape, jnp.float32) * spread
    moment = jax.random.truncated_normal(subkeys[1], -3.0, 3.0, shape, jnp.float32) * moment_size
    average = weight + jax.random.truncated_normal(subkeys[2], -3.0, 3.0, shape, jnp.float32) * (0.3 * spread)
    return jnp.stack([weight, moment, average])


def draw_edge_in_state(key, part):
    key = jax.random.fold_in(key, 11)
    return stacked_draw(key, (F, EH), F ** (-0.5), 0.35 * F ** (-0.5))


def draw_edge_in_bias_state(key, part):
    key = jax.random.fold_in(key, 12)
    return stacked_draw(key, (EH,), 0.3, 0.4 * F ** (-0.5))


def draw_edge_out_state(key, part):
    key = jax.random.fold_in(key, 13)
    return stacked_draw(key, (EH, H * H), (EH * H * 8) ** (-0.5), 0.375 * (EH * H * 8) ** (-0.5))


def draw_edge_out_bias_state(key, part):
    key = jax.random.fold_in(key, 14)
    return stacked_draw(key, (H * H,), 0.3 / (H * 17) ** 0.5, 0.625 * (EH * H * 8) ** (-0.5))


def draw_gate_in_state(key, part):
    key = jax.random.fold_in(key, 15)
    return stacked_draw(key, (H, 3 * H), H ** (-0.5), 0.4 * H ** (-0.5))


def draw_gate_hidden_state(key, part):
    key = jax.random.fold_in(key, 16)
    return stacked_draw(key, (H, 3 * H), H ** (-0.5), 0.4 * H ** (-0.5))


def draw_gate_bias_state(key, part):
    key = jax.random.fold_in(key, 17)
    return stacked_draw(key, (2, 3 * H), 0.1, 0.4 * H ** (-0.5))


def plant(values, key, least, high):
    place = [jax.random.randint(jax.random.fold_in(key, axis), (), 0, length) for axis, length in enumerate(values.shape)]
    longest = values.shape.index(max(values.shape))
    neighbour = place[:longest] + [(place[longest] + 1) % values.shape[longest]] + place[longest + 1:]
    return values.at[tuple(place)].set(least).at[tuple(neighbour)].set(high)


def block_scale(stream_key, extent, shards, least, high):
    level, own = 1.0, jax.random.fold_in(stream_key, 6)
    for axis_at, parts in shards:
        steps = jnp.exp(jax.random.uniform(jax.random.fold_in(own, axis_at), (parts,), jnp.float32, least / len(shards), high / len(shards)))
        level = level * jnp.repeat(steps, extent[axis_at] // parts).reshape([-1 if axis == axis_at else 1 for axis in range(len(extent))])
    return level


def bell_draw(own_key, extent, scale, most, cuts=(), held_as=jnp.bfloat16):
    drawn = jax.random.normal(own_key, extent, jnp.float32) * scale
    if len(cuts) > 0:
        drawn = block_scale(own_key, extent, cuts, -0.22, 0.18) * drawn
    return jnp.clip(drawn, min=-most, max=most).astype(held_as)


def setup_inputs(seed: int = 0) -> dict:
    seeds = jax.random.split(jax.random.key(seed), 17)
    node_states = bell_draw(seeds[0], (NODES, H), 1.0, 6.0, ((0, 8),))
    edge_feats = bell_draw(seeds[1], (EDGES, F), 1.0, 6.0, ((0, 8),))
    edge_src = draw_edge_src(jax.random.fold_in(seeds[16], 71), 0)
    edge_dst = draw_edge_dst(jax.random.fold_in(seeds[16], 71), 0)
    atom_counts = draw_atom_counts(jax.random.fold_in(seeds[16], 71), 0)
    edge_counts = draw_edge_counts(jax.random.fold_in(seeds[16], 71), 0)
    mol_group = plant(jax.random.randint(seeds[6], (MOLS,), 0, 2), jax.random.fold_in(seeds[6], 1), 0, 1).astype(jnp.int32)
    col_mask = plant((jax.random.randint(seeds[7], (2, F), 0, 4) < 3).astype(jnp.int32), jax.random.fold_in(seeds[7], 1), 0, 1)
    cotangent = bell_draw(seeds[8], (NODES, H), 1.0, 6.0, ((0, 8),))
    edge_in_state = draw_edge_in_state(jax.random.fold_in(seeds[16], 71), 0)
    edge_in_bias_state = draw_edge_in_bias_state(jax.random.fold_in(seeds[16], 71), 0)
    edge_out_state = draw_edge_out_state(jax.random.fold_in(seeds[16], 71), 0)
    edge_out_bias_state = draw_edge_out_bias_state(jax.random.fold_in(seeds[16], 71), 0)
    gate_in_state = draw_gate_in_state(jax.random.fold_in(seeds[16], 71), 0)
    gate_hidden_state = draw_gate_hidden_state(jax.random.fold_in(seeds[16], 71), 0)
    gate_bias_state = draw_gate_bias_state(jax.random.fold_in(seeds[16], 71), 0)
    return {"node_states": node_states, "edge_feats": edge_feats, "edge_src": edge_src, "edge_dst": edge_dst, "atom_counts": atom_counts, "edge_counts": edge_counts, "mol_group": mol_group, "col_mask": col_mask, "cotangent": cotangent, "edge_in_state": edge_in_state, "edge_in_bias_state": edge_in_bias_state, "edge_out_state": edge_out_state, "edge_out_bias_state": edge_out_bias_state, "gate_in_state": gate_in_state, "gate_hidden_state": gate_hidden_state, "gate_bias_state": gate_bias_state}


@jax.custom_vjp
def low(v):
    return lax.optimization_barrier(v.astype(jnp.bfloat16)).astype(jnp.float32)

@jax.custom_vjp
def low_back(v):
    return v

def low_keep(v):
    return (low(v), None)

def low_pass(kept, grad):
    return (grad,)

def back_keep(v):
    return (v, None)

def back_low(kept, grad):
    return (low(grad),)
low.defvjp(low_keep, low_pass)
low_back.defvjp(back_keep, back_low)
precise = lax.Precision.HIGHEST
momentum_coef = 0.9
average_decay = 0.9

def matmul_exact(left_side, right_side):
    return jnp.dot(left_side, right_side, precision=precise, preferred_element_type=jnp.float32)

def nesterov_step(stacked, gradient, step_rate):
    scaled = step_rate * gradient
    moment_new = momentum_coef * stacked[1] + scaled
    weight_new = stacked[0] - (scaled + momentum_coef * moment_new)
    average_new = average_decay * stacked[2] + (1.0 - average_decay) * weight_new
    return jnp.stack([weight_new, moment_new, average_new])

def molecule_forward(weights, inputs):
    in_weight, in_bias, out_weight, out_bias, gate_input, gate_hidden, gate_bias = weights
    features, source, target, atom_count, edge_total, node_state = inputs
    slot_ids = jnp.arange(ATOM_CAP)
    in_use = (jnp.arange(EDGE_CAP) < edge_total).astype(jnp.float32)
    node_live = (slot_ids < atom_count).astype(jnp.float32)[:, None]
    from_hot = (source[:, None] == slot_ids[None, :]).astype(jnp.float32)
    to_hot = (target[:, None] == slot_ids[None, :]).astype(jnp.float32) * in_use[:, None]
    pre_act = low_back(matmul_exact(features, in_weight) + in_bias)
    hidden = low(jax.nn.relu(pre_act))
    entries = low_back(low(matmul_exact(hidden, out_weight) + out_bias)).reshape(EDGE_CAP, H, H)
    block_rows = H // N_ROW
    for layer_index in range(LAYERS):
        state_low = low(node_state)
        from_src = matmul_exact(from_hot, state_low)
        blocks = []
        for block_index in range(N_ROW):
            block = entries[:, block_index * block_rows:(block_index + 1) * block_rows, :]
            blocks.append(jnp.einsum('eij,ej->ei', block, low_back(from_src), precision=precise))
        per_edge = low(jnp.concatenate(blocks, axis=1))
        message = low_back(low(jnp.einsum('ea,ei->ai', to_hot, per_edge, precision=precise)))
        from_msg = low_back(matmul_exact(message, gate_input) + gate_bias[0])
        from_state = low_back(matmul_exact(state_low, gate_hidden) + gate_bias[1])
        reset_gate = jax.nn.sigmoid(from_msg[:, :H] + from_state[:, :H])
        update = jax.nn.sigmoid(from_msg[:, H:2 * H] + from_state[:, H:2 * H])
        candidate = jnp.tanh(from_msg[:, 2 * H:] + reset_gate * from_state[:, 2 * H:])
        node_state = node_live * ((1.0 - update) * candidate + update * node_state)
    return node_state

def reference(node_states, edge_feats, edge_src, edge_dst, atom_counts, edge_counts, mol_group, col_mask, cotangent, edge_in_state, edge_in_bias_state, edge_out_state, edge_out_bias_state, gate_in_state, gate_hidden_state, gate_bias_state):
    columns = jnp.where(mol_group[:, None] == 1, col_mask[1][None, :], col_mask[0][None, :]).astype(jnp.float32)
    features = edge_feats.astype(jnp.float32).reshape(MOLS, EDGE_CAP, F) * columns[:, None, :]
    offsets = (jnp.arange(MOLS) * ATOM_CAP).astype(jnp.int32)[:, None]
    source = edge_src.reshape(MOLS, EDGE_CAP) - offsets
    target = edge_dst.reshape(MOLS, EDGE_CAP) - offsets
    masters = (edge_in_state[0], edge_in_bias_state[0], edge_out_state[0], edge_out_bias_state[0], gate_in_state[0], gate_hidden_state[0], gate_bias_state[0])

    def forward(weights, start):
        in_weight, in_bias, out_weight, out_bias, gate_input, gate_hidden, gate_bias = weights
        rounded = (low(in_weight), in_bias, low(out_weight), out_bias, low(gate_input), low(gate_hidden), gate_bias)

        def per_molecule(inputs):
            return molecule_forward(rounded, inputs)
        result = lax.map(jax.checkpoint(per_molecule), (features, source, target, atom_counts, edge_counts, start.reshape(MOLS, ATOM_CAP, H)))
        return result.reshape(NODES, H)
    states, pullback = jax.vjp(forward, masters, node_states.astype(jnp.float32))
    weight_grads, state_grad = pullback(cotangent.astype(jnp.float32))
    in_w_grad, in_b_grad, out_w_grad, out_b_grad, gate_in_grad, gate_hidden_grad, gate_bias_grad = weight_grads
    rate_in = F ** (-0.5) / (0.2 * math.sqrt(EDGES))
    rate_out = (EH * H * 8) ** (-0.5) / (0.4 * math.sqrt(EDGES))
    rate_gate = H ** (-0.5) / (0.5 * math.sqrt(NODES))
    return (states, state_grad, in_w_grad, nesterov_step(edge_in_state, in_w_grad, rate_in), in_b_grad, nesterov_step(edge_in_bias_state, in_b_grad, rate_in), out_w_grad, nesterov_step(edge_out_state, out_w_grad, rate_out), out_b_grad, nesterov_step(edge_out_bias_state, out_b_grad, rate_out), gate_in_grad, nesterov_step(gate_in_state, gate_in_grad, rate_gate), gate_hidden_grad, nesterov_step(gate_hidden_state, gate_hidden_grad, rate_gate), gate_bias_grad, nesterov_step(gate_bias_state, gate_bias_grad, rate_gate))
```

```python
import jax
import jax.numpy as jnp
from jax import lax
from jax.sharding import PartitionSpec as P

LAYERS = 2

momentum_coef = 0.9
average_decay = 0.9


def nesterov_step(stacked, gradient, step_rate):
    scaled = step_rate * gradient
    moment_new = momentum_coef * stacked[1] + scaled
    weight_new = stacked[0] - (scaled + momentum_coef * moment_new)
    average_new = average_decay * stacked[2] + (1.0 - average_decay) * weight_new
    return jnp.stack([weight_new, moment_new, average_new])


def dot32(pattern, *sides):
    return jnp.einsum(pattern, *sides, preferred_element_type=jnp.float32)


def low(value):
    return value.astype(jnp.bfloat16)


def gru_forward(message, node_state, state_low, node_live, gate_in_low, gate_hidden_low, gate_bias):
    width = node_state.shape[1]
    from_msg = dot32("nh,hg->ng", message, gate_in_low) + gate_bias[0]
    from_state = dot32("nh,hg->ng", state_low, gate_hidden_low) + gate_bias[1]
    reset_gate = jax.nn.sigmoid(from_msg[:, :width] + from_state[:, :width])
    update = jax.nn.sigmoid(from_msg[:, width : 2 * width] + from_state[:, width : 2 * width])
    hidden_part = from_state[:, 2 * width :]
    candidate = jnp.tanh(from_msg[:, 2 * width :] + reset_gate * hidden_part)
    new_state = node_live * ((1.0 - update) * candidate + update * node_state)
    return (new_state, (reset_gate, update, candidate, hidden_part))


def gru_backward(upstream, kept_gates, message, node_state, state_low, node_live, gate_in_low, gate_hidden_low):
    reset_gate, update, candidate, hidden_part = kept_gates
    masked = upstream * node_live
    d_cand = masked * (1.0 - update) * (1.0 - candidate * candidate)
    d_update = masked * (node_state - candidate) * update * (1.0 - update)
    d_reset = d_cand * hidden_part * reset_gate * (1.0 - reset_gate)
    msg_side = low(jnp.concatenate([d_reset, d_update, d_cand], axis=1))
    state_side = low(jnp.concatenate([d_reset, d_update, d_cand * reset_gate], axis=1))
    in_grad = dot32("nh,ng->hg", message, msg_side)
    hidden_grad = dot32("nh,ng->hg", state_low, state_side)
    bias_grad = jnp.stack(
        [
            jnp.sum(msg_side.astype(jnp.float32), axis=0),
            jnp.sum(state_side.astype(jnp.float32), axis=0),
        ]
    )
    d_message = low(dot32("ng,hg->nh", msg_side, gate_in_low))
    d_state = masked * update + dot32("ng,hg->nh", state_side, gate_hidden_low)
    return (d_message, d_state, in_grad, hidden_grad, bias_grad)


def per_device(
    node_states,
    edge_feats,
    edge_src,
    edge_dst,
    atom_counts,
    edge_counts,
    mol_group,
    col_mask,
    cotangent,
    edge_in_state,
    edge_in_bias_state,
    edge_out_state,
    edge_out_bias_state,
    gate_in_state,
    gate_hidden_state,
    gate_bias_state,
):
    mol_here = atom_counts.shape[0]
    node_here, width = node_states.shape
    atom_cap = node_here // mol_here
    edge_cap = edge_feats.shape[0] // mol_here
    rows_here = edge_out_bias_state.shape[1] // width
    row_start = lax.axis_index("row") * rows_here
    offsets = (lax.axis_index("mol") * node_here + jnp.arange(mol_here) * atom_cap)[:, None]
    source = edge_src.reshape(mol_here, edge_cap) - offsets
    target = edge_dst.reshape(mol_here, edge_cap) - offsets
    in_use = jnp.arange(edge_cap)[None, :] < edge_counts[:, None]
    pair = jnp.where(in_use, source * atom_cap + target, -1)
    pair_hot = low(pair[:, :, None] == jnp.arange(atom_cap * atom_cap)[None, None, :])
    columns = low(jnp.where(mol_group[:, None] == 1, col_mask[1][None, :], col_mask[0][None, :]))
    features = edge_feats.reshape(mol_here, edge_cap, -1) * columns[:, None, :]
    node_live = (
        (jnp.arange(atom_cap)[None, :] < atom_counts[:, None]).astype(jnp.float32).reshape(node_here, 1)
    )
    in_low = low(edge_in_state[0])
    out_low = lax.all_gather(low(edge_out_state[0]), "mol", axis=0, tiled=True)
    out_low = out_low.reshape(-1, rows_here, width)
    out_bias = low(edge_out_bias_state[0]).reshape(rows_here, width)
    gate_in_low = low(gate_in_state[0])
    gate_hidden_low = low(gate_hidden_state[0])
    gate_bias = gate_bias_state[0]

    pre_act = dot32("mef,fk->mek", features, in_low) + edge_in_bias_state[0]
    hidden = low(jax.nn.relu(pre_act))
    pair_sum = low(dot32("mep,mek->mpk", pair_hot, hidden)).reshape(
        mol_here, atom_cap, atom_cap, -1
    )
    pair_count = low(jnp.sum(pair_hot.astype(jnp.float32), axis=1)).reshape(
        mol_here, atom_cap, atom_cap
    )

    node_state = node_states.astype(jnp.float32)
    kept_layers = []
    for layer_index in range(LAYERS):
        state_low = low(node_state)
        by_mol = state_low.reshape(mol_here, atom_cap, width)
        spread = low(dot32("mwj,kij->mwik", by_mol, out_low))
        spread_bias = low(dot32("mwj,ij->mwi", by_mol, out_bias))
        piece = dot32("mwvk,mwik->mvi", pair_sum, spread) + dot32(
            "mwv,mwi->mvi", pair_count, spread_bias
        )
        message = lax.all_gather(
            low(piece).reshape(node_here, rows_here), "row", axis=1, tiled=True
        )
        new_state, kept_gates = gru_forward(
            message, node_state, state_low, node_live, gate_in_low, gate_hidden_low, gate_bias
        )
        kept_layers.append((node_state, state_low, message, kept_gates, spread))
        node_state = new_state
    upstream = cotangent.astype(jnp.float32)
    gate_in_grad = gate_hidden_grad = gate_bias_grad = 0.0
    out_weight_grad = out_bias_grad = pair_grad = 0.0
    for layer_index in reversed(range(LAYERS)):
        prev_state, prev_low, message, kept_gates, spread = kept_layers[layer_index]
        d_message, d_state, layer_in, layer_hidden, layer_bias = gru_backward(
            upstream, kept_gates, message, prev_state, prev_low, node_live, gate_in_low, gate_hidden_low
        )
        gate_in_grad = gate_in_grad + layer_in
        gate_hidden_grad = gate_hidden_grad + layer_hidden
        gate_bias_grad = gate_bias_grad + layer_bias
        by_mol = prev_low.reshape(mol_here, atom_cap, width)
        rows_grad = lax.dynamic_slice_in_dim(d_message, row_start, rows_here, 1).reshape(
            mol_here, atom_cap, rows_here
        )
        gathered = low(dot32("mwvk,mvi->mwik", pair_sum, rows_grad))
        gathered_bias = low(dot32("mwv,mvi->mwi", pair_count, rows_grad))
        back = dot32("mwik,kij->mwj", gathered, out_low) + dot32(
            "mwi,ij->mwj", gathered_bias, out_bias
        )
        upstream = d_state + lax.psum(low(back).reshape(node_here, width), "row").astype(
            jnp.float32
        )
        out_weight_grad = out_weight_grad + dot32("mwik,mwj->kij", gathered, by_mol)
        out_bias_grad = out_bias_grad + dot32("mwi,mwj->ij", gathered_bias, by_mol)
        pair_grad = pair_grad + dot32("mvi,mwik->mwvk", rows_grad, spread)
    state_grad = upstream
    hidden_grad = dot32(
        "mep,mpk->mek", pair_hot, low(pair_grad).reshape(mol_here, atom_cap * atom_cap, -1)
    )
    pre_grad = low(jnp.where(pre_act > 0, hidden_grad, 0.0))
    in_weight_grad = dot32("mef,mek->fk", features, pre_grad)
    in_bias_grad = jnp.sum(pre_grad.astype(jnp.float32), axis=(0, 1))

    out_rows = lax.psum_scatter(
        low(out_weight_grad.reshape(out_low.shape[0], -1)), "mol", scatter_dimension=0, tiled=True
    ).astype(jnp.float32)
    out_bias_total, gate_in_total, gate_hidden_total, gate_bias_total = (
        lax.psum(low(part), "mol").astype(jnp.float32)
        for part in (out_bias_grad.reshape(-1), gate_in_grad, gate_hidden_grad, gate_bias_grad)
    )
    in_weight_total, in_bias_total = lax.psum((in_weight_grad, in_bias_grad), ("mol", "row"))
    edges_all = edge_feats.shape[0] * lax.axis_size("mol")
    nodes_all = node_here * lax.axis_size("mol")
    feat_width = edge_feats.shape[1]
    edge_hidden = edge_in_state.shape[2]
    rate_in = feat_width ** (-0.5) / (0.2 * edges_all**0.5)
    rate_out = (edge_hidden * width * 8) ** (-0.5) / (0.4 * edges_all**0.5)
    rate_gate = width ** (-0.5) / (0.5 * nodes_all**0.5)
    return (
        node_state,
        state_grad,
        in_weight_total,
        nesterov_step(edge_in_state, in_weight_total, rate_in),
        in_bias_total,
        nesterov_step(edge_in_bias_state, in_bias_total, rate_in),
        out_rows,
        nesterov_step(edge_out_state, out_rows, rate_out),
        out_bias_total,
        nesterov_step(edge_out_bias_state, out_bias_total, rate_out),
        gate_in_total,
        nesterov_step(gate_in_state, gate_in_total, rate_gate),
        gate_hidden_total,
        nesterov_step(gate_hidden_state, gate_hidden_total, rate_gate),
        gate_bias_total,
        nesterov_step(gate_bias_state, gate_bias_total, rate_gate),
    )


def solution(mesh):
    return jax.shard_map(
        per_device,
        mesh=mesh,
        in_specs=(
            P("mol", None),
            P("mol", None),
            P("mol"),
            P("mol"),
            P("mol"),
            P("mol"),
            P("mol"),
            P(),
            P("mol", None),
            P(),
            P(),
            P(None, "mol", "row"),
            P(None, "row"),
            P(),
            P(),
            P(),
        ),
        out_specs=(
            P("mol", None),
            P("mol", None),
            P(),
            P(),
            P(),
            P(),
            P("mol", "row"),
            P(None, "mol", "row"),
            P("row"),
            P(None, "row"),
            P(),
            P(),
            P(),
            P(),
            P(),
            P(),
        ),
        check_vma=False,
    )
```

```python
import functools
from typing import Any, NamedTuple

import jax
import jax.numpy as jnp
import numpy as np
from jax import lax
from jax.experimental import pallas as pl
from jax.experimental.pallas import tpu as pltpu
from jax.sharding import PartitionSpec as P

LAYERS = 2
HALF = 8
LANES = 128
PARTS = 2
MOL, ROW = "mol", "row"
MESH = pl.DeviceIdType.MESH
VMEM_BYTES = 58 * 1024 * 1024

momentum_coef = 0.9
average_decay = 0.9
f32 = jnp.float32
bf16 = jnp.bfloat16


def dot(left, right):
    return lax.dot_general(left, right, (((1,), (0,)), ((), ())), preferred_element_type=f32)


def dot_nt(left, right):
    return lax.dot_general(left, right, (((1,), (1,)), ((), ())), preferred_element_type=f32)


def dot_tn(left, right):
    return lax.dot_general(left, right, (((0,), (0,)), ((), ())), preferred_element_type=f32)


def low(value):
    return value.astype(bf16)


def iota(shape, axis):
    return lax.broadcasted_iota(jnp.int32, shape, axis)


def hot(mask):
    return low(jnp.where(mask, 1.0, 0.0))


class Sizes:
    def __init__(self, mesh, node_states, edge_feats, atom_counts, edge_in_state, edge_out_bias_state):
        self.n_mol, self.n_row = mesh.shape["mol"], mesh.shape["row"]
        self.mols = atom_counts.shape[0]
        self.nodes, self.width = node_states.shape
        self.cap = self.nodes // self.mols
        self.edges = edge_feats.shape[0] // self.mols
        self.feats = edge_feats.shape[1]
        self.units = edge_in_state.shape[2]
        self.rows = edge_out_bias_state.shape[1] // self.width
        self.per = self.units // self.n_mol
        self.halves = self.mols // HALF
        self.vpad = 32
        self.wpad = self.cap + self.cap % 2
        self.lanes = self.mols * self.vpad
        self.half_lanes = HALF * self.vpad
        self.half_rows = HALF * self.wpad
        self.span = self.wpad * self.units
        self.fused = self.per % 16 == 0
        self.gate_rows = 6 * self.width
        self.small_rows = self.gate_rows + 16 + self.rows
        self.chunk = -(-self.small_rows // (16 * self.n_mol)) * 16


class Operands(NamedTuple):
    nodes: Any
    feats_t: Any
    src: Any
    dst: Any
    atoms: Any
    edges: Any
    group: Any
    col_mask: Any
    cot: Any
    w1: Any
    b1: Any
    w2: Any
    b2: Any
    wi: Any
    wh: Any
    bg: Any
    perm_in_c: Any
    perm_c: Any


class Results(NamedTuple):
    states: Any
    state_grad: Any
    out_rows: Any
    small_out: Any
    w1_out: Any


class Scratch(NamedTuple):
    nodes_v: Any
    feats_v: Any
    src_v: Any
    dst_v: Any
    cot_v: Any
    w2_v: Any
    wi_v: Any
    wh_v: Any
    perm_in: Any
    perm: Any
    w2s: Any
    w2t: Any
    stage: Any
    hid: Any
    idx: Any
    s2: Any
    counts: Any
    cnt: Any
    t2: Any
    d2: Any
    e2: Any
    e_acc: Any
    dw_acc: Any
    ob_acc: Any
    live: Any
    h: Any
    hb: Any
    hbw: Any
    hbw_t: Any
    gates: Any
    mt: Any
    dmt: Any
    dmn: Any
    dm: Any
    dgi: Any
    dgh: Any
    wib: Any
    whb: Any
    wit: Any
    wht: Any
    bcol: Any
    gt: Any
    spart: Any
    rs_in: Any
    sred: Any
    dwp: Any
    dw_in: Any
    dw_mid: Any
    dw_in2: Any
    sm_part: Any
    sm_in: Any
    sm_red: Any
    w1_part: Any
    w1_in: Any
    w1_mid: Any
    w1_in2: Any
    col_mask_v: Any
    w1_v: Any
    b1_v: Any
    bg_v: Any
    b2_v: Any
    group_s: Any
    edges_s: Any
    atoms_s: Any
    states_v: Any
    state_grad_v: Any
    out_rows_v: Any
    lsem: Any
    osem: Any
    w2_send: Any
    w2_recv: Any
    w2_fsend: Any
    m_send: Any
    m_recv: Any
    rs_send: Any
    rs_recv: Any
    ag_send: Any
    ag_recv: Any
    dw_send: Any
    dw_recv: Any
    dw2_send: Any
    dw2_recv: Any
    sm_send: Any
    sm_recv: Any
    sa_send: Any
    sa_recv: Any
    wr_send: Any
    wr_recv: Any
    wm_send: Any
    wm_recv: Any


def step_kernel(z, *refs):
    n_in, n_out = len(Operands._fields), len(Results._fields)
    a = Operands(*refs[:n_in])
    o = Results(*refs[n_in : n_in + n_out])
    r = Scratch(*refs[n_in + n_out :])
    atoms, edges, group = r.atoms_s, r.edges_s, r.group_s
    me, row = lax.axis_index(MOL), lax.axis_index(ROW)
    n_mol, n_row, rows, units, per = z.n_mol, z.n_row, z.rows, z.units, z.per
    width, halves = z.width, range(z.halves)
    row_at = pl.multiple_of(row * rows, rows)

    def others(index, count):
        return [lax.rem(index + step, count) for step in range(1, count)]

    mol_peers, row_peers = others(me, n_mol), others(row, n_row)

    def remote(source, target, send, recv, axis, device):
        return pltpu.make_async_remote_copy(
            src_ref=source,
            dst_ref=target,
            send_sem=send,
            recv_sem=recv,
            device_id={axis: device},
            device_id_type=MESH,
        )

    sent, stored = [], []

    def push(*args):
        remote(*args).start()
        sent.append(args)

    def store(source, target):
        pltpu.make_async_copy(source, target, r.osem.at[len(stored)]).start()
        stored.append((source, target))

    def arrived(there, send, recv, axis, device):
        remote(there, there, send, recv, axis, device).wait_recv()

    started = []

    def fetch(source, target):
        copy = pltpu.make_async_copy(source, target, r.lsem.at[len(started)])
        copy.start()
        started.append(copy)
        return copy

    barrier = pltpu.get_barrier_semaphore()
    for peer in mol_peers:
        pl.semaphore_signal(barrier, inc=1, device_id={MOL: peer}, device_id_type=MESH)
    for peer in row_peers:
        pl.semaphore_signal(barrier, inc=1, device_id={ROW: peer}, device_id_type=MESH)
    in_w2 = fetch(a.w2.at[0], r.w2_v) if z.fused else fetch(a.w2, r.w2s)
    in_small = (
        fetch(a.col_mask, r.col_mask_v),
        fetch(a.w1.at[0], r.w1_v),
        fetch(a.b1, r.b1_v),
        fetch(a.group, r.group_s),
        fetch(a.edges, r.edges_s),
        fetch(a.atoms, r.atoms_s),
    )
    in_src, in_dst = fetch(a.src, r.src_v), fetch(a.dst, r.dst_v)
    in_feats, in_nodes = fetch(a.feats_t, r.feats_v), fetch(a.nodes, r.nodes_v)
    in_perms = fetch(a.perm_in_c, r.perm_in), fetch(a.perm_c, r.perm)
    in_wi, in_wh = fetch(a.wi.at[0], r.wi_v), fetch(a.wh.at[0], r.wh_v)
    in_cot = fetch(a.cot, r.cot_v)
    in_bg, in_b2 = fetch(a.bg.at[0], r.bg_v), fetch(a.b2, r.b2_v)

    w2s, stage = r.w2s, r.stage
    partner = me + 1 - 2 * lax.rem(me, 2)
    same = [lax.rem(me + 2 * step, n_mol) for step in range(1, n_mol // 2)]
    same_of_partner = [lax.rem(partner + 2 * step, n_mol) for step in range(1, n_mol // 2)]

    some = rows // PARTS

    def block_of(ref, owner):
        return ref.at[:, pl.ds(pl.multiple_of(owner * per, 16), per), :]

    def part_of(owner, part):
        return w2s.at[pl.ds(part * some, some), pl.ds(pl.multiple_of(owner * per, 16), per), :]

    def forwards(part):
        copies = []
        for at, peer in enumerate(same):
            there, recv = part_of(peer, part), r.w2_recv.at[part, peer]
            copies.append(remote(there, there, r.w2_fsend.at[part, at], recv, MOL, partner))
        return copies

    def forward_part(part):
        for at, (peer, copy) in enumerate(zip(same, forwards(part))):
            there = part_of(peer, part)
            arrived(there, r.w2_send.at[part, at], r.w2_recv.at[part, peer], MOL, peer)
            copy.start()

    def whole_part(part):
        for peer in [partner] + same_of_partner:
            there = part_of(peer, part)
            arrived(there, r.w2_send.at[part, 0], r.w2_recv.at[part, peer], MOL, partner)

    for copy in in_small:
        copy.wait()
    lane_mol = iota((1, z.lanes), 1) // z.vpad
    lane_v = lax.rem(iota((1, z.lanes), 1), z.vpad)
    half_mol = iota((HALF, z.half_lanes), 1) // z.vpad == iota((HALF, z.half_lanes), 0)
    fold = hot(iota((rows, rows * HALF), 1) // HALF == iota((rows, rows * HALF), 0))
    tile_v = hot(lax.rem(iota((z.vpad, z.half_lanes), 1), z.vpad) == iota((z.vpad, z.half_lanes), 0))
    live_to = jnp.zeros((1, z.lanes), jnp.int32)
    for m in range(z.mols):
        live_to = jnp.where(lane_mol == m, atoms[m], live_to)
    live_all = jnp.where(lane_v < live_to, 1.0, 0.0)
    for half in halves:
        lanes = slice(half * z.half_lanes, (half + 1) * z.half_lanes)
        r.live[half] = jnp.broadcast_to(live_all[:, lanes], (8, z.half_lanes))
    r.e_acc[...] = jnp.zeros(r.e_acc.shape, f32)
    r.dw_acc[...] = jnp.zeros(r.dw_acc.shape, f32)
    r.ob_acc[...] = jnp.zeros(r.ob_acc.shape, f32)

    mask_cols = jnp.concatenate(
        [r.col_mask_v[...].astype(f32), jnp.zeros((8 - a.col_mask.shape[0], z.feats), f32)], axis=0
    )
    mask_cols = jnp.concatenate([mask_cols, jnp.zeros((8, LANES - z.feats), f32)], axis=1).T
    masks = [low(jnp.broadcast_to(mask_cols[: z.feats, g : g + 1], (z.feats, z.edges))) for g in (0, 1)]
    w1_low = low(r.w1_v[...])
    b1_row = r.b1_v[0:1, :]

    if z.fused:
        in_w2.wait()
        for i in range(rows):
            stage[i] = low(r.w2_v[:, i * LANES : (i + 1) * LANES])
        w2s[:, pl.ds(pl.multiple_of(me * per, 16), per), :] = stage[...]
    pl.semaphore_wait(barrier, n_mol - 1 + n_row - 1)
    if z.fused:
        for part in range(PARTS):
            for at, peer in enumerate(same + [partner]):
                push(
                    stage.at[pl.ds(part * some, some)],
                    part_of(me, part),
                    r.w2_send.at[part, at],
                    r.w2_recv.at[part, me],
                    MOL,
                    peer,
                )

    s2, hid, idx, counts = r.s2, r.hid, r.idx, r.counts
    for copy in (in_src, in_dst, in_feats):
        copy.wait()
    lines = z.edges // LANES
    edge_at = iota((1, z.edges), 1)
    v_id = low(iota((z.vpad, z.edges), 0).astype(f32))
    one, zero = jnp.ones((), bf16), jnp.zeros((), bf16)

    def pair_hots(ends, count):
        from_all = low(jnp.broadcast_to(ends[0:1], (z.vpad, z.edges)))
        to_all = low(jnp.broadcast_to(ends[1:2], (z.vpad, z.edges)))
        to_hot = jnp.where(to_all == v_id, one, zero)
        from_hot = jnp.where(from_all == v_id, one, zero)
        pair_hot = [
            jnp.where(from_all == jnp.full((), w, bf16), to_hot, zero) for w in range(count)
        ]
        return from_hot, to_hot, jnp.concatenate(pair_hot, axis=0)

    def one_molecule(half, m8):
        m = half * HALF + m8
        at = pl.multiple_of(m * z.edges, z.edges)
        base = (me * z.mols + m) * z.cap
        kept = jnp.where(group[m] == 1, masks[1], masks[0])
        feats_m = r.feats_v[:, pl.ds(at, z.edges)] * kept
        r.feats_v[:, pl.ds(at, z.edges)] = feats_m
        hidden = low(jnp.maximum(dot_tn(feats_m, w1_low) + b1_row, 0.0))
        hid[m] = hidden.T

        def line(ref):
            return jnp.concatenate(
                [ref[pl.ds(m * lines + t, 1), :] for t in range(lines)], axis=1
            )

        from_at = line(r.src_v) - base
        to_at = jnp.where(edge_at < edges[m], line(r.dst_v) - base, 2 * z.vpad)
        ends = jnp.concatenate([from_at, to_at, jnp.zeros((6, z.edges), jnp.int32)], axis=0)
        ends = ends.astype(f32)
        idx[m] = ends
        from_hot, to_hot, pair_hot = pair_hots(ends, z.cap)
        sums = low(dot(pair_hot, hidden))
        for w in range(z.cap):
            s2[half, m8 * z.vpad : (m8 + 1) * z.vpad, w * units : (w + 1) * units] = sums[
                w * z.vpad : (w + 1) * z.vpad
            ]
        found = dot(low(dot_nt(from_hot, to_hot)), tile_v)
        found = jnp.where(iota(found.shape, 1) // z.vpad == m8, found, 0.0)
        counts[half, :, m8 : m8 + 1, :] = found[: z.wpad].reshape(z.wpad, 1, z.half_lanes)

    def half_sums(half, carry):
        s2[half, :, z.cap * units :] = jnp.zeros((z.half_lanes, (z.wpad - z.cap) * units), bf16)
        for m8 in range(HALF):
            if z.fused and m8 == HALF - 2:
                pl.when(half == z.halves - 1)(functools.partial(forward_part, 0))
            one_molecule(half, m8)
        r.cnt[half] = low(counts[half].reshape(z.half_rows, z.half_lanes))
        return carry

    lax.fori_loop(0, z.halves, half_sums, 0)
    if z.fused:
        for part in range(1, PARTS):
            forward_part(part)

    h, hb, hbw, hbw_t = r.h, r.hb, r.hbw, r.hbw_t
    for copy in (in_nodes, *in_perms):
        copy.wait()

    def set_rows(layer, half):
        hb[layer, half] = low(h[layer, half])
        hbw[layer, half] = low(dot_nt(r.perm[...], hb[layer, half]))
        hbw_t[layer, half] = low(dot_nt(hb[layer, half], r.perm[...]))

    def rows_in(value, target):
        moved = dot_tn(value, r.perm_in[...])
        for half in halves:
            target[half] = moved[:, half * z.half_lanes : (half + 1) * z.half_lanes]

    rows_in(r.nodes_v[...], h.at[0])
    for half in halves:
        set_rows(0, half)
    wib, whb, wit, wht, bcol = r.wib, r.whb, r.wit, r.wht, r.bcol
    in_b2.wait()
    b2_low = low(
        jnp.concatenate([r.b2_v[0:1, i * LANES : (i + 1) * LANES] for i in range(rows)], axis=0)
    )

    if not z.fused:
        in_w2.wait()

    t2, mt, gates, w2t = r.t2, r.mt, r.gates, r.w2t

    def two(at):
        return slice(at * 2 * units, (at + 1) * 2 * units)

    def wide(block):
        return jnp.concatenate([block] * (z.half_lanes // LANES), axis=1)

    def spread(layer, half, part):
        state = hbw[layer, half]

        def pair(at):
            ip = part * (some // 2) + at
            both = dot_nt(state, w2s[2 * ip : 2 * ip + 2].reshape(2 * units, width))
            at = ip * 2 * HALF
            for w in range(z.wpad):
                s = slice(w * HALF, (w + 1) * HALF)
                t2[layer, half, pl.ds(at, 2 * HALF), w * units : (w + 1) * units] = low(
                    jnp.concatenate([both[s, :units], both[s, units:]], axis=0)
                )

        for at in range(some // 2):
            pair(at)

    def messages(layer, half):
        state = hbw[layer, half]
        bias = dot(low(dot_nt(b2_low, state)), r.cnt[half])
        full = dot_nt(t2[layer, half], s2[half]).reshape(rows, HALF, z.half_lanes)
        full = jnp.where(half_mol[None], full + bias[:, None, :], 0.0)
        full = low(full.reshape(rows * HALF, z.half_lanes))
        mt[layer, half, pl.ds(row_at, rows), :] = low(dot(fold, full))
        share(mt, r.m_send, r.m_recv, layer, half)

    def row_pushes(ref, send, recv, layer, half):
        mine = ref.at[layer, half, pl.ds(row_at, rows), :]
        return [
            remote(mine, mine, send.at[layer, half, at], recv.at[layer, half, row], ROW, peer)
            for at, peer in enumerate(row_peers)
        ]

    def share(*args):
        for copy in row_pushes(*args):
            copy.start()

    def collect(ref, send, recv, layer, half):
        for peer in row_peers:
            there = ref.at[layer, half, pl.ds(pl.multiple_of(peer * rows, rows), rows), :]
            arrived(there, send.at[layer, half, 0], recv.at[layer, half, peer], ROW, peer)

    def state_side(layer, half):
        gates[layer, half, 0] = dot(wht[...], hb[layer, half]) + wide(bcol[1])

    def gru(layer, half):
        collect(mt, r.m_send, r.m_recv, layer, half)
        from_msg = dot(wit[...], mt[layer, half]) + wide(bcol[0])
        from_state = gates[layer, half, 0]
        reset = jax.nn.sigmoid(from_msg[:width] + from_state[:width])
        update = jax.nn.sigmoid(from_msg[width : 2 * width] + from_state[width : 2 * width])
        new = jnp.tanh(from_msg[2 * width :] + reset * from_state[2 * width :])
        gates[layer, half, 1, :width] = reset
        gates[layer, half, 1, width : 2 * width] = update
        gates[layer, half, 1, 2 * width :] = new
        h[layer + 1, half] = r.live[half, 0:1] * ((1.0 - update) * new + update * h[layer, half])

    gt, dgi, dgh, dm, dmt, dmn = r.gt, r.dgi, r.dgh, r.dm, r.dmt, r.dmn
    d2, spart, sred = r.d2, r.spart, r.sred

    def gru_back(layer, half):
        up = gt[half] * r.live[half, 0:1]
        reset = gates[layer, half, 1, :width]
        update = gates[layer, half, 1, width : 2 * width]
        new = gates[layer, half, 1, 2 * width :]
        d_new = up * (1.0 - update) * (1.0 - new * new)
        d_update = up * (h[layer, half] - new) * update * (1.0 - update)
        d_reset = d_new * gates[layer, half, 0, 2 * width :] * reset * (1.0 - reset)
        msg_side = low(jnp.concatenate([d_reset, d_update, d_new], axis=0))
        dgi[layer, half] = msg_side
        dgh[layer, half, : 2 * width] = msg_side[: 2 * width]
        dgh[layer, half, 2 * width :] = low(d_new * reset)
        part = low(dot(wib[pl.ds(row_at, rows), :], msg_side))
        dm[layer, half] = part
        spread = jnp.where(half_mol[None], part.astype(f32)[:, None, :], 0.0)
        spread = spread.reshape(rows * HALF, z.half_lanes)
        dmt[layer, half] = low(spread)
        dmn[layer, half] = low(spread.T)
        gt[half] = up * update + dot(whb[...], dgh[layer, half])

    def gathered(layer, half):
        def pair(wp):
            lanes = two(wp)
            both = dot(dmt[layer, half], s2[half, :, lanes])
            at = wp * 2 * HALF
            for i in range(rows):
                part = both[i * HALF : (i + 1) * HALF]
                d2[pl.ds(at, 2 * HALF), i * units : (i + 1) * units] = low(
                    jnp.concatenate([part[:, :units], part[:, units:]], axis=0)
                )

        for wp in range(z.wpad // 2):
            pair(wp)

    def bias_rows(layer, half):
        return low(dot_nt(dm[layer, half], r.cnt[half]))

    def state_part(layer, half):
        biases = bias_rows(layer, half)
        r.ob_acc[...] += dot(biases, hbw[layer, half])
        back = dot_nt(w2t[...], d2[...]) + dot_tn(b2_low, biases)
        spart[layer, half] = low(dot(low(back), r.perm[...]))
        for copy in part_pushes(layer, half):
            copy.start()

    def part_pushes(layer, half):
        return [
            remote(
                spart.at[layer, half, pl.ds(pl.multiple_of(peer * rows, rows), rows), :],
                r.rs_in.at[layer, half, row],
                r.rs_send.at[layer, half, at],
                r.rs_recv.at[layer, half, row],
                ROW,
                peer,
            )
            for at, peer in enumerate(row_peers)
        ]

    def state_sum(layer, half):
        total = spart[layer, half, pl.ds(row_at, rows), :].astype(f32)
        for peer in row_peers:
            there = r.rs_in.at[layer, half, peer]
            arrived(there, r.rs_send.at[layer, half, 0], r.rs_recv.at[layer, half, peer], ROW, peer)
            total = total + r.rs_in[layer, half, peer].astype(f32)
        sred[layer, half, pl.ds(row_at, rows), :] = low(total)
        share(sred, r.ag_send, r.ag_recv, layer, half)

    def settle():
        def one_step(t, carry):
            layer, half = lax.div(t, z.halves), lax.rem(t, z.halves)
            for copy in row_pushes(mt, r.m_send, r.m_recv, layer, half):
                copy.wait_send()
            for copy in part_pushes(layer, half):
                copy.wait_send()
            for copy in row_pushes(sred, r.ag_send, r.ag_recv, layer, half):
                copy.wait_send()
            return carry

        lax.fori_loop(0, LAYERS * z.halves, one_step, 0)
        for args in sent:
            remote(*args).wait_send()
        for copy in small_copies():
            copy.wait_send()
        if z.fused:
            for copy in owner_copies():
                copy.wait_send()
            for part in range(PARTS):
                for copy in forwards(part):
                    copy.wait_send()

    def rows_out(value):
        total = None
        for half in halves:
            rest = value(half)
            lanes = slice(half * z.half_lanes, (half + 1) * z.half_lanes)
            for _ in range(3):
                part = low(rest)
                rest = rest - part.astype(f32)
                moved = dot_nt(r.perm_in[:, lanes], part)
                total = moved if total is None else total + moved
        return total

    dwp, dw_acc, e2, e_acc = r.dwp, r.dw_acc, r.e2, r.e_acc

    def weight_grad(layer, half):
        for ip in range(rows // 2):
            at = two(ip)
            dw_acc[:, at] += dot(hbw_t[layer, half], d2[:, at])

    def pair_grad(layer, half):
        for wp in range(z.wpad // 2):
            at = two(wp)
            total = e_acc[half, :, at] + dot(dmn[layer, half], t2[layer, half, :, at])
            e_acc[half, :, at] = total
            e2[half, :, at] = low(total)

    def gate_weights():
        in_wi.wait()
        in_wh.wait()
        wib[...] = low(r.wi_v[...])
        whb[...] = low(r.wh_v[...])
        wit[...] = low(r.wi_v[...].T)
        wht[...] = low(r.wh_v[...].T)
        in_cot.wait()
        in_bg.wait()
        bias_t = jnp.concatenate([r.bg_v[...], jnp.zeros((6, 3 * width), f32)], axis=0).T
        for side in range(2):
            bcol[side] = jnp.broadcast_to(bias_t[:, side : side + 1], (3 * width, LANES))
        rows_in(r.cot_v[...], r.gt)
        for i in range(rows):
            w2t[:, i * units : (i + 1) * units] = w2s[i].T
        for half in halves:
            state_side(0, half)

    def forward_step(t, carry):
        layer, half = lax.div(t, z.halves), lax.rem(t, z.halves)

        @pl.when(layer > 0)
        def _():
            gru(layer - 1, half)
            set_rows(layer, half)

        for part in range(PARTS):
            if z.fused and part > 0:
                pl.when(t == 0)(functools.partial(whole_part, part))
            spread(layer, half, part)
        messages(layer, half)
        pl.when(t == z.halves - 1)(gate_weights)
        pl.when(layer > 0)(functools.partial(state_side, layer, half))
        return carry

    if z.fused:
        whole_part(0)
    lax.fori_loop(0, LAYERS * z.halves, forward_step, 0)

    last = LAYERS - 1

    def back_half(layer, half):
        @pl.when(layer == last)
        def _():
            gru(last, half)

        @pl.when(layer < last)
        def _():
            collect(sred, r.ag_send, r.ag_recv, layer + 1, half)
            gt[half] += sred[layer + 1, half].astype(f32)

        gru_back(layer, half)
        gathered(layer, half)
        state_part(layer, half)
        weight_grad(layer, half)

    def pair_half(layer, half):
        pair_grad(layer, half)

        @pl.when(layer == last)
        def _():
            state_sum(last, half)

    def backward_layer(t, carry):
        layer = last - t
        lax.fori_loop(0, z.halves, lambda half, c: back_half(layer, half) or c, 0)
        lax.fori_loop(0, z.halves, lambda half, c: pair_half(layer, half) or c, 0)

        @pl.when(layer == last)
        def _():
            r.states_v[...] = rows_out(lambda half: h[LAYERS, half])
            store(r.states_v, o.states)

        return carry

    lax.fori_loop(0, LAYERS, backward_layer, 0)

    for i in range(rows):
        dwp[i] = low(dw_acc[:, i * units : (i + 1) * units].T)
    theirs = [lax.rem(partner + 2 * step, n_mol) for step in range(n_mol // 2)]
    ours = [lax.rem(me + 2 * step, n_mol) for step in range(n_mol // 2)]
    if z.fused:
        for at, owner in enumerate(theirs):
            push(block_of(dwp, owner), r.dw_in.at[at], r.dw_send.at[at], r.dw_recv.at[at], MOL, partner)

    sm_part, sm_in, sm_red = r.sm_part, r.sm_in, r.sm_red
    every = [(layer, half) for layer in range(LAYERS) for half in halves]

    def summed(pieces):
        return functools.reduce(jnp.add, pieces)

    def beside(ref):
        return jnp.concatenate([ref[e] for e in every], axis=1)

    for at, (side, grads) in enumerate(((mt, dgi), (hb, dgh))):
        total = dot_nt(beside(side), beside(grads))
        for third in range(3):
            first = (3 * at + third) * width
            sm_part[first : first + width, :] = low(total[:, third * width : (third + 1) * width])
    ones = jnp.ones((8, len(every) * z.half_lanes), bf16)
    bias_lines = []
    for grads in (dgi, dgh):
        total = dot_nt(ones, beside(grads))
        bias_lines += [total[0:1, third * width : (third + 1) * width] for third in range(3)]
    bias_lines.append(jnp.zeros((10, width), f32))
    sm_part[z.gate_rows : z.gate_rows + 16, :] = low(jnp.concatenate(bias_lines, axis=0))
    sm_part[z.gate_rows + 16 : z.small_rows, :] = low(r.ob_acc[...])
    if z.chunk * n_mol > z.small_rows:
        sm_part[z.small_rows :, :] = jnp.zeros((z.chunk * n_mol - z.small_rows, width), bf16)

    def chunk_of(ref, owner):
        return ref.at[pl.ds(pl.multiple_of(owner * z.chunk, 16), z.chunk), :]

    for at, peer in enumerate(mol_peers):
        push(chunk_of(sm_part, peer), sm_in.at[me], r.sm_send.at[at], r.sm_recv.at[me], MOL, peer)

    def owner_copies():
        return [
            remote(r.dw_mid.at[at], r.dw_in2.at[at], r.dw2_send.at[at], r.dw2_recv.at[at], MOL, owner)
            for at, owner in enumerate(ours)
            if at > 0
        ]

    def small_copies():
        mine = chunk_of(sm_red, me)
        return [
            remote(mine, mine, r.sa_send.at[at], r.sa_recv.at[me], MOL, peer)
            for at, peer in enumerate(mol_peers)
        ]

    def between():
        if z.fused:
            for at, owner in enumerate(ours):
                arrived(r.dw_in.at[at], r.dw_send.at[at], r.dw_recv.at[at], MOL, partner)
                own = dwp[:, pl.ds(pl.multiple_of(owner * per, 16), per), :].astype(f32)
                r.dw_mid[at] = low(own + r.dw_in[at].astype(f32))
                if at > 0:
                    owner_copies()[at - 1].start()
        total = sm_part[pl.ds(pl.multiple_of(me * z.chunk, 16), z.chunk), :].astype(f32)
        for peer in mol_peers:
            arrived(sm_in.at[peer], r.sm_send.at[0], r.sm_recv.at[peer], MOL, peer)
            total = total + sm_in[peer].astype(f32)
        sm_red[pl.ds(pl.multiple_of(me * z.chunk, 16), z.chunk), :] = low(total)
        for copy in small_copies():
            copy.start()
        for half in halves:
            state_sum(0, half)

    def edge_grad(half, m8):
        m = half * HALF + m8
        at = pl.multiple_of(m * z.edges, z.edges)
        _, _, pair_hot = pair_hots(idx[m], z.wpad)
        slot = slice(m8 * z.vpad, (m8 + 1) * z.vpad)
        grads = [e2[half, slot, w * units : (w + 1) * units] for w in range(z.wpad)]
        d_hidden = dot_tn(jnp.concatenate(grads, axis=0), pair_hot)
        d_pre = low(jnp.where(hid[m].astype(f32) > 0.0, d_hidden, 0.0))
        feats_m = r.feats_v[:, pl.ds(at, z.edges)]
        feats_m = jnp.concatenate([feats_m, jnp.ones((16, z.edges), bf16)], axis=0)
        return dot_nt(feats_m, d_pre)

    def half_grad(half, total):
        total = total + summed([edge_grad(half, m8) for m8 in range(HALF)])
        pl.when(half == 0)(between)
        return total

    total = lax.fori_loop(0, z.halves, half_grad, jnp.zeros((z.feats + 16, units), f32))
    w1_part, w1_in, w1_mid, w1_in2 = r.w1_part, r.w1_in, r.w1_mid, r.w1_in2
    w1_part[...] = total[: z.feats + 8]
    for at, peer in enumerate(row_peers):
        push(w1_part, w1_in.at[row], r.wr_send.at[at], r.wr_recv.at[row], ROW, peer)
    w1_in[row] = w1_part[...]

    if z.fused:
        total = r.dw_mid[0].astype(f32)
        for at in range(1, n_mol // 2):
            arrived(r.dw_in2.at[at], r.dw2_send.at[at], r.dw2_recv.at[at], MOL, partner)
            total = total + r.dw_in2[at].astype(f32)
        for i in range(rows):
            r.out_rows_v[:, i * LANES : (i + 1) * LANES] = total[i]
        store(r.out_rows_v, o.out_rows)
    else:
        store(dwp, o.out_rows)

    for peer in row_peers:
        arrived(w1_in.at[peer], r.wr_send.at[0], r.wr_recv.at[peer], ROW, peer)
    total = w1_in[0]
    for at in range(1, n_row):
        total = total + w1_in[at]
    w1_mid[...] = total
    for at, peer in enumerate(mol_peers):
        push(w1_mid, w1_in2.at[me], r.wm_send.at[at], r.wm_recv.at[me], MOL, peer)
    w1_in2[me] = w1_mid[...]

    for half in halves:
        collect(sred, r.ag_send, r.ag_recv, 0, half)
    r.state_grad_v[...] = rows_out(lambda half: gt[half] + sred[0, half].astype(f32))
    store(r.state_grad_v, o.state_grad)
    for peer in mol_peers:
        arrived(chunk_of(sm_red, peer), r.sa_send.at[0], r.sa_recv.at[peer], MOL, peer)
    store(sm_red, o.small_out)
    for peer in mol_peers:
        arrived(w1_in2.at[peer], r.wm_send.at[0], r.wm_recv.at[peer], MOL, peer)
    total = w1_in2[0]
    for at in range(1, n_mol):
        total = total + w1_in2[at]
    settle()
    w1_part[...] = total
    store(w1_part, o.w1_out)
    for at, (source, target) in enumerate(stored):
        pltpu.make_async_copy(source, target, r.osem.at[at]).wait()


def run_step(z, args, w2_all):
    (node_states, edge_feats, edge_src, edge_dst, atom_counts, edge_counts, mol_group, col_mask,
     cotangent, edge_in_state, edge_in_bias_state, edge_out_state, edge_out_bias_state,
     gate_in_state, gate_hidden_state, gate_bias_state) = args
    any_spec = pl.BlockSpec(memory_space=pl.ANY)
    v = pltpu.VMEM
    dma = pltpu.SemaphoreType.DMA
    rows, width, units, per = z.rows, z.width, z.units, z.per
    n_mol, n_row, halves = z.n_mol, z.n_row, z.halves
    half_rows, half_lanes = z.half_rows, z.half_lanes
    both = (LAYERS, halves)
    full = rows * HALF
    lines = (z.mols * z.edges // LANES, LANES)
    step_in = (rows, per, LANES)
    lane = np.arange(z.lanes)
    lane_mol, lane_v = lane // z.vpad, lane % z.vpad
    node = np.where(lane_v < z.cap, lane_mol * z.cap + lane_v, -1)
    perm_in = (np.arange(z.nodes)[:, None] == node[None, :]).astype(np.float32)
    row_at = np.arange(half_rows)
    row_lane = (row_at % HALF) * z.vpad + row_at // HALF
    perm = (row_lane[:, None] == np.arange(half_lanes)[None, :]).astype(np.float32)
    operands = Operands(
        nodes=(node_states, any_spec),
        feats_t=(edge_feats.T, any_spec),
        src=(edge_src.reshape(lines), any_spec),
        dst=(edge_dst.reshape(lines), any_spec),
        atoms=(atom_counts, any_spec),
        edges=(edge_counts, any_spec),
        group=(mol_group, any_spec),
        col_mask=(col_mask, any_spec),
        cot=(cotangent, any_spec),
        w1=(edge_in_state, any_spec),
        b1=(edge_in_bias_state, any_spec),
        w2=(edge_out_state if z.fused else w2_all, any_spec),
        b2=(edge_out_bias_state, any_spec),
        wi=(gate_in_state, any_spec),
        wh=(gate_hidden_state, any_spec),
        bg=(gate_bias_state, any_spec),
        perm_in_c=(jnp.asarray(perm_in, bf16), any_spec),
        perm_c=(jnp.asarray(perm, bf16), any_spec),
    )
    outs = [
        jax.ShapeDtypeStruct((z.nodes, width), f32),
        jax.ShapeDtypeStruct((z.nodes, width), f32),
        jax.ShapeDtypeStruct((per, rows * width), f32)
        if z.fused
        else jax.ShapeDtypeStruct((rows, units, width), bf16),
        jax.ShapeDtypeStruct((n_mol * z.chunk, width), bf16),
        jax.ShapeDtypeStruct((z.feats + 8, units), f32),
    ]
    row_sems = dma(both + (n_row,))
    mol_sems = dma((n_mol,))
    scratch = Scratch(
        nodes_v=v((z.nodes, width), bf16),
        feats_v=v((z.feats, z.mols * z.edges), bf16),
        src_v=v(lines, jnp.int32),
        dst_v=v(lines, jnp.int32),
        cot_v=v((z.nodes, width), bf16),
        w2_v=v((per, rows * width), f32),
        wi_v=v((width, 3 * width), f32),
        wh_v=v((width, 3 * width), f32),
        perm_in=v((z.nodes, z.lanes), bf16),
        perm=v((half_rows, half_lanes), bf16),
        w2s=v((rows, units, width), bf16),
        w2t=v((width, rows * units), bf16),
        stage=v(step_in, bf16),
        hid=v((z.mols, units, z.edges), bf16),
        idx=v((z.mols, 8, z.edges), f32),
        s2=v((halves, half_lanes, z.span), bf16),
        counts=v((halves, z.wpad, HALF, half_lanes), f32),
        cnt=v((halves, half_rows, half_lanes), bf16),
        t2=v(both + (full, z.span), bf16),
        d2=v((half_rows, rows * units), bf16),
        e2=v((halves, half_lanes, z.span), bf16),
        e_acc=v((halves, half_lanes, z.span), f32),
        dw_acc=v((width, rows * units), f32),
        ob_acc=v((rows, width), f32),
        live=v((halves, 8, half_lanes), f32),
        h=v((LAYERS + 1, halves, width, half_lanes), f32),
        hb=v(both + (width, half_lanes), bf16),
        hbw=v(both + (half_rows, width), bf16),
        hbw_t=v(both + (width, half_rows), bf16),
        gates=v(both + (2, 3 * width, half_lanes), f32),
        mt=v(both + (width, half_lanes), bf16),
        dmt=v(both + (full, half_lanes), bf16),
        dmn=v(both + (half_lanes, full), bf16),
        dm=v(both + (rows, half_lanes), bf16),
        dgi=v(both + (3 * width, half_lanes), bf16),
        dgh=v(both + (3 * width, half_lanes), bf16),
        wib=v((width, 3 * width), bf16),
        whb=v((width, 3 * width), bf16),
        wit=v((3 * width, width), bf16),
        wht=v((3 * width, width), bf16),
        bcol=v((2, 3 * width, LANES), f32),
        gt=v((halves, width, half_lanes), f32),
        spart=v(both + (width, half_lanes), bf16),
        rs_in=v(both + (n_row, rows, half_lanes), bf16),
        sred=v(both + (width, half_lanes), bf16),
        dwp=v((rows, units, width), bf16),
        dw_in=v((n_mol // 2,) + step_in, bf16),
        dw_mid=v((n_mol // 2,) + step_in, bf16),
        dw_in2=v((n_mol // 2,) + step_in, bf16),
        sm_part=v((n_mol * z.chunk, width), bf16),
        sm_in=v((n_mol, z.chunk, width), bf16),
        sm_red=v((n_mol * z.chunk, width), bf16),
        w1_part=v((z.feats + 8, units), f32),
        w1_in=v((n_row, z.feats + 8, units), f32),
        w1_mid=v((z.feats + 8, units), f32),
        w1_in2=v((n_mol, z.feats + 8, units), f32),
        col_mask_v=v(col_mask.shape, jnp.int32),
        w1_v=v(edge_in_state.shape[1:], f32),
        b1_v=v(edge_in_bias_state.shape, f32),
        bg_v=v(gate_bias_state.shape[1:], f32),
        b2_v=v(edge_out_bias_state.shape, f32),
        group_s=pltpu.SMEM(mol_group.shape, jnp.int32),
        edges_s=pltpu.SMEM(edge_counts.shape, jnp.int32),
        atoms_s=pltpu.SMEM(atom_counts.shape, jnp.int32),
        states_v=v((z.nodes, width), f32),
        state_grad_v=v((z.nodes, width), f32),
        out_rows_v=v((per, rows * width), f32),
        lsem=dma((len(operands),)),
        osem=dma((len(outs),)),
        w2_send=dma((PARTS, n_mol)),
        w2_recv=dma((PARTS, n_mol)),
        w2_fsend=dma((PARTS, n_mol)),
        m_send=row_sems,
        m_recv=row_sems,
        rs_send=row_sems,
        rs_recv=row_sems,
        ag_send=row_sems,
        ag_recv=row_sems,
        dw_send=mol_sems,
        dw_recv=mol_sems,
        dw2_send=mol_sems,
        dw2_recv=mol_sems,
        sm_send=mol_sems,
        sm_recv=mol_sems,
        sa_send=mol_sems,
        sa_recv=mol_sems,
        wr_send=dma((n_row,)),
        wr_recv=dma((n_row,)),
        wm_send=mol_sems,
        wm_recv=mol_sems,
    )
    return pl.pallas_call(
        functools.partial(step_kernel, z),
        out_shape=outs,
        in_specs=[spec for _, spec in operands],
        out_specs=[any_spec] * len(outs),
        scratch_shapes=list(scratch),
        compiler_params=pltpu.CompilerParams(
            collective_id=0, has_side_effects=True, vmem_limit_bytes=VMEM_BYTES
        ),
        name="step",
    )(*[array for array, _ in operands])


def nesterov(state, grad, rate, out):
    scaled = rate * grad
    moment = momentum_coef * state[1] + scaled
    weight = state[0] - (scaled + momentum_coef * moment)
    out[0] = weight
    out[1] = moment
    out[2] = average_decay * state[2] + (1.0 - average_decay) * weight


def nesterov_line(state, grad, rate, out):
    scaled = rate * grad
    moment = momentum_coef * state[1:2, :] + scaled
    weight = state[0:1, :] - (scaled + momentum_coef * moment)
    out[0:1, :] = weight
    out[1:2, :] = moment
    out[2:3, :] = average_decay * state[2:3, :] + (1.0 - average_decay) * weight


class Update(NamedTuple):
    states: Any
    state_grad: Any
    out_rows: Any
    small: Any
    w1_sum: Any
    w1: Any
    b1: Any
    w2: Any
    b2: Any
    wi: Any
    wh: Any
    bg: Any


class Updated(NamedTuple):
    states: Any
    state_grad: Any
    w1_g: Any
    w1_n: Any
    b1_g: Any
    b1_n: Any
    w2_g: Any
    w2_n: Any
    b2_g: Any
    b2_n: Any
    wi_g: Any
    wi_n: Any
    wh_g: Any
    wh_n: Any
    bg_g: Any
    bg_n: Any


def update_kernel(z, rates, *refs):
    n_in, n_out = len(Update._fields), len(Updated._fields)
    given, out = Update(*refs[:n_in]), Updated(*refs[n_in : n_in + n_out])
    refs = refs[n_in + n_out :]
    here, new = Update(*refs[:n_in]), Updated(*refs[n_in : n_in + n_out])
    in_sem, out_sem = refs[n_in + n_out :]
    rate_in, rate_out, rate_gate = rates
    width = z.width
    sent = []

    def send(source, target):
        copy = pltpu.make_async_copy(source, target, out_sem.at[len(sent)])
        copy.start()
        sent.append(copy)

    fetched = Update(
        *[pltpu.make_async_copy(given[at], here[at], in_sem.at[at]) for at in range(n_in)]
    )
    order = (fetched.wi, fetched.small, fetched.wh, fetched.w2, fetched.out_rows)
    passed = (fetched.states, fetched.state_grad)
    rest = (fetched.bg, fetched.b2, fetched.w1, fetched.b1, fetched.w1_sum)
    for copy in order + passed + rest:
        copy.start()

    def thirds(at):
        parts = [here.small[(3 * at + t) * width : (3 * at + t + 1) * width, :] for t in range(3)]
        return jnp.concatenate(parts, axis=1).astype(f32)

    fetched.wi.wait()
    fetched.small.wait()
    total = thirds(0)
    new.wi_g[...] = total
    nesterov(here.wi, total, rate_gate, new.wi_n)
    send(new.wi_g, out.wi_g)
    send(new.wi_n, out.wi_n)
    fetched.wh.wait()
    total = thirds(1)
    new.wh_g[...] = total
    nesterov(here.wh, total, rate_gate, new.wh_n)
    send(new.wh_g, out.wh_g)
    send(new.wh_n, out.wh_n)
    fetched.w2.wait()
    fetched.out_rows.wait()
    send(here.out_rows, out.w2_g)
    nesterov(here.w2, here.out_rows[...], rate_out, new.w2_n)
    send(new.w2_n, out.w2_n)
    for copy in passed + rest:
        copy.wait()
    send(here.states, out.states)
    send(here.state_grad, out.state_grad)
    lines = here.small[z.gate_rows : z.gate_rows + 16, :].astype(f32)
    total = jnp.concatenate(
        [
            jnp.concatenate([lines[3 * side + t : 3 * side + t + 1, :] for t in range(3)], axis=1)
            for side in range(2)
        ],
        axis=0,
    )
    new.bg_g[...] = total
    nesterov(here.bg, total, rate_gate, new.bg_n)
    send(new.bg_g, out.bg_g)
    send(new.bg_n, out.bg_n)
    total = here.small[z.gate_rows + 16 : z.gate_rows + 16 + z.rows, :].astype(f32)
    new.b2_g[...] = total
    total = jnp.concatenate([total[i : i + 1, :] for i in range(z.rows)], axis=1)
    nesterov_line(here.b2, total, rate_out, new.b2_n)
    send(new.b2_g, out.b2_g)
    send(new.b2_n, out.b2_n)
    total = here.w1_sum[: z.feats, :]
    new.w1_g[...] = total
    nesterov(here.w1, total, rate_in, new.w1_n)
    send(new.w1_g, out.w1_g)
    send(new.w1_n, out.w1_n)
    total = here.w1_sum[z.feats : z.feats + 1, :]
    new.b1_g[...] = total
    nesterov_line(here.b1, total, rate_in, new.b1_n)
    send(new.b1_g, out.b1_g)
    send(new.b1_n, out.b1_n)
    for copy in sent:
        copy.wait()


def per_device(mesh, *args):
    (node_states, edge_feats, edge_src, edge_dst, atom_counts, edge_counts, mol_group, col_mask,
     cotangent, edge_in_state, edge_in_bias_state, edge_out_state, edge_out_bias_state,
     gate_in_state, gate_hidden_state, gate_bias_state) = args
    z = Sizes(mesh, node_states, edge_feats, atom_counts, edge_in_state, edge_out_bias_state)
    w2_all = None
    if not z.fused:
        w2_all = lax.all_gather(low(edge_out_state[0]), "mol", axis=0, tiled=True)
        w2_all = w2_all.reshape(z.units, z.rows, z.width).swapaxes(0, 1)
    states, state_grad, out_rows, small, w1_sum = run_step(z, args, w2_all)
    if not z.fused:
        out_rows = out_rows.swapaxes(0, 1).reshape(z.units, z.rows * z.width)
        out_rows = lax.psum_scatter(out_rows, "mol", scatter_dimension=0, tiled=True).astype(f32)
    edges_all = edge_feats.shape[0] * z.n_mol
    nodes_all = z.nodes * z.n_mol
    rates = (
        z.feats ** (-0.5) / (0.2 * edges_all**0.5),
        (z.units * z.width * 8) ** (-0.5) / (0.4 * edges_all**0.5),
        z.width ** (-0.5) / (0.5 * nodes_all**0.5),
    )
    any_spec = pl.BlockSpec(memory_space=pl.ANY)
    operands = [
        states, state_grad, out_rows, small, w1_sum, edge_in_state, edge_in_bias_state,
        edge_out_state, edge_out_bias_state, gate_in_state, gate_hidden_state, gate_bias_state,
    ]
    outs = [
        states.shape, state_grad.shape, (z.feats, z.units), edge_in_state.shape,
        (1, z.units), edge_in_bias_state.shape, out_rows.shape, edge_out_state.shape,
        (z.rows, z.width), edge_out_bias_state.shape, (z.width, 3 * z.width), gate_in_state.shape,
        (z.width, 3 * z.width), gate_hidden_state.shape, (2, 3 * z.width), gate_bias_state.shape,
    ]
    results = pl.pallas_call(
        functools.partial(update_kernel, z, rates),
        out_shape=[jax.ShapeDtypeStruct(shape, f32) for shape in outs],
        in_specs=[any_spec] * len(operands),
        out_specs=[any_spec] * len(outs),
        scratch_shapes=[pltpu.VMEM(array.shape, array.dtype) for array in operands]
        + [pltpu.VMEM(shape, f32) for shape in outs]
        + [pltpu.SemaphoreType.DMA((len(operands),)), pltpu.SemaphoreType.DMA((len(outs),))],
        compiler_params=pltpu.CompilerParams(vmem_limit_bytes=VMEM_BYTES),
        name="update",
    )(*operands)
    results = list(results)
    results[4] = results[4].reshape(-1)
    results[8] = results[8].reshape(-1)
    return tuple(results)


def solution(mesh):
    return jax.shard_map(
        functools.partial(per_device, mesh),
        mesh=mesh,
        in_specs=(
            P(MOL, None),
            P(MOL, None),
            P(MOL),
            P(MOL),
            P(MOL),
            P(MOL),
            P(MOL),
            P(),
            P(MOL, None),
            P(),
            P(),
            P(None, MOL, ROW),
            P(None, ROW),
            P(),
            P(),
            P(),
        ),
        out_specs=(
            P(MOL, None),
            P(MOL, None),
            P(),
            P(),
            P(),
            P(),
            P(MOL, ROW),
            P(None, MOL, ROW),
            P(ROW),
            P(None, ROW),
            P(),
            P(),
            P(),
            P(),
            P(),
            P(),
        ),
        check_vma=False,
    )
```

```python
import functools
from typing import Any, NamedTuple

import jax
import jax.numpy as jnp
import numpy as np
from jax import lax
from jax.experimental import pallas as pl
from jax.experimental.pallas import tpu as pltpu
from jax.sharding import PartitionSpec as P

LAYERS = 2
HALF = 8
LANES = 128
PARTS = 1
MOL, ROW = "mol", "row"
MESH = pl.DeviceIdType.MESH
VMEM_BYTES = 58 * 1024 * 1024

momentum_coef = 0.9
average_decay = 0.9
f32 = jnp.float32
bf16 = jnp.bfloat16


def dot(left, right):
    return lax.dot_general(left, right, (((1,), (0,)), ((), ())), preferred_element_type=f32)


def dot_nt(left, right):
    return lax.dot_general(left, right, (((1,), (1,)), ((), ())), preferred_element_type=f32)


def dot_tn(left, right):
    return lax.dot_general(left, right, (((0,), (0,)), ((), ())), preferred_element_type=f32)


def low(value):
    return value.astype(bf16)


def iota(shape, axis):
    return lax.broadcasted_iota(jnp.int32, shape, axis)


def hot(mask):
    return low(jnp.where(mask, 1.0, 0.0))


class Sizes:
    def __init__(self, mesh, node_states, edge_feats, atom_counts, edge_in_state, edge_out_bias_state):
        self.n_mol, self.n_row = mesh.shape["mol"], mesh.shape["row"]
        self.mols = atom_counts.shape[0]
        self.nodes, self.width = node_states.shape
        self.cap = self.nodes // self.mols
        self.edges = edge_feats.shape[0] // self.mols
        self.feats = edge_feats.shape[1]
        self.units = edge_in_state.shape[2]
        self.rows = edge_out_bias_state.shape[1] // self.width
        self.per = self.units // self.n_mol
        self.halves = self.mols // HALF
        self.vpad = 32
        self.wpad = self.cap + self.cap % 2
        self.lanes = self.mols * self.vpad
        self.half_lanes = HALF * self.vpad
        self.half_rows = HALF * self.wpad
        self.span = self.wpad * self.units
        self.fused = self.per % 16 == 0
        self.gate_rows = 6 * self.width
        self.small_rows = self.gate_rows + 16 + self.rows
        self.chunk = -(-self.small_rows // (16 * self.n_mol)) * 16


class Operands(NamedTuple):
    nodes: Any
    feats_t: Any
    src: Any
    dst: Any
    atoms: Any
    edges: Any
    group: Any
    col_mask: Any
    cot: Any
    w1: Any
    b1: Any
    w2: Any
    b2: Any
    wi: Any
    wh: Any
    bg: Any
    perm_in_c: Any
    perm_c: Any


class Results(NamedTuple):
    states: Any
    state_grad: Any
    out_rows: Any
    small_out: Any
    w1_out: Any


class Scratch(NamedTuple):
    nodes_v: Any
    feats_v: Any
    src_v: Any
    dst_v: Any
    cot_v: Any
    w2_v: Any
    wi_v: Any
    wh_v: Any
    perm_in: Any
    perm: Any
    w2s: Any
    stage: Any
    hid: Any
    idx: Any
    s2: Any
    counts: Any
    cnt: Any
    t2: Any
    d2: Any
    e2: Any
    e_acc: Any
    dw_acc: Any
    ob_acc: Any
    gate_acc: Any
    gate_bias_acc: Any
    live: Any
    h: Any
    hb: Any
    hbw: Any
    hbw_t: Any
    gates: Any
    mt: Any
    dmt: Any
    dmn: Any
    dm: Any
    dgi: Any
    dgh: Any
    wib: Any
    whb: Any
    wit: Any
    wht: Any
    bcol: Any
    gt: Any
    spart: Any
    rs_in: Any
    sred: Any
    dwp: Any
    dw_in: Any
    dw_mid: Any
    dw_in2: Any
    sm_part: Any
    sm_in: Any
    sm_red: Any
    w1_part: Any
    w1_in: Any
    w1_mid: Any
    col_mask_v: Any
    w1_v: Any
    b1_v: Any
    bg_v: Any
    b2_v: Any
    group_s: Any
    edges_s: Any
    atoms_s: Any
    states_v: Any
    state_grad_v: Any
    out_rows_v: Any
    lsem: Any
    osem: Any
    w2_send: Any
    w2_recv: Any
    w2_fsend: Any
    m_send: Any
    m_recv: Any
    rs_send: Any
    rs_recv: Any
    ag_send: Any
    ag_recv: Any
    dw_send: Any
    dw_recv: Any
    dw2_send: Any
    dw2_recv: Any
    sm_send: Any
    sm_recv: Any
    sa_send: Any
    sa_recv: Any
    wr_send: Any
    wr_recv: Any
    wm_send: Any
    wm_recv: Any


def step_kernel(z, *refs):
    n_in, n_out = len(Operands._fields), len(Results._fields)
    a = Operands(*refs[:n_in])
    o = Results(*refs[n_in : n_in + n_out])
    r = Scratch(*refs[n_in + n_out :])
    atoms, edges, group = r.atoms_s, r.edges_s, r.group_s
    me, row = lax.axis_index(MOL), lax.axis_index(ROW)
    n_mol, n_row, rows, units, per = z.n_mol, z.n_row, z.rows, z.units, z.per
    width, halves = z.width, range(z.halves)
    row_at = pl.multiple_of(row * rows, rows)

    def others(index, count):
        return [lax.rem(index + step, count) for step in range(1, count)]

    mol_peers, row_peers = others(me, n_mol), others(row, n_row)

    def remote(source, target, send, recv, axis, device):
        return pltpu.make_async_remote_copy(
            src_ref=source,
            dst_ref=target,
            send_sem=send,
            recv_sem=recv,
            device_id={axis: device},
            device_id_type=MESH,
        )

    sent, stored = [], []

    def push(*args):
        remote(*args).start()
        sent.append(args)

    def store(source, target):
        pltpu.make_async_copy(source, target, r.osem.at[len(stored)]).start()
        stored.append((source, target))

    def arrived(there, send, recv, axis, device):
        remote(there, there, send, recv, axis, device).wait_recv()

    started = []

    def fetch(source, target):
        copy = pltpu.make_async_copy(source, target, r.lsem.at[len(started)])
        copy.start()
        started.append(copy)
        return copy

    barrier = pltpu.get_barrier_semaphore()
    for peer in mol_peers:
        pl.semaphore_signal(barrier, inc=1, device_id={MOL: peer}, device_id_type=MESH)
    for peer in row_peers:
        pl.semaphore_signal(barrier, inc=1, device_id={ROW: peer}, device_id_type=MESH)
    in_w2 = fetch(a.w2.at[0], r.w2_v) if z.fused else fetch(a.w2, r.w2s)
    in_small = (
        fetch(a.col_mask, r.col_mask_v),
        fetch(a.w1.at[0], r.w1_v),
        fetch(a.b1, r.b1_v),
        fetch(a.group, r.group_s),
        fetch(a.edges, r.edges_s),
        fetch(a.atoms, r.atoms_s),
    )
    in_src, in_dst = fetch(a.src, r.src_v), fetch(a.dst, r.dst_v)
    in_feats, in_nodes = fetch(a.feats_t, r.feats_v), fetch(a.nodes, r.nodes_v)
    in_perms = fetch(a.perm_in_c, r.perm_in), fetch(a.perm_c, r.perm)
    in_wi, in_wh = fetch(a.wi.at[0], r.wi_v), fetch(a.wh.at[0], r.wh_v)
    in_cot = fetch(a.cot, r.cot_v)
    in_bg, in_b2 = fetch(a.bg.at[0], r.bg_v), fetch(a.b2, r.b2_v)

    w2s, stage = r.w2s, r.stage
    partner = me + 1 - 2 * lax.rem(me, 2)
    same = [lax.rem(me + 2 * step, n_mol) for step in range(1, n_mol // 2)]
    same_of_partner = [lax.rem(partner + 2 * step, n_mol) for step in range(1, n_mol // 2)]

    some = rows // PARTS

    def block_of(ref, owner):
        return ref.at[:, pl.ds(pl.multiple_of(owner * per, 16), per), :]

    def part_of(owner, part):
        return w2s.at[pl.ds(part * some, some), pl.ds(pl.multiple_of(owner * per, 16), per), :]

    def forwards(part):
        copies = []
        for at, peer in enumerate(same):
            there, recv = part_of(peer, part), r.w2_recv.at[part, peer]
            copies.append(remote(there, there, r.w2_fsend.at[part, at], recv, MOL, partner))
        return copies

    def forward_part(part):
        for at, (peer, copy) in enumerate(zip(same, forwards(part))):
            there = part_of(peer, part)
            arrived(there, r.w2_send.at[part, at], r.w2_recv.at[part, peer], MOL, peer)
            copy.start()

    def whole_part(part):
        for peer in [partner] + same_of_partner:
            there = part_of(peer, part)
            arrived(there, r.w2_send.at[part, 0], r.w2_recv.at[part, peer], MOL, partner)

    for copy in in_small:
        copy.wait()
    lane_mol = iota((1, z.lanes), 1) // z.vpad
    lane_v = lax.rem(iota((1, z.lanes), 1), z.vpad)
    half_mol = iota((HALF, z.half_lanes), 1) // z.vpad == iota((HALF, z.half_lanes), 0)
    tile_v = hot(lax.rem(iota((z.vpad, z.half_lanes), 1), z.vpad) == iota((z.vpad, z.half_lanes), 0))
    live_to = jnp.zeros((1, z.lanes), jnp.int32)
    for m in range(z.mols):
        live_to = jnp.where(lane_mol == m, atoms[m], live_to)
    live_all = jnp.where(lane_v < live_to, 1.0, 0.0)
    for half in halves:
        lanes = slice(half * z.half_lanes, (half + 1) * z.half_lanes)
        r.live[half] = jnp.broadcast_to(live_all[:, lanes], (8, z.half_lanes))
    r.e_acc[...] = jnp.zeros(r.e_acc.shape, f32)
    r.dw_acc[...] = jnp.zeros(r.dw_acc.shape, f32)
    r.ob_acc[...] = jnp.zeros(r.ob_acc.shape, f32)

    mask_cols = jnp.concatenate(
        [r.col_mask_v[...].astype(f32), jnp.zeros((8 - a.col_mask.shape[0], z.feats), f32)], axis=0
    )
    mask_cols = jnp.concatenate([mask_cols, jnp.zeros((8, LANES - z.feats), f32)], axis=1).T
    masks = [low(jnp.broadcast_to(mask_cols[: z.feats, g : g + 1], (z.feats, z.edges))) for g in (0, 1)]
    w1_low = low(r.w1_v[...])
    b1_row = r.b1_v[0:1, :]

    if z.fused:
        in_w2.wait()
        for i in range(rows):
            stage[i] = low(r.w2_v[:, i * LANES : (i + 1) * LANES])
        w2s[:, pl.ds(pl.multiple_of(me * per, 16), per), :] = stage[...]
    pl.semaphore_wait(barrier, n_mol - 1 + n_row - 1)
    if z.fused:
        for part in range(PARTS):
            for at, peer in enumerate(same + [partner]):
                push(
                    stage.at[pl.ds(part * some, some)],
                    part_of(me, part),
                    r.w2_send.at[part, at],
                    r.w2_recv.at[part, me],
                    MOL,
                    peer,
                )

    s2, hid, idx, counts = r.s2, r.hid, r.idx, r.counts
    for copy in (in_src, in_dst, in_feats):
        copy.wait()
    lines = z.edges // LANES
    edge_at = iota((1, z.edges), 1)
    v_id = low(iota((z.vpad, z.edges), 0).astype(f32))
    one, zero = jnp.ones((), bf16), jnp.zeros((), bf16)

    def pair_hots(ends, count):
        from_all = low(jnp.broadcast_to(ends[0:1], (z.vpad, z.edges)))
        to_all = low(jnp.broadcast_to(ends[1:2], (z.vpad, z.edges)))
        to_hot = jnp.where(to_all == v_id, one, zero)
        from_hot = jnp.where(from_all == v_id, one, zero)
        pair_hot = [
            jnp.where(from_all == jnp.full((), w, bf16), to_hot, zero) for w in range(count)
        ]
        return from_hot, to_hot, jnp.concatenate(pair_hot, axis=0)

    def one_molecule(half, m8):
        m = half * HALF + m8
        at = pl.multiple_of(m * z.edges, z.edges)
        base = (me * z.mols + m) * z.cap
        kept = jnp.where(group[m] == 1, masks[1], masks[0])
        feats_m = r.feats_v[:, pl.ds(at, z.edges)] * kept
        r.feats_v[:, pl.ds(at, z.edges)] = feats_m
        hidden = low(jnp.maximum(dot_tn(feats_m, w1_low) + b1_row, 0.0))
        hid[m] = hidden.T

        def line(ref):
            return jnp.concatenate(
                [ref[pl.ds(m * lines + t, 1), :] for t in range(lines)], axis=1
            )

        from_at = line(r.src_v) - base
        to_at = jnp.where(edge_at < edges[m], line(r.dst_v) - base, 2 * z.vpad)
        ends = jnp.concatenate([from_at, to_at, jnp.zeros((6, z.edges), jnp.int32)], axis=0)
        ends = ends.astype(f32)
        idx[m] = ends
        from_hot, to_hot, pair_hot = pair_hots(ends, z.cap)
        sums = low(dot(pair_hot, hidden))
        for w in range(z.cap):
            s2[half, m8 * z.vpad : (m8 + 1) * z.vpad, w * units : (w + 1) * units] = sums[
                w * z.vpad : (w + 1) * z.vpad
            ]
        found = dot(low(dot_nt(from_hot, to_hot)), tile_v)
        found = jnp.where(iota(found.shape, 1) // z.vpad == m8, found, 0.0)
        counts[half, :, m8 : m8 + 1, :] = found[: z.wpad].reshape(z.wpad, 1, z.half_lanes)

    def half_sums(half, carry):
        s2[half, :, z.cap * units :] = jnp.zeros((z.half_lanes, (z.wpad - z.cap) * units), bf16)
        for m8 in range(HALF):
            one_molecule(half, m8)
        r.cnt[half] = low(counts[half].reshape(z.half_rows, z.half_lanes))
        return carry

    lax.fori_loop(0, z.halves, half_sums, 0)
    if z.fused:
        for part in range(PARTS):
            forward_part(part)

    h, hb, hbw, hbw_t = r.h, r.hb, r.hbw, r.hbw_t
    for copy in (in_nodes, *in_perms):
        copy.wait()

    def set_rows(layer, half):
        hb[layer, half] = low(h[layer, half])
        hbw[layer, half] = low(dot_nt(r.perm[...], hb[layer, half]))
        hbw_t[layer, half] = low(dot_nt(hb[layer, half], r.perm[...]))

    def rows_in(value, target):
        moved = dot_tn(value, r.perm_in[...])
        for half in halves:
            target[half] = moved[:, half * z.half_lanes : (half + 1) * z.half_lanes]

    rows_in(r.nodes_v[...], h.at[0])
    for half in halves:
        set_rows(0, half)
    wib, whb, wit, wht, bcol = r.wib, r.whb, r.wit, r.wht, r.bcol
    in_b2.wait()
    b2_low = low(
        jnp.concatenate([r.b2_v[0:1, i * LANES : (i + 1) * LANES] for i in range(rows)], axis=0)
    )

    if not z.fused:
        in_w2.wait()

    t2, mt, gates = r.t2, r.mt, r.gates

    def two(at):
        return slice(at * 2 * units, (at + 1) * 2 * units)

    def wide(block):
        return jnp.concatenate([block] * (z.half_lanes // LANES), axis=1)

    def spread(layer, half, part):
        state = hbw[layer, half]

        def pair(at):
            ip = part * (some // 2) + at
            both = dot_nt(state, w2s[2 * ip : 2 * ip + 2].reshape(2 * units, width))
            at = ip * 2 * HALF
            for w in range(z.wpad):
                s = slice(w * HALF, (w + 1) * HALF)
                t2[layer, half, pl.ds(at, 2 * HALF), w * units : (w + 1) * units] = low(
                    jnp.concatenate([both[s, :units], both[s, units:]], axis=0)
                )

        for at in range(some // 2):
            pair(at)

    def messages(layer, half):
        state = hbw[layer, half]
        bias = dot(low(dot_nt(b2_low, state)), r.cnt[half])
        full = dot_nt(t2[layer, half], s2[half]).reshape(rows, HALF, z.half_lanes)
        full = jnp.where(half_mol[None], full + bias[:, None, :], 0.0)
        mt[layer, half, pl.ds(row_at, rows), :] = low(jnp.sum(full, axis=1))
        share(mt, r.m_send, r.m_recv, layer, half)

    def row_pushes(ref, send, recv, layer, half):
        mine = ref.at[layer, half, pl.ds(row_at, rows), :]
        return [
            remote(mine, mine, send.at[layer, half, at], recv.at[layer, half, row], ROW, peer)
            for at, peer in enumerate(row_peers)
        ]

    def share(*args):
        for copy in row_pushes(*args):
            copy.start()

    def collect(ref, send, recv, layer, half):
        for peer in row_peers:
            there = ref.at[layer, half, pl.ds(pl.multiple_of(peer * rows, rows), rows), :]
            arrived(there, send.at[layer, half, 0], recv.at[layer, half, peer], ROW, peer)

    def state_side(layer, half):
        gates[layer, half, 0] = dot(wht[...], hb[layer, half]) + wide(bcol[1])

    def gru(layer, half):
        collect(mt, r.m_send, r.m_recv, layer, half)
        from_msg = dot(wit[...], mt[layer, half]) + wide(bcol[0])
        from_state = gates[layer, half, 0]
        reset = jax.nn.sigmoid(from_msg[:width] + from_state[:width])
        update = jax.nn.sigmoid(from_msg[width : 2 * width] + from_state[width : 2 * width])
        new = jnp.tanh(from_msg[2 * width :] + reset * from_state[2 * width :])
        gates[layer, half, 1, :width] = reset
        gates[layer, half, 1, width : 2 * width] = update
        gates[layer, half, 1, 2 * width :] = new
        h[layer + 1, half] = r.live[half, 0:1] * ((1.0 - update) * new + update * h[layer, half])

    gt, dgi, dgh, dm, dmt, dmn = r.gt, r.dgi, r.dgh, r.dm, r.dmt, r.dmn
    d2, spart, sred = r.d2, r.spart, r.sred

    def gru_back(layer, half):
        up = gt[half] * r.live[half, 0:1]
        reset = gates[layer, half, 1, :width]
        update = gates[layer, half, 1, width : 2 * width]
        new = gates[layer, half, 1, 2 * width :]
        d_new = up * (1.0 - update) * (1.0 - new * new)
        d_update = up * (h[layer, half] - new) * update * (1.0 - update)
        d_reset = d_new * gates[layer, half, 0, 2 * width :] * reset * (1.0 - reset)
        msg_side = low(jnp.concatenate([d_reset, d_update, d_new], axis=0))
        dgi[layer, half] = msg_side
        dgh[layer, half, : 2 * width] = msg_side[: 2 * width]
        dgh[layer, half, 2 * width :] = low(d_new * reset)
        part = low(dot(wib[pl.ds(row_at, rows), :], msg_side))
        dm[layer, half] = part
        spread = jnp.where(half_mol[None], part.astype(f32)[:, None, :], 0.0)
        spread = spread.reshape(rows * HALF, z.half_lanes)
        dmt[layer, half] = low(spread)
        dmn[layer, half] = low(spread.T)
        gt[half] = up * update + dot(whb[...], dgh[layer, half])

    def gathered(layer, half):
        def pair(wp):
            lanes = two(wp)
            both = dot(dmt[layer, half], s2[half, :, lanes])
            at = wp * 2 * HALF
            for i in range(rows):
                part = both[i * HALF : (i + 1) * HALF]
                d2[pl.ds(at, 2 * HALF), i * units : (i + 1) * units] = low(
                    jnp.concatenate([part[:, :units], part[:, units:]], axis=0)
                )

        for wp in range(z.wpad // 2):
            pair(wp)

    def bias_rows(layer, half):
        return low(dot_nt(dm[layer, half], r.cnt[half]))

    def state_part(layer, half):
        biases = bias_rows(layer, half)
        r.ob_acc[...] += dot(biases, hbw[layer, half])
        back = dot(d2[...], w2s[...].reshape(rows * units, width)) + dot_tn(biases, b2_low)
        spart[layer, half] = low(dot_tn(low(back), r.perm[...]))
        for copy in part_pushes(layer, half):
            copy.start()

    def part_pushes(layer, half):
        return [
            remote(
                spart.at[layer, half, pl.ds(pl.multiple_of(peer * rows, rows), rows), :],
                r.rs_in.at[layer, half, row],
                r.rs_send.at[layer, half, at],
                r.rs_recv.at[layer, half, row],
                ROW,
                peer,
            )
            for at, peer in enumerate(row_peers)
        ]

    def state_sum(layer, half):
        total = spart[layer, half, pl.ds(row_at, rows), :].astype(f32)
        for peer in row_peers:
            there = r.rs_in.at[layer, half, peer]
            arrived(there, r.rs_send.at[layer, half, 0], r.rs_recv.at[layer, half, peer], ROW, peer)
            total = total + r.rs_in[layer, half, peer].astype(f32)
        sred[layer, half, pl.ds(row_at, rows), :] = low(total)
        share(sred, r.ag_send, r.ag_recv, layer, half)

    def settle():
        def one_step(t, carry):
            layer, half = lax.div(t, z.halves), lax.rem(t, z.halves)
            for copy in row_pushes(mt, r.m_send, r.m_recv, layer, half):
                copy.wait_send()
            for copy in part_pushes(layer, half):
                copy.wait_send()
            for copy in row_pushes(sred, r.ag_send, r.ag_recv, layer, half):
                copy.wait_send()
            return carry

        lax.fori_loop(0, LAYERS * z.halves, one_step, 0)
        for args in sent:
            remote(*args).wait_send()
        for copy in small_copies():
            copy.wait_send()
        if z.fused:
            for copy in pair_copies():
                copy.wait_send()
            for part in range(PARTS):
                for copy in forwards(part):
                    copy.wait_send()

    def rows_out(value):
        total = None
        for half in halves:
            rest = value(half)
            lanes = slice(half * z.half_lanes, (half + 1) * z.half_lanes)
            for _ in range(3):
                part = low(rest)
                rest = rest - part.astype(f32)
                moved = dot_nt(r.perm_in[:, lanes], part)
                total = moved if total is None else total + moved
        return total

    dwp, dw_acc, e2, e_acc = r.dwp, r.dw_acc, r.e2, r.e_acc

    def weight_grad(layer, half):
        for ip in range(rows // 2):
            at = two(ip)
            dw_acc[:, at] += dot(hbw_t[layer, half], d2[:, at])

    def pair_grad(layer, half):
        for wp in range(z.wpad // 2):
            at = two(wp)
            total = e_acc[half, :, at] + dot(dmn[layer, half], t2[layer, half, :, at])
            e_acc[half, :, at] = total
            e2[half, :, at] = low(total)

    def gate_weights():
        in_wi.wait()
        in_wh.wait()
        wib[...] = low(r.wi_v[...])
        whb[...] = low(r.wh_v[...])
        wit[...] = low(r.wi_v[...].T)
        wht[...] = low(r.wh_v[...].T)
        in_cot.wait()
        in_bg.wait()
        bias_t = jnp.concatenate([r.bg_v[...], jnp.zeros((6, 3 * width), f32)], axis=0).T
        for side in range(2):
            bcol[side] = jnp.broadcast_to(bias_t[:, side : side + 1], (3 * width, LANES))
        rows_in(r.cot_v[...], r.gt)
        for half in halves:
            state_side(0, half)

    def forward_step(t, carry):
        layer, half = lax.div(t, z.halves), lax.rem(t, z.halves)

        @pl.when(layer > 0)
        def _():
            gru(layer - 1, half)
            set_rows(layer, half)

        for part in range(PARTS):
            if z.fused and part > 0:
                pl.when(t == 0)(functools.partial(whole_part, part))
            spread(layer, half, part)
        messages(layer, half)
        pl.when(t == z.halves - 1)(gate_weights)
        pl.when(layer > 0)(functools.partial(state_side, layer, half))
        return carry

    if z.fused:
        whole_part(0)
    lax.fori_loop(0, LAYERS * z.halves, forward_step, 0)

    last = LAYERS - 1

    ones = jnp.ones((8, z.lanes), bf16)

    def beside(ref, layer):
        return jnp.concatenate([ref[layer, half] for half in halves], axis=1)

    def gate_sums(layer):
        sums = []
        for at, (side, grads) in enumerate(((mt, dgi), (hb, dgh))):
            grads = beside(grads, layer)
            sums.append((dot_nt(beside(side, layer), grads), dot_nt(ones, grads)))
        return sums

    def back_half(layer, half):
        @pl.when(layer == last)
        def _():
            gru(last, half)

        @pl.when(layer < last)
        def _():
            collect(sred, r.ag_send, r.ag_recv, layer + 1, half)
            gt[half] += sred[layer + 1, half].astype(f32)

        gru_back(layer, half)
        gathered(layer, half)
        state_part(layer, half)
        weight_grad(layer, half)

    def pair_half(layer, half):
        pair_grad(layer, half)
        pl.when(layer == last)(functools.partial(state_sum, last, half))

    theirs = [lax.rem(partner + 2 * step, n_mol) for step in range(n_mol // 2)]
    ours = [lax.rem(me + 2 * step, n_mol) for step in range(n_mol // 2)]

    def pair_copies():
        return [
            remote(block_of(dwp, owner), r.dw_in.at[at], r.dw_send.at[at], r.dw_recv.at[at], MOL, partner)
            for at, owner in enumerate(theirs)
        ]

    def weight_out():
        for i in range(rows):
            dwp[i] = low(dw_acc[:, i * units : (i + 1) * units]).T
        if z.fused:
            for copy in pair_copies():
                copy.start()

    def backward_layer(t, carry):
        layer = last - t
        lax.fori_loop(0, z.halves, lambda half, c: back_half(layer, half) or c, 0)
        pl.when(layer == 0)(weight_out)
        lax.fori_loop(0, z.halves, lambda half, c: pair_half(layer, half) or c, 0)

        @pl.when(layer == last)
        def _():
            r.states_v[...] = rows_out(lambda half: h[LAYERS, half])
            store(r.states_v, o.states)
            for at, (weight, bias) in enumerate(gate_sums(last)):
                r.gate_acc[at], r.gate_bias_acc[at] = weight, bias

        return carry

    lax.fori_loop(0, LAYERS, backward_layer, 0)

    sm_part, sm_in = r.sm_part, r.sm_in
    bias_lines = []
    for at, (weight, bias) in enumerate(gate_sums(0)):
        weight, bias = weight + r.gate_acc[at], bias + r.gate_bias_acc[at]
        for third in range(3):
            first = (3 * at + third) * width
            sm_part[first : first + width, :] = low(weight[:, third * width : (third + 1) * width])
        bias_lines += [bias[0:1, third * width : (third + 1) * width] for third in range(3)]
    bias_lines.append(jnp.zeros((10, width), f32))
    sm_part[z.gate_rows : z.gate_rows + 16, :] = low(jnp.concatenate(bias_lines, axis=0))
    sm_part[z.gate_rows + 16 : z.small_rows, :] = low(r.ob_acc[...])
    if z.chunk * n_mol > z.small_rows:
        sm_part[z.small_rows :, :] = jnp.zeros((z.chunk * n_mol - z.small_rows, width), bf16)

    def chunk_of(ref, owner):
        return ref.at[pl.ds(pl.multiple_of(owner * z.chunk, 16), z.chunk), :]

    for at, peer in enumerate(mol_peers):
        push(chunk_of(sm_part, peer), sm_in.at[me], r.sm_send.at[at], r.sm_recv.at[me], MOL, peer)
    if z.fused:
        for at, owner in enumerate(ours):
            arrived(r.dw_in.at[at], r.dw_send.at[at], r.dw_recv.at[at], MOL, partner)
            own = dwp[:, pl.ds(pl.multiple_of(owner * per, 16), per), :].astype(f32)
            r.dw_mid[at] = low(own + r.dw_in[at].astype(f32))
            if at > 0:
                push(r.dw_mid.at[at], r.dw_in2.at[at], r.dw2_send.at[at], r.dw2_recv.at[at], MOL, owner)

    def small_copies():
        return [
            remote(r.sm_red, chunk_of(o.small_out, me), r.sa_send.at[at], r.sa_recv.at[me], MOL, peer)
            for at, peer in enumerate(mol_peers)
        ]

    def between():
        for half in halves:
            state_sum(0, half)

    def summed(pieces):
        return functools.reduce(jnp.add, pieces)

    def edge_grad(half, m8):
        m = half * HALF + m8
        at = pl.multiple_of(m * z.edges, z.edges)
        _, _, pair_hot = pair_hots(idx[m], z.wpad)
        slot = slice(m8 * z.vpad, (m8 + 1) * z.vpad)
        grads = [e2[half, slot, w * units : (w + 1) * units] for w in range(z.wpad)]
        d_hidden = dot_tn(jnp.concatenate(grads, axis=0), pair_hot)
        d_pre = low(jnp.where(hid[m].astype(f32) > 0.0, d_hidden, 0.0))
        feats_m = r.feats_v[:, pl.ds(at, z.edges)]
        feats_m = jnp.concatenate([feats_m, jnp.ones((16, z.edges), bf16)], axis=0)
        return dot_nt(d_pre, feats_m)

    def half_grad(half, total):
        total = total + summed([edge_grad(half, m8) for m8 in range(HALF)])
        pl.when(half == 0)(between)
        return total

    total = lax.fori_loop(0, z.halves, half_grad, jnp.zeros((units, z.feats + 16), f32))
    w1_part, w1_in, w1_mid = r.w1_part, r.w1_in, r.w1_mid
    total = jnp.concatenate([total, jnp.zeros((units, LANES - z.feats - 16), f32)], axis=1).T
    w1_part[...] = total[: z.feats + 8]
    for at, peer in enumerate(row_peers):
        push(w1_part, w1_in.at[row], r.wr_send.at[at], r.wr_recv.at[row], ROW, peer)
    w1_in[row] = w1_part[...]

    total = sm_part[pl.ds(pl.multiple_of(me * z.chunk, 16), z.chunk), :].astype(f32)
    for peer in mol_peers:
        arrived(sm_in.at[peer], r.sm_send.at[0], r.sm_recv.at[peer], MOL, peer)
        total = total + sm_in[peer].astype(f32)
    r.sm_red[...] = low(total)
    for copy in small_copies():
        copy.start()
    store(r.sm_red, chunk_of(o.small_out, me))
    for peer in row_peers:
        arrived(w1_in.at[peer], r.wr_send.at[0], r.wr_recv.at[peer], ROW, peer)
    total = w1_in[0]
    for at in range(1, n_row):
        total = total + w1_in[at]
    w1_mid[...] = total
    for at, peer in enumerate(mol_peers):
        push(w1_mid, o.w1_out.at[me], r.wm_send.at[at], r.wm_recv.at[me], MOL, peer)
    store(w1_mid, o.w1_out.at[me])

    for half in halves:
        collect(sred, r.ag_send, r.ag_recv, 0, half)
    r.state_grad_v[...] = rows_out(lambda half: gt[half] + sred[0, half].astype(f32))
    store(r.state_grad_v, o.state_grad)
    settle()
    if z.fused:
        total = r.dw_mid[0].astype(f32)
        for at in range(1, n_mol // 2):
            arrived(r.dw_in2.at[at], r.dw2_send.at[at], r.dw2_recv.at[at], MOL, partner)
            total = total + r.dw_in2[at].astype(f32)
        for i in range(rows):
            r.out_rows_v[:, i * LANES : (i + 1) * LANES] = total[i]
        store(r.out_rows_v, o.out_rows)
    else:
        store(dwp, o.out_rows)
    for peer in mol_peers:
        arrived(o.w1_out.at[peer], r.wm_send.at[0], r.wm_recv.at[peer], MOL, peer)
    for peer in mol_peers:
        arrived(chunk_of(o.small_out, peer), r.sa_send.at[0], r.sa_recv.at[peer], MOL, peer)
    for at, (source, target) in enumerate(stored):
        pltpu.make_async_copy(source, target, r.osem.at[at]).wait()


def run_step(z, args, w2_all):
    (node_states, edge_feats, edge_src, edge_dst, atom_counts, edge_counts, mol_group, col_mask,
     cotangent, edge_in_state, edge_in_bias_state, edge_out_state, edge_out_bias_state,
     gate_in_state, gate_hidden_state, gate_bias_state) = args
    any_spec = pl.BlockSpec(memory_space=pl.ANY)
    v = pltpu.VMEM
    dma = pltpu.SemaphoreType.DMA
    rows, width, units, per = z.rows, z.width, z.units, z.per
    n_mol, n_row, halves = z.n_mol, z.n_row, z.halves
    half_rows, half_lanes = z.half_rows, z.half_lanes
    both = (LAYERS, halves)
    full = rows * HALF
    lines = (z.mols * z.edges // LANES, LANES)
    step_in = (rows, per, LANES)
    lane = np.arange(z.lanes)
    lane_mol, lane_v = lane // z.vpad, lane % z.vpad
    node = np.where(lane_v < z.cap, lane_mol * z.cap + lane_v, -1)
    perm_in = (np.arange(z.nodes)[:, None] == node[None, :]).astype(np.float32)
    row_at = np.arange(half_rows)
    row_lane = (row_at % HALF) * z.vpad + row_at // HALF
    perm = (row_lane[:, None] == np.arange(half_lanes)[None, :]).astype(np.float32)
    operands = Operands(
        nodes=(node_states, any_spec),
        feats_t=(edge_feats.T, any_spec),
        src=(edge_src.reshape(lines), any_spec),
        dst=(edge_dst.reshape(lines), any_spec),
        atoms=(atom_counts, any_spec),
        edges=(edge_counts, any_spec),
        group=(mol_group, any_spec),
        col_mask=(col_mask, any_spec),
        cot=(cotangent, any_spec),
        w1=(edge_in_state, any_spec),
        b1=(edge_in_bias_state, any_spec),
        w2=(edge_out_state if z.fused else w2_all, any_spec),
        b2=(edge_out_bias_state, any_spec),
        wi=(gate_in_state, any_spec),
        wh=(gate_hidden_state, any_spec),
        bg=(gate_bias_state, any_spec),
        perm_in_c=(jnp.asarray(perm_in, bf16), any_spec),
        perm_c=(jnp.asarray(perm, bf16), any_spec),
    )
    outs = [
        jax.ShapeDtypeStruct((z.nodes, width), f32),
        jax.ShapeDtypeStruct((z.nodes, width), f32),
        jax.ShapeDtypeStruct((per, rows * width), f32)
        if z.fused
        else jax.ShapeDtypeStruct((rows, units, width), bf16),
        jax.ShapeDtypeStruct((n_mol * z.chunk, width), bf16),
        jax.ShapeDtypeStruct((n_mol, z.feats + 8, units), f32),
    ]
    row_sems = dma(both + (n_row,))
    mol_sems = dma((n_mol,))
    scratch = Scratch(
        nodes_v=v((z.nodes, width), bf16),
        feats_v=v((z.feats, z.mols * z.edges), bf16),
        src_v=v(lines, jnp.int32),
        dst_v=v(lines, jnp.int32),
        cot_v=v((z.nodes, width), bf16),
        w2_v=v((per, rows * width), f32),
        wi_v=v((width, 3 * width), f32),
        wh_v=v((width, 3 * width), f32),
        perm_in=v((z.nodes, z.lanes), bf16),
        perm=v((half_rows, half_lanes), bf16),
        w2s=v((rows, units, width), bf16),
        stage=v(step_in, bf16),
        hid=v((z.mols, units, z.edges), bf16),
        idx=v((z.mols, 8, z.edges), f32),
        s2=v((halves, half_lanes, z.span), bf16),
        counts=v((halves, z.wpad, HALF, half_lanes), f32),
        cnt=v((halves, half_rows, half_lanes), bf16),
        t2=v(both + (full, z.span), bf16),
        d2=v((half_rows, rows * units), bf16),
        e2=v((halves, half_lanes, z.span), bf16),
        e_acc=v((halves, half_lanes, z.span), f32),
        dw_acc=v((width, rows * units), f32),
        ob_acc=v((rows, width), f32),
        gate_acc=v((2, width, 3 * width), f32),
        gate_bias_acc=v((2, 8, 3 * width), f32),
        live=v((halves, 8, half_lanes), f32),
        h=v((LAYERS + 1, halves, width, half_lanes), f32),
        hb=v(both + (width, half_lanes), bf16),
        hbw=v(both + (half_rows, width), bf16),
        hbw_t=v(both + (width, half_rows), bf16),
        gates=v(both + (2, 3 * width, half_lanes), f32),
        mt=v(both + (width, half_lanes), bf16),
        dmt=v(both + (full, half_lanes), bf16),
        dmn=v(both + (half_lanes, full), bf16),
        dm=v(both + (rows, half_lanes), bf16),
        dgi=v(both + (3 * width, half_lanes), bf16),
        dgh=v(both + (3 * width, half_lanes), bf16),
        wib=v((width, 3 * width), bf16),
        whb=v((width, 3 * width), bf16),
        wit=v((3 * width, width), bf16),
        wht=v((3 * width, width), bf16),
        bcol=v((2, 3 * width, LANES), f32),
        gt=v((halves, width, half_lanes), f32),
        spart=v(both + (width, half_lanes), bf16),
        rs_in=v(both + (n_row, rows, half_lanes), bf16),
        sred=v(both + (width, half_lanes), bf16),
        dwp=v((rows, units, width), bf16),
        dw_in=v((n_mol // 2,) + step_in, bf16),
        dw_mid=v((n_mol // 2,) + step_in, bf16),
        dw_in2=v((n_mol // 2,) + step_in, bf16),
        sm_part=v((n_mol * z.chunk, width), bf16),
        sm_in=v((n_mol, z.chunk, width), bf16),
        sm_red=v((z.chunk, width), bf16),
        w1_part=v((z.feats + 8, units), f32),
        w1_in=v((n_row, z.feats + 8, units), f32),
        w1_mid=v((z.feats + 8, units), f32),
        col_mask_v=v(col_mask.shape, jnp.int32),
        w1_v=v(edge_in_state.shape[1:], f32),
        b1_v=v(edge_in_bias_state.shape, f32),
        bg_v=v(gate_bias_state.shape[1:], f32),
        b2_v=v(edge_out_bias_state.shape, f32),
        group_s=pltpu.SMEM(mol_group.shape, jnp.int32),
        edges_s=pltpu.SMEM(edge_counts.shape, jnp.int32),
        atoms_s=pltpu.SMEM(atom_counts.shape, jnp.int32),
        states_v=v((z.nodes, width), f32),
        state_grad_v=v((z.nodes, width), f32),
        out_rows_v=v((per, rows * width), f32),
        lsem=dma((len(operands),)),
        osem=dma((8,)),
        w2_send=dma((PARTS, n_mol)),
        w2_recv=dma((PARTS, n_mol)),
        w2_fsend=dma((PARTS, n_mol)),
        m_send=row_sems,
        m_recv=row_sems,
        rs_send=row_sems,
        rs_recv=row_sems,
        ag_send=row_sems,
        ag_recv=row_sems,
        dw_send=mol_sems,
        dw_recv=mol_sems,
        dw2_send=mol_sems,
        dw2_recv=mol_sems,
        sm_send=mol_sems,
        sm_recv=mol_sems,
        sa_send=mol_sems,
        sa_recv=mol_sems,
        wr_send=dma((n_row,)),
        wr_recv=dma((n_row,)),
        wm_send=mol_sems,
        wm_recv=mol_sems,
    )
    return pl.pallas_call(
        functools.partial(step_kernel, z),
        out_shape=outs,
        in_specs=[spec for _, spec in operands],
        out_specs=[any_spec] * len(outs),
        scratch_shapes=list(scratch),
        compiler_params=pltpu.CompilerParams(
            collective_id=0, has_side_effects=True, vmem_limit_bytes=VMEM_BYTES
        ),
        name="step",
    )(*[array for array, _ in operands])


def nesterov(state, grad, rate, out):
    scaled = rate * grad
    moment = momentum_coef * state[1] + scaled
    weight = state[0] - (scaled + momentum_coef * moment)
    out[0] = weight
    out[1] = moment
    out[2] = average_decay * state[2] + (1.0 - average_decay) * weight


def nesterov_line(state, grad, rate, out):
    scaled = rate * grad
    moment = momentum_coef * state[1:2, :] + scaled
    weight = state[0:1, :] - (scaled + momentum_coef * moment)
    out[0:1, :] = weight
    out[1:2, :] = moment
    out[2:3, :] = average_decay * state[2:3, :] + (1.0 - average_decay) * weight


class Update(NamedTuple):
    states: Any
    state_grad: Any
    out_rows: Any
    small: Any
    w1_sum: Any
    w1: Any
    b1: Any
    w2: Any
    b2: Any
    wi: Any
    wh: Any
    bg: Any


class Updated(NamedTuple):
    states: Any
    state_grad: Any
    w1_g: Any
    w1_n: Any
    b1_g: Any
    b1_n: Any
    w2_g: Any
    w2_n: Any
    b2_g: Any
    b2_n: Any
    wi_g: Any
    wi_n: Any
    wh_g: Any
    wh_n: Any
    bg_g: Any
    bg_n: Any


def update_kernel(z, rates, *refs):
    n_in, n_out = len(Update._fields), len(Updated._fields)
    given, out = Update(*refs[:n_in]), Updated(*refs[n_in : n_in + n_out])
    refs = refs[n_in + n_out :]
    here, new = Update(*refs[:n_in]), Updated(*refs[n_in : n_in + n_out])
    in_sem, out_sem = refs[n_in + n_out :]
    rate_in, rate_out, rate_gate = rates
    width = z.width
    sent = []

    def send(source, target):
        copy = pltpu.make_async_copy(source, target, out_sem.at[len(sent)])
        copy.start()
        sent.append(copy)

    fetched = Update(
        *[pltpu.make_async_copy(given[at], here[at], in_sem.at[at]) for at in range(n_in)]
    )
    order = (fetched.wi, fetched.small, fetched.wh, fetched.w2, fetched.out_rows)
    passed = (fetched.states, fetched.state_grad)
    rest = (fetched.bg, fetched.b2, fetched.w1, fetched.b1, fetched.w1_sum)
    for copy in order + passed + rest:
        copy.start()

    def thirds(at):
        parts = [here.small[(3 * at + t) * width : (3 * at + t + 1) * width, :] for t in range(3)]
        return jnp.concatenate(parts, axis=1).astype(f32)

    fetched.wi.wait()
    fetched.small.wait()
    total = thirds(0)
    new.wi_g[...] = total
    nesterov(here.wi, total, rate_gate, new.wi_n)
    send(new.wi_g, out.wi_g)
    send(new.wi_n, out.wi_n)
    fetched.wh.wait()
    total = thirds(1)
    new.wh_g[...] = total
    nesterov(here.wh, total, rate_gate, new.wh_n)
    send(new.wh_g, out.wh_g)
    send(new.wh_n, out.wh_n)
    fetched.w2.wait()
    fetched.out_rows.wait()
    send(here.out_rows, out.w2_g)
    nesterov(here.w2, here.out_rows[...], rate_out, new.w2_n)
    send(new.w2_n, out.w2_n)
    for copy in passed + rest:
        copy.wait()
    send(here.states, out.states)
    send(here.state_grad, out.state_grad)
    lines = here.small[z.gate_rows : z.gate_rows + 16, :].astype(f32)
    total = jnp.concatenate(
        [
            jnp.concatenate([lines[3 * side + t : 3 * side + t + 1, :] for t in range(3)], axis=1)
            for side in range(2)
        ],
        axis=0,
    )
    new.bg_g[...] = total
    nesterov(here.bg, total, rate_gate, new.bg_n)
    send(new.bg_g, out.bg_g)
    send(new.bg_n, out.bg_n)
    total = here.small[z.gate_rows + 16 : z.gate_rows + 16 + z.rows, :].astype(f32)
    new.b2_g[...] = total
    total = jnp.concatenate([total[i : i + 1, :] for i in range(z.rows)], axis=1)
    nesterov_line(here.b2, total, rate_out, new.b2_n)
    send(new.b2_g, out.b2_g)
    send(new.b2_n, out.b2_n)
    w1_sum = sum(here.w1_sum[at] for at in range(z.n_mol))
    total = w1_sum[: z.feats, :]
    new.w1_g[...] = total
    nesterov(here.w1, total, rate_in, new.w1_n)
    send(new.w1_g, out.w1_g)
    send(new.w1_n, out.w1_n)
    total = w1_sum[z.feats : z.feats + 1, :]
    new.b1_g[...] = total
    nesterov_line(here.b1, total, rate_in, new.b1_n)
    send(new.b1_g, out.b1_g)
    send(new.b1_n, out.b1_n)
    for copy in sent:
        copy.wait()


def per_device(mesh, *args):
    (node_states, edge_feats, edge_src, edge_dst, atom_counts, edge_counts, mol_group, col_mask,
     cotangent, edge_in_state, edge_in_bias_state, edge_out_state, edge_out_bias_state,
     gate_in_state, gate_hidden_state, gate_bias_state) = args
    z = Sizes(mesh, node_states, edge_feats, atom_counts, edge_in_state, edge_out_bias_state)
    w2_all = None
    if not z.fused:
        w2_all = lax.all_gather(low(edge_out_state[0]), "mol", axis=0, tiled=True)
        w2_all = w2_all.reshape(z.units, z.rows, z.width).swapaxes(0, 1)
    states, state_grad, out_rows, small, w1_sum = run_step(z, args, w2_all)
    if not z.fused:
        out_rows = out_rows.swapaxes(0, 1).reshape(z.units, z.rows * z.width)
        out_rows = lax.psum_scatter(out_rows, "mol", scatter_dimension=0, tiled=True).astype(f32)
    edges_all = edge_feats.shape[0] * z.n_mol
    nodes_all = z.nodes * z.n_mol
    rates = (
        z.feats ** (-0.5) / (0.2 * edges_all**0.5),
        (z.units * z.width * 8) ** (-0.5) / (0.4 * edges_all**0.5),
        z.width ** (-0.5) / (0.5 * nodes_all**0.5),
    )
    any_spec = pl.BlockSpec(memory_space=pl.ANY)
    operands = [
        states, state_grad, out_rows, small, w1_sum, edge_in_state, edge_in_bias_state,
        edge_out_state, edge_out_bias_state, gate_in_state, gate_hidden_state, gate_bias_state,
    ]
    outs = [
        states.shape, state_grad.shape, (z.feats, z.units), edge_in_state.shape,
        (1, z.units), edge_in_bias_state.shape, out_rows.shape, edge_out_state.shape,
        (z.rows, z.width), edge_out_bias_state.shape, (z.width, 3 * z.width), gate_in_state.shape,
        (z.width, 3 * z.width), gate_hidden_state.shape, (2, 3 * z.width), gate_bias_state.shape,
    ]
    results = pl.pallas_call(
        functools.partial(update_kernel, z, rates),
        out_shape=[jax.ShapeDtypeStruct(shape, f32) for shape in outs],
        in_specs=[any_spec] * len(operands),
        out_specs=[any_spec] * len(outs),
        scratch_shapes=[pltpu.VMEM(array.shape, array.dtype) for array in operands]
        + [pltpu.VMEM(shape, f32) for shape in outs]
        + [pltpu.SemaphoreType.DMA((len(operands),)), pltpu.SemaphoreType.DMA((len(outs),))],
        compiler_params=pltpu.CompilerParams(vmem_limit_bytes=VMEM_BYTES),
        name="update",
    )(*operands)
    results = list(results)
    results[4] = results[4].reshape(-1)
    results[8] = results[8].reshape(-1)
    return tuple(results)


def solution(mesh):
    return jax.shard_map(
        functools.partial(per_device, mesh),
        mesh=mesh,
        in_specs=(
            P(MOL, None),
            P(MOL, None),
            P(MOL),
            P(MOL),
            P(MOL),
            P(MOL),
            P(MOL),
            P(),
            P(MOL, None),
            P(),
            P(),
            P(None, MOL, ROW),
            P(None, ROW),
            P(),
            P(),
            P(),
        ),
        out_specs=(
            P(MOL, None),
            P(MOL, None),
            P(),
            P(),
            P(),
            P(),
            P(MOL, ROW),
            P(None, MOL, ROW),
            P(ROW),
            P(None, ROW),
            P(),
            P(),
            P(),
            P(),
            P(),
            P(),
        ),
        check_vma=False,
    )
```

```python
import functools
from typing import Any, NamedTuple

import jax
import jax.numpy as jnp
import numpy as np
from jax import lax
from jax.experimental import pallas as pl
from jax.experimental.pallas import tpu as pltpu
from jax.sharding import PartitionSpec as P

LAYERS = 2
HALF = 8
LANES = 128
PARTS = 1
MOL, ROW = "mol", "row"
MESH = pl.DeviceIdType.MESH
VMEM_BYTES = 58 * 1024 * 1024

momentum_coef = 0.9
average_decay = 0.9
f32 = jnp.float32
bf16 = jnp.bfloat16


def dot(left, right):
    return lax.dot_general(left, right, (((1,), (0,)), ((), ())), preferred_element_type=f32)


def dot_nt(left, right):
    return lax.dot_general(left, right, (((1,), (1,)), ((), ())), preferred_element_type=f32)


def dot_tn(left, right):
    return lax.dot_general(left, right, (((0,), (0,)), ((), ())), preferred_element_type=f32)


def low(value):
    return value.astype(bf16)


def iota(shape, axis):
    return lax.broadcasted_iota(jnp.int32, shape, axis)


def hot(mask):
    return low(jnp.where(mask, 1.0, 0.0))


class Sizes:
    def __init__(self, mesh, node_states, edge_feats, atom_counts, edge_in_state, edge_out_bias_state):
        self.n_mol, self.n_row = mesh.shape["mol"], mesh.shape["row"]
        self.mols = atom_counts.shape[0]
        self.nodes, self.width = node_states.shape
        self.cap = self.nodes // self.mols
        self.edges = edge_feats.shape[0] // self.mols
        self.feats = edge_feats.shape[1]
        self.units = edge_in_state.shape[2]
        self.rows = edge_out_bias_state.shape[1] // self.width
        self.per = self.units // self.n_mol
        self.halves = self.mols // HALF
        self.vpad = 32
        self.wpad = self.cap + self.cap % 2
        self.lanes = self.mols * self.vpad
        self.half_lanes = HALF * self.vpad
        self.half_rows = HALF * self.wpad
        self.span = self.wpad * self.units
        self.fused = self.per % 16 == 0
        self.gate_rows = 6 * self.width
        self.small_rows = self.gate_rows + 16 + self.rows
        self.chunk = -(-self.small_rows // (16 * self.n_mol)) * 16


class Operands(NamedTuple):
    nodes: Any
    feats_t: Any
    src: Any
    dst: Any
    atoms: Any
    edges: Any
    group: Any
    col_mask: Any
    cot: Any
    w1: Any
    b1: Any
    w2: Any
    b2: Any
    wi: Any
    wh: Any
    bg: Any
    perm_in_c: Any
    perm_c: Any


class Results(NamedTuple):
    states: Any
    state_grad: Any
    out_rows: Any
    small_out: Any
    w1_out: Any


class Scratch(NamedTuple):
    nodes_v: Any
    feats_v: Any
    src_v: Any
    dst_v: Any
    cot_v: Any
    w2_v: Any
    wi_v: Any
    wh_v: Any
    perm_in: Any
    perm: Any
    w2s: Any
    stage: Any
    hid: Any
    idx: Any
    s2: Any
    counts: Any
    cnt: Any
    t2: Any
    d2: Any
    e2: Any
    e_acc: Any
    dw_acc: Any
    ob_acc: Any
    gate_acc: Any
    gate_bias_acc: Any
    live: Any
    h: Any
    hb: Any
    hbw: Any
    hbw_t: Any
    gates: Any
    mt: Any
    dmt: Any
    dmn: Any
    dm: Any
    dgi: Any
    dgh: Any
    wib: Any
    whb: Any
    wit: Any
    wht: Any
    bcol: Any
    gt: Any
    spart: Any
    rs_in: Any
    sred: Any
    dwp: Any
    dw_in: Any
    dw_mid: Any
    dw_in2: Any
    sm_part: Any
    sm_in: Any
    sm_red: Any
    w1_part: Any
    w1_in: Any
    w1_mid: Any
    col_mask_v: Any
    w1_v: Any
    b1_v: Any
    bg_v: Any
    b2_v: Any
    group_s: Any
    edges_s: Any
    atoms_s: Any
    states_v: Any
    state_grad_v: Any
    out_rows_v: Any
    lsem: Any
    osem: Any
    w2_send: Any
    w2_recv: Any
    w2_fsend: Any
    m_send: Any
    m_recv: Any
    rs_send: Any
    rs_recv: Any
    ag_send: Any
    ag_recv: Any
    dw_send: Any
    dw_recv: Any
    dw2_send: Any
    dw2_recv: Any
    sm_send: Any
    sm_recv: Any
    sa_send: Any
    sa_recv: Any
    wr_send: Any
    wr_recv: Any
    wm_send: Any
    wm_recv: Any


def step_kernel(z, *refs):
    n_in, n_out = len(Operands._fields), len(Results._fields)
    a = Operands(*refs[:n_in])
    o = Results(*refs[n_in : n_in + n_out])
    r = Scratch(*refs[n_in + n_out :])
    atoms, edges, group = r.atoms_s, r.edges_s, r.group_s
    me, row = lax.axis_index(MOL), lax.axis_index(ROW)
    n_mol, n_row, rows, units, per = z.n_mol, z.n_row, z.rows, z.units, z.per
    width, halves = z.width, range(z.halves)
    row_at = pl.multiple_of(row * rows, rows)

    def others(index, count):
        return [lax.rem(index + step, count) for step in range(1, count)]

    def far_first(index, count):
        upper, mirror = lax.div(2 * index, count), count - 1 - index
        from_low = [at + lax.div(at + count - index, count) for at in range(count - 1)]
        from_high = [count - 1 - at - lax.div(at + count - mirror, count) for at in range(count - 1)]
        return [upper * low_at + (1 - upper) * high_at for low_at, high_at in zip(from_low, from_high)]

    def flipped(index, mask):
        bits = [1 << b for b in range(n_mol.bit_length() - 1)]
        return sum(bit * lax.rem(lax.div(index, bit) + (1 if mask & bit else 0), 2) for bit in bits)

    by_distance = sorted(range(1, n_mol), key=lambda mask: (-(mask // 2).bit_count(), -mask))
    mol_peers, row_peers = [flipped(me, mask) for mask in by_distance], far_first(row, n_row)

    def remote(source, target, send, recv, axis, device):
        return pltpu.make_async_remote_copy(
            src_ref=source,
            dst_ref=target,
            send_sem=send,
            recv_sem=recv,
            device_id={axis: device},
            device_id_type=MESH,
        )

    sent, stored = [], []

    def push(*args):
        remote(*args).start()
        sent.append(args)

    def store(source, target):
        pltpu.make_async_copy(source, target, r.osem.at[len(stored)]).start()
        stored.append((source, target))

    def arrived(there, send, recv, axis, device):
        remote(there, there, send, recv, axis, device).wait_recv()

    started = []

    def fetch(source, target):
        copy = pltpu.make_async_copy(source, target, r.lsem.at[len(started)])
        copy.start()
        started.append(copy)
        return copy

    barrier = pltpu.get_barrier_semaphore()
    for peer in mol_peers:
        pl.semaphore_signal(barrier, inc=1, device_id={MOL: peer}, device_id_type=MESH)
    for peer in row_peers:
        pl.semaphore_signal(barrier, inc=1, device_id={ROW: peer}, device_id_type=MESH)
    in_w2 = fetch(a.w2.at[0], r.w2_v) if z.fused else fetch(a.w2, r.w2s)
    in_small = (
        fetch(a.col_mask, r.col_mask_v),
        fetch(a.w1.at[0], r.w1_v),
        fetch(a.b1, r.b1_v),
        fetch(a.group, r.group_s),
        fetch(a.edges, r.edges_s),
        fetch(a.atoms, r.atoms_s),
    )
    in_src, in_dst = fetch(a.src, r.src_v), fetch(a.dst, r.dst_v)
    in_feats, in_nodes = fetch(a.feats_t, r.feats_v), fetch(a.nodes, r.nodes_v)
    in_perms = fetch(a.perm_in_c, r.perm_in), fetch(a.perm_c, r.perm)
    in_wi, in_wh = fetch(a.wi.at[0], r.wi_v), fetch(a.wh.at[0], r.wh_v)
    in_cot = fetch(a.cot, r.cot_v)
    in_bg, in_b2 = fetch(a.bg.at[0], r.bg_v), fetch(a.b2, r.b2_v)

    w2s, stage = r.w2s, r.stage
    partner = me + 1 - 2 * lax.rem(me, 2)
    same = [flipped(me, mask) for mask in by_distance if mask % 2 == 0]
    same_of_partner = [flipped(partner, mask) for mask in by_distance if mask % 2 == 0]

    some = rows // PARTS

    def block_of(ref, owner):
        return ref.at[:, pl.ds(pl.multiple_of(owner * per, 16), per), :]

    def part_of(owner, part):
        return w2s.at[pl.ds(part * some, some), pl.ds(pl.multiple_of(owner * per, 16), per), :]

    def forwards(part):
        copies = []
        for at, peer in enumerate(same):
            there, recv = part_of(peer, part), r.w2_recv.at[part, peer]
            copies.append(remote(there, there, r.w2_fsend.at[part, at], recv, MOL, partner))
        return copies

    def forward_part(part):
        for at, (peer, copy) in enumerate(zip(same, forwards(part))):
            there = part_of(peer, part)
            arrived(there, r.w2_send.at[part, at], r.w2_recv.at[part, peer], MOL, peer)
            copy.start()

    def whole_part(part):
        for peer in [partner] + same_of_partner:
            there = part_of(peer, part)
            arrived(there, r.w2_send.at[part, 0], r.w2_recv.at[part, peer], MOL, partner)

    for copy in in_small:
        copy.wait()
    lane_mol = iota((1, z.lanes), 1) // z.vpad
    lane_v = lax.rem(iota((1, z.lanes), 1), z.vpad)
    half_mol = iota((HALF, z.half_lanes), 1) // z.vpad == iota((HALF, z.half_lanes), 0)
    tile_v = hot(lax.rem(iota((z.vpad, z.half_lanes), 1), z.vpad) == iota((z.vpad, z.half_lanes), 0))
    live_to = jnp.zeros((1, z.lanes), jnp.int32)
    for m in range(z.mols):
        live_to = jnp.where(lane_mol == m, atoms[m], live_to)
    live_all = jnp.where(lane_v < live_to, 1.0, 0.0)
    for half in halves:
        lanes = slice(half * z.half_lanes, (half + 1) * z.half_lanes)
        r.live[half] = jnp.broadcast_to(live_all[:, lanes], (8, z.half_lanes))
    r.e_acc[...] = jnp.zeros(r.e_acc.shape, f32)
    r.dw_acc[...] = jnp.zeros(r.dw_acc.shape, f32)
    r.ob_acc[...] = jnp.zeros(r.ob_acc.shape, f32)

    mask_cols = jnp.concatenate(
        [r.col_mask_v[...].astype(f32), jnp.zeros((8 - a.col_mask.shape[0], z.feats), f32)], axis=0
    )
    mask_cols = jnp.concatenate([mask_cols, jnp.zeros((8, LANES - z.feats), f32)], axis=1).T
    masks = [low(jnp.broadcast_to(mask_cols[: z.feats, g : g + 1], (z.feats, z.edges))) for g in (0, 1)]
    w1_low = low(r.w1_v[...])
    b1_row = r.b1_v[0:1, :]

    if z.fused:
        in_w2.wait()
        for i in range(rows):
            stage[i] = low(r.w2_v[:, i * LANES : (i + 1) * LANES])
        w2s[:, pl.ds(pl.multiple_of(me * per, 16), per), :] = stage[...]
    pl.semaphore_wait(barrier, n_mol - 1 + n_row - 1)
    if z.fused:
        for part in range(PARTS):
            for at, peer in enumerate(same + [partner]):
                push(
                    stage.at[pl.ds(part * some, some)],
                    part_of(me, part),
                    r.w2_send.at[part, at],
                    r.w2_recv.at[part, me],
                    MOL,
                    peer,
                )

    s2, hid, idx, counts = r.s2, r.hid, r.idx, r.counts
    for copy in (in_src, in_dst, in_feats):
        copy.wait()
    lines = z.edges // LANES
    edge_at = iota((1, z.edges), 1)
    v_id = low(iota((z.vpad, z.edges), 0).astype(f32))
    one, zero = jnp.ones((), bf16), jnp.zeros((), bf16)

    def pair_hots(ends, count):
        from_all = low(jnp.broadcast_to(ends[0:1], (z.vpad, z.edges)))
        to_all = low(jnp.broadcast_to(ends[1:2], (z.vpad, z.edges)))
        to_hot = jnp.where(to_all == v_id, one, zero)
        from_hot = jnp.where(from_all == v_id, one, zero)
        pair_hot = [
            jnp.where(from_all == jnp.full((), w, bf16), to_hot, zero) for w in range(count)
        ]
        return from_hot, to_hot, jnp.concatenate(pair_hot, axis=0)

    def one_molecule(half, m8):
        m = half * HALF + m8
        at = pl.multiple_of(m * z.edges, z.edges)
        base = (me * z.mols + m) * z.cap
        kept = jnp.where(group[m] == 1, masks[1], masks[0])
        feats_m = r.feats_v[:, pl.ds(at, z.edges)] * kept
        r.feats_v[:, pl.ds(at, z.edges)] = feats_m
        hidden = low(jnp.maximum(dot_tn(feats_m, w1_low) + b1_row, 0.0))
        hid[m] = hidden.T

        def line(ref):
            return jnp.concatenate(
                [ref[pl.ds(m * lines + t, 1), :] for t in range(lines)], axis=1
            )

        from_at = line(r.src_v) - base
        to_at = jnp.where(edge_at < edges[m], line(r.dst_v) - base, 2 * z.vpad)
        ends = jnp.concatenate([from_at, to_at, jnp.zeros((6, z.edges), jnp.int32)], axis=0)
        ends = ends.astype(f32)
        idx[m] = ends
        from_hot, to_hot, pair_hot = pair_hots(ends, z.cap)
        sums = low(dot(pair_hot, hidden))
        for w in range(z.cap):
            s2[half, m8 * z.vpad : (m8 + 1) * z.vpad, w * units : (w + 1) * units] = sums[
                w * z.vpad : (w + 1) * z.vpad
            ]
        found = dot(low(dot_nt(from_hot, to_hot)), tile_v)
        found = jnp.where(iota(found.shape, 1) // z.vpad == m8, found, 0.0)
        counts[half, :, m8 : m8 + 1, :] = found[: z.wpad].reshape(z.wpad, 1, z.half_lanes)

    def half_sums(half, carry):
        s2[half, :, z.cap * units :] = jnp.zeros((z.half_lanes, (z.wpad - z.cap) * units), bf16)
        for m8 in range(HALF):
            one_molecule(half, m8)
        r.cnt[half] = low(counts[half].reshape(z.half_rows, z.half_lanes))
        return carry

    lax.fori_loop(0, z.halves, half_sums, 0)
    if z.fused:
        for part in range(PARTS):
            forward_part(part)

    h, hb, hbw, hbw_t = r.h, r.hb, r.hbw, r.hbw_t
    for copy in (in_nodes, *in_perms):
        copy.wait()

    def set_rows(layer, half):
        hb[layer, half] = low(h[layer, half])
        hbw[layer, half] = low(dot_nt(r.perm[...], hb[layer, half]))
        hbw_t[layer, half] = low(dot_nt(hb[layer, half], r.perm[...]))

    def rows_in(value, target):
        moved = dot_tn(value, r.perm_in[...])
        for half in halves:
            target[half] = moved[:, half * z.half_lanes : (half + 1) * z.half_lanes]

    rows_in(r.nodes_v[...], h.at[0])
    for half in halves:
        set_rows(0, half)
    wib, whb, wit, wht, bcol = r.wib, r.whb, r.wit, r.wht, r.bcol
    in_b2.wait()
    b2_low = low(
        jnp.concatenate([r.b2_v[0:1, i * LANES : (i + 1) * LANES] for i in range(rows)], axis=0)
    )

    if not z.fused:
        in_w2.wait()

    t2, mt, gates = r.t2, r.mt, r.gates

    def two(at):
        return slice(at * 2 * units, (at + 1) * 2 * units)

    def wide(block):
        return jnp.concatenate([block] * (z.half_lanes // LANES), axis=1)

    def spread(layer, half, part):
        state = hbw[layer, half]

        def pair(at):
            ip = part * (some // 2) + at
            both = dot_nt(state, w2s[2 * ip : 2 * ip + 2].reshape(2 * units, width))
            at = ip * 2 * HALF
            for w in range(z.wpad):
                s = slice(w * HALF, (w + 1) * HALF)
                t2[layer, half, pl.ds(at, 2 * HALF), w * units : (w + 1) * units] = low(
                    jnp.concatenate([both[s, :units], both[s, units:]], axis=0)
                )

        for at in range(some // 2):
            pair(at)

    def messages(layer, half):
        state = hbw[layer, half]
        bias = dot(low(dot_nt(b2_low, state)), r.cnt[half])
        full = dot_nt(t2[layer, half], s2[half]).reshape(rows, HALF, z.half_lanes)
        full = jnp.where(half_mol[None], full + bias[:, None, :], 0.0)
        mt[layer, half, pl.ds(row_at, rows), :] = low(jnp.sum(full, axis=1))
        share(mt, r.m_send, r.m_recv, layer, half)

    def row_pushes(ref, send, recv, layer, half):
        mine = ref.at[layer, half, pl.ds(row_at, rows), :]
        return [
            remote(mine, mine, send.at[layer, half, at], recv.at[layer, half, row], ROW, peer)
            for at, peer in enumerate(row_peers)
        ]

    def share(*args):
        for copy in row_pushes(*args):
            copy.start()

    def collect(ref, send, recv, layer, half):
        for peer in row_peers:
            there = ref.at[layer, half, pl.ds(pl.multiple_of(peer * rows, rows), rows), :]
            arrived(there, send.at[layer, half, 0], recv.at[layer, half, peer], ROW, peer)

    def state_side(layer, half):
        gates[layer, half, 0] = dot(wht[...], hb[layer, half]) + wide(bcol[1])

    def gru(layer, half):
        collect(mt, r.m_send, r.m_recv, layer, half)
        from_msg = dot(wit[...], mt[layer, half]) + wide(bcol[0])
        from_state = gates[layer, half, 0]
        reset = jax.nn.sigmoid(from_msg[:width] + from_state[:width])
        update = jax.nn.sigmoid(from_msg[width : 2 * width] + from_state[width : 2 * width])
        new = jnp.tanh(from_msg[2 * width :] + reset * from_state[2 * width :])
        gates[layer, half, 1, :width] = reset
        gates[layer, half, 1, width : 2 * width] = update
        gates[layer, half, 1, 2 * width :] = new
        h[layer + 1, half] = r.live[half, 0:1] * ((1.0 - update) * new + update * h[layer, half])

    gt, dgi, dgh, dm, dmt, dmn = r.gt, r.dgi, r.dgh, r.dm, r.dmt, r.dmn
    d2, spart, sred = r.d2, r.spart, r.sred

    def gru_back(layer, half):
        up = gt[half] * r.live[half, 0:1]
        reset = gates[layer, half, 1, :width]
        update = gates[layer, half, 1, width : 2 * width]
        new = gates[layer, half, 1, 2 * width :]
        d_new = up * (1.0 - update) * (1.0 - new * new)
        d_update = up * (h[layer, half] - new) * update * (1.0 - update)
        d_reset = d_new * gates[layer, half, 0, 2 * width :] * reset * (1.0 - reset)
        msg_side = low(jnp.concatenate([d_reset, d_update, d_new], axis=0))
        dgi[layer, half] = msg_side
        dgh[layer, half, : 2 * width] = msg_side[: 2 * width]
        dgh[layer, half, 2 * width :] = low(d_new * reset)
        part = low(dot(wib[pl.ds(row_at, rows), :], msg_side))
        dm[layer, half] = part
        spread = jnp.where(half_mol[None], part.astype(f32)[:, None, :], 0.0)
        spread = spread.reshape(rows * HALF, z.half_lanes)
        dmt[layer, half] = low(spread)
        dmn[layer, half] = low(spread.T)
        gt[half] = up * update + dot(whb[...], dgh[layer, half])

    def gathered(layer, half):
        def pair(wp):
            lanes = two(wp)
            both = dot(dmt[layer, half], s2[half, :, lanes])
            at = wp * 2 * HALF
            for i in range(rows):
                part = both[i * HALF : (i + 1) * HALF]
                d2[pl.ds(at, 2 * HALF), i * units : (i + 1) * units] = low(
                    jnp.concatenate([part[:, :units], part[:, units:]], axis=0)
                )

        for wp in range(z.wpad // 2):
            pair(wp)

    def bias_rows(layer, half):
        return low(dot_nt(dm[layer, half], r.cnt[half]))

    def state_part(layer, half):
        biases = bias_rows(layer, half)
        r.ob_acc[...] += dot(biases, hbw[layer, half])
        back = dot(d2[...], w2s[...].reshape(rows * units, width)) + dot_tn(biases, b2_low)
        spart[layer, half] = low(dot_tn(low(back), r.perm[...]))
        for copy in part_pushes(layer, half):
            copy.start()

    def part_pushes(layer, half):
        return [
            remote(
                spart.at[layer, half, pl.ds(pl.multiple_of(peer * rows, rows), rows), :],
                r.rs_in.at[layer, half, row],
                r.rs_send.at[layer, half, at],
                r.rs_recv.at[layer, half, row],
                ROW,
                peer,
            )
            for at, peer in enumerate(row_peers)
        ]

    def state_sum(layer, half):
        total = spart[layer, half, pl.ds(row_at, rows), :].astype(f32)
        for peer in row_peers:
            there = r.rs_in.at[layer, half, peer]
            arrived(there, r.rs_send.at[layer, half, 0], r.rs_recv.at[layer, half, peer], ROW, peer)
            total = total + r.rs_in[layer, half, peer].astype(f32)
        sred[layer, half, pl.ds(row_at, rows), :] = low(total)
        share(sred, r.ag_send, r.ag_recv, layer, half)

    def settle():
        def one_step(t, carry):
            layer, half = lax.div(t, z.halves), lax.rem(t, z.halves)
            for copy in row_pushes(mt, r.m_send, r.m_recv, layer, half):
                copy.wait_send()
            for copy in part_pushes(layer, half):
                copy.wait_send()
            for copy in row_pushes(sred, r.ag_send, r.ag_recv, layer, half):
                copy.wait_send()
            return carry

        lax.fori_loop(0, LAYERS * z.halves, one_step, 0)
        for args in sent:
            remote(*args).wait_send()
        for copy in small_copies():
            copy.wait_send()
        if z.fused:
            for copy in pair_copies():
                copy.wait_send()
            for part in range(PARTS):
                for copy in forwards(part):
                    copy.wait_send()

    def rows_out(value):
        total = None
        for half in halves:
            rest = value(half)
            lanes = slice(half * z.half_lanes, (half + 1) * z.half_lanes)
            for _ in range(3):
                part = low(rest)
                rest = rest - part.astype(f32)
                moved = dot_nt(r.perm_in[:, lanes], part)
                total = moved if total is None else total + moved
        return total

    dwp, dw_acc, e2, e_acc = r.dwp, r.dw_acc, r.e2, r.e_acc

    def weight_grad(layer, half):
        for ip in range(rows // 2):
            at = two(ip)
            dw_acc[:, at] += dot(hbw_t[layer, half], d2[:, at])

    def pair_grad(layer, half):
        for wp in range(z.wpad // 2):
            at = two(wp)
            total = e_acc[half, :, at] + dot(dmn[layer, half], t2[layer, half, :, at])
            e_acc[half, :, at] = total
            e2[half, :, at] = low(total)

    def gate_weights():
        in_wi.wait()
        in_wh.wait()
        wib[...] = low(r.wi_v[...])
        whb[...] = low(r.wh_v[...])
        wit[...] = low(r.wi_v[...].T)
        wht[...] = low(r.wh_v[...].T)
        in_cot.wait()
        in_bg.wait()
        bias_t = jnp.concatenate([r.bg_v[...], jnp.zeros((6, 3 * width), f32)], axis=0).T
        for side in range(2):
            bcol[side] = jnp.broadcast_to(bias_t[:, side : side + 1], (3 * width, LANES))
        rows_in(r.cot_v[...], r.gt)
        for half in halves:
            state_side(0, half)

    def forward_step(t, carry):
        layer, half = lax.div(t, z.halves), lax.rem(t, z.halves)

        @pl.when(layer > 0)
        def _():
            gru(layer - 1, half)
            set_rows(layer, half)

        for part in range(PARTS):
            if z.fused and part > 0:
                pl.when(t == 0)(functools.partial(whole_part, part))
            spread(layer, half, part)
        messages(layer, half)
        pl.when(t == z.halves - 1)(gate_weights)
        pl.when(layer > 0)(functools.partial(state_side, layer, half))
        return carry

    if z.fused:
        whole_part(0)
    lax.fori_loop(0, LAYERS * z.halves, forward_step, 0)

    last = LAYERS - 1

    ones = jnp.ones((8, z.lanes), bf16)

    def beside(ref, layer):
        return jnp.concatenate([ref[layer, half] for half in halves], axis=1)

    def gate_sums(layer):
        sums = []
        for at, (side, grads) in enumerate(((mt, dgi), (hb, dgh))):
            grads = beside(grads, layer)
            sums.append((dot_nt(beside(side, layer), grads), dot_nt(ones, grads)))
        return sums

    def back_half(layer, half):
        @pl.when(layer == last)
        def _():
            gru(last, half)

        @pl.when(layer < last)
        def _():
            collect(sred, r.ag_send, r.ag_recv, layer + 1, half)
            gt[half] += sred[layer + 1, half].astype(f32)

        gru_back(layer, half)
        gathered(layer, half)
        state_part(layer, half)
        weight_grad(layer, half)

    def pair_half(layer, half):
        pair_grad(layer, half)
        pl.when(layer == last)(functools.partial(state_sum, last, half))

    theirs = [lax.rem(partner + 2 * step, n_mol) for step in range(n_mol // 2)]
    ours = [lax.rem(me + 2 * step, n_mol) for step in range(n_mol // 2)]

    def pair_copies():
        return [
            remote(block_of(dwp, owner), r.dw_in.at[at], r.dw_send.at[at], r.dw_recv.at[at], MOL, partner)
            for at, owner in enumerate(theirs)
        ]

    def weight_out():
        for i in range(rows):
            dwp[i] = low(dw_acc[:, i * units : (i + 1) * units]).T
        if z.fused:
            for copy in pair_copies():
                copy.start()

    def backward_layer(t, carry):
        layer = last - t
        lax.fori_loop(0, z.halves, lambda half, c: back_half(layer, half) or c, 0)
        pl.when(layer == 0)(weight_out)
        lax.fori_loop(0, z.halves, lambda half, c: pair_half(layer, half) or c, 0)

        @pl.when(layer == last)
        def _():
            r.states_v[...] = rows_out(lambda half: h[LAYERS, half])
            store(r.states_v, o.states)
            for at, (weight, bias) in enumerate(gate_sums(last)):
                r.gate_acc[at], r.gate_bias_acc[at] = weight, bias

        return carry

    lax.fori_loop(0, LAYERS, backward_layer, 0)

    sm_part, sm_in = r.sm_part, r.sm_in
    bias_lines = []
    for at, (weight, bias) in enumerate(gate_sums(0)):
        weight, bias = weight + r.gate_acc[at], bias + r.gate_bias_acc[at]
        for third in range(3):
            first = (3 * at + third) * width
            sm_part[first : first + width, :] = low(weight[:, third * width : (third + 1) * width])
        bias_lines += [bias[0:1, third * width : (third + 1) * width] for third in range(3)]
    bias_lines.append(jnp.zeros((10, width), f32))
    sm_part[z.gate_rows : z.gate_rows + 16, :] = low(jnp.concatenate(bias_lines, axis=0))
    sm_part[z.gate_rows + 16 : z.small_rows, :] = low(r.ob_acc[...])
    if z.chunk * n_mol > z.small_rows:
        sm_part[z.small_rows :, :] = jnp.zeros((z.chunk * n_mol - z.small_rows, width), bf16)

    def chunk_of(ref, owner):
        return ref.at[pl.ds(pl.multiple_of(owner * z.chunk, 16), z.chunk), :]

    for at, peer in enumerate(mol_peers):
        push(chunk_of(sm_part, peer), sm_in.at[me], r.sm_send.at[at], r.sm_recv.at[me], MOL, peer)
    if z.fused:
        for at, owner in enumerate(ours):
            arrived(r.dw_in.at[at], r.dw_send.at[at], r.dw_recv.at[at], MOL, partner)
            own = dwp[:, pl.ds(pl.multiple_of(owner * per, 16), per), :].astype(f32)
            r.dw_mid[at] = low(own + r.dw_in[at].astype(f32))
            if at > 0:
                push(r.dw_mid.at[at], r.dw_in2.at[at], r.dw2_send.at[at], r.dw2_recv.at[at], MOL, owner)

    def small_copies():
        return [
            remote(r.sm_red, chunk_of(o.small_out, me), r.sa_send.at[at], r.sa_recv.at[me], MOL, peer)
            for at, peer in enumerate(mol_peers)
        ]

    def between():
        for half in halves:
            state_sum(0, half)

    def summed(pieces):
        return functools.reduce(jnp.add, pieces)

    def edge_grad(half, m8):
        m = half * HALF + m8
        at = pl.multiple_of(m * z.edges, z.edges)
        _, _, pair_hot = pair_hots(idx[m], z.wpad)
        slot = slice(m8 * z.vpad, (m8 + 1) * z.vpad)
        grads = [e2[half, slot, w * units : (w + 1) * units] for w in range(z.wpad)]
        d_hidden = dot_tn(jnp.concatenate(grads, axis=0), pair_hot)
        d_pre = low(jnp.where(hid[m].astype(f32) > 0.0, d_hidden, 0.0))
        feats_m = r.feats_v[:, pl.ds(at, z.edges)]
        feats_m = jnp.concatenate([feats_m, jnp.ones((16, z.edges), bf16)], axis=0)
        return dot_nt(d_pre, feats_m)

    def half_grad(half, total):
        total = total + summed([edge_grad(half, m8) for m8 in range(HALF)])
        pl.when(half == 0)(between)
        return total

    total = lax.fori_loop(0, z.halves, half_grad, jnp.zeros((units, z.feats + 16), f32))
    w1_part, w1_in, w1_mid = r.w1_part, r.w1_in, r.w1_mid
    total = jnp.concatenate([total, jnp.zeros((units, LANES - z.feats - 16), f32)], axis=1).T
    w1_part[...] = total[: z.feats + 8]
    for at, peer in enumerate(row_peers):
        push(w1_part, w1_in.at[row], r.wr_send.at[at], r.wr_recv.at[row], ROW, peer)
    w1_in[row] = w1_part[...]

    total = sm_part[pl.ds(pl.multiple_of(me * z.chunk, 16), z.chunk), :].astype(f32)
    for peer in mol_peers:
        arrived(sm_in.at[peer], r.sm_send.at[0], r.sm_recv.at[peer], MOL, peer)
        total = total + sm_in[peer].astype(f32)
    r.sm_red[...] = low(total)
    for copy in small_copies():
        copy.start()
    store(r.sm_red, chunk_of(o.small_out, me))
    for peer in row_peers:
        arrived(w1_in.at[peer], r.wr_send.at[0], r.wr_recv.at[peer], ROW, peer)
    total = w1_in[0]
    for at in range(1, n_row):
        total = total + w1_in[at]
    w1_mid[...] = total
    for at, peer in enumerate(mol_peers):
        push(w1_mid, o.w1_out.at[me], r.wm_send.at[at], r.wm_recv.at[me], MOL, peer)
    store(w1_mid, o.w1_out.at[me])

    for half in halves:
        collect(sred, r.ag_send, r.ag_recv, 0, half)
    r.state_grad_v[...] = rows_out(lambda half: gt[half] + sred[0, half].astype(f32))
    store(r.state_grad_v, o.state_grad)
    settle()
    if z.fused:
        total = r.dw_mid[0].astype(f32)
        for at in range(1, n_mol // 2):
            arrived(r.dw_in2.at[at], r.dw2_send.at[at], r.dw2_recv.at[at], MOL, partner)
            total = total + r.dw_in2[at].astype(f32)
        for i in range(rows):
            r.out_rows_v[:, i * LANES : (i + 1) * LANES] = total[i]
        store(r.out_rows_v, o.out_rows)
    else:
        store(dwp, o.out_rows)
    for peer in mol_peers:
        arrived(o.w1_out.at[peer], r.wm_send.at[0], r.wm_recv.at[peer], MOL, peer)
    for peer in mol_peers:
        arrived(chunk_of(o.small_out, peer), r.sa_send.at[0], r.sa_recv.at[peer], MOL, peer)
    for at, (source, target) in enumerate(stored):
        pltpu.make_async_copy(source, target, r.osem.at[at]).wait()


def run_step(z, args, w2_all):
    (node_states, edge_feats, edge_src, edge_dst, atom_counts, edge_counts, mol_group, col_mask,
     cotangent, edge_in_state, edge_in_bias_state, edge_out_state, edge_out_bias_state,
     gate_in_state, gate_hidden_state, gate_bias_state) = args
    any_spec = pl.BlockSpec(memory_space=pl.ANY)
    v = pltpu.VMEM
    dma = pltpu.SemaphoreType.DMA
    rows, width, units, per = z.rows, z.width, z.units, z.per
    n_mol, n_row, halves = z.n_mol, z.n_row, z.halves
    half_rows, half_lanes = z.half_rows, z.half_lanes
    both = (LAYERS, halves)
    full = rows * HALF
    lines = (z.mols * z.edges // LANES, LANES)
    step_in = (rows, per, LANES)
    lane = np.arange(z.lanes)
    lane_mol, lane_v = lane // z.vpad, lane % z.vpad
    node = np.where(lane_v < z.cap, lane_mol * z.cap + lane_v, -1)
    perm_in = (np.arange(z.nodes)[:, None] == node[None, :]).astype(np.float32)
    row_at = np.arange(half_rows)
    row_lane = (row_at % HALF) * z.vpad + row_at // HALF
    perm = (row_lane[:, None] == np.arange(half_lanes)[None, :]).astype(np.float32)
    operands = Operands(
        nodes=(node_states, any_spec),
        feats_t=(edge_feats.T, any_spec),
        src=(edge_src.reshape(lines), any_spec),
        dst=(edge_dst.reshape(lines), any_spec),
        atoms=(atom_counts, any_spec),
        edges=(edge_counts, any_spec),
        group=(mol_group, any_spec),
        col_mask=(col_mask, any_spec),
        cot=(cotangent, any_spec),
        w1=(edge_in_state, any_spec),
        b1=(edge_in_bias_state, any_spec),
        w2=(edge_out_state if z.fused else w2_all, any_spec),
        b2=(edge_out_bias_state, any_spec),
        wi=(gate_in_state, any_spec),
        wh=(gate_hidden_state, any_spec),
        bg=(gate_bias_state, any_spec),
        perm_in_c=(jnp.asarray(perm_in, bf16), any_spec),
        perm_c=(jnp.asarray(perm, bf16), any_spec),
    )
    outs = [
        jax.ShapeDtypeStruct((z.nodes, width), f32),
        jax.ShapeDtypeStruct((z.nodes, width), f32),
        jax.ShapeDtypeStruct((per, rows * width), f32)
        if z.fused
        else jax.ShapeDtypeStruct((rows, units, width), bf16),
        jax.ShapeDtypeStruct((n_mol * z.chunk, width), bf16),
        jax.ShapeDtypeStruct((n_mol, z.feats + 8, units), f32),
    ]
    row_sems = dma(both + (n_row,))
    mol_sems = dma((n_mol,))
    scratch = Scratch(
        nodes_v=v((z.nodes, width), bf16),
        feats_v=v((z.feats, z.mols * z.edges), bf16),
        src_v=v(lines, jnp.int32),
        dst_v=v(lines, jnp.int32),
        cot_v=v((z.nodes, width), bf16),
        w2_v=v((per, rows * width), f32),
        wi_v=v((width, 3 * width), f32),
        wh_v=v((width, 3 * width), f32),
        perm_in=v((z.nodes, z.lanes), bf16),
        perm=v((half_rows, half_lanes), bf16),
        w2s=v((rows, units, width), bf16),
        stage=v(step_in, bf16),
        hid=v((z.mols, units, z.edges), bf16),
        idx=v((z.mols, 8, z.edges), f32),
        s2=v((halves, half_lanes, z.span), bf16),
        counts=v((halves, z.wpad, HALF, half_lanes), f32),
        cnt=v((halves, half_rows, half_lanes), bf16),
        t2=v(both + (full, z.span), bf16),
        d2=v((half_rows, rows * units), bf16),
        e2=v((halves, half_lanes, z.span), bf16),
        e_acc=v((halves, half_lanes, z.span), f32),
        dw_acc=v((width, rows * units), f32),
        ob_acc=v((rows, width), f32),
        gate_acc=v((2, width, 3 * width), f32),
        gate_bias_acc=v((2, 8, 3 * width), f32),
        live=v((halves, 8, half_lanes), f32),
        h=v((LAYERS + 1, halves, width, half_lanes), f32),
        hb=v(both + (width, half_lanes), bf16),
        hbw=v(both + (half_rows, width), bf16),
        hbw_t=v(both + (width, half_rows), bf16),
        gates=v(both + (2, 3 * width, half_lanes), f32),
        mt=v(both + (width, half_lanes), bf16),
        dmt=v(both + (full, half_lanes), bf16),
        dmn=v(both + (half_lanes, full), bf16),
        dm=v(both + (rows, half_lanes), bf16),
        dgi=v(both + (3 * width, half_lanes), bf16),
        dgh=v(both + (3 * width, half_lanes), bf16),
        wib=v((width, 3 * width), bf16),
        whb=v((width, 3 * width), bf16),
        wit=v((3 * width, width), bf16),
        wht=v((3 * width, width), bf16),
        bcol=v((2, 3 * width, LANES), f32),
        gt=v((halves, width, half_lanes), f32),
        spart=v(both + (width, half_lanes), bf16),
        rs_in=v(both + (n_row, rows, half_lanes), bf16),
        sred=v(both + (width, half_lanes), bf16),
        dwp=v((rows, units, width), bf16),
        dw_in=v((n_mol // 2,) + step_in, bf16),
        dw_mid=v((n_mol // 2,) + step_in, bf16),
        dw_in2=v((n_mol // 2,) + step_in, bf16),
        sm_part=v((n_mol * z.chunk, width), bf16),
        sm_in=v((n_mol, z.chunk, width), bf16),
        sm_red=v((z.chunk, width), bf16),
        w1_part=v((z.feats + 8, units), f32),
        w1_in=v((n_row, z.feats + 8, units), f32),
        w1_mid=v((z.feats + 8, units), f32),
        col_mask_v=v(col_mask.shape, jnp.int32),
        w1_v=v(edge_in_state.shape[1:], f32),
        b1_v=v(edge_in_bias_state.shape, f32),
        bg_v=v(gate_bias_state.shape[1:], f32),
        b2_v=v(edge_out_bias_state.shape, f32),
        group_s=pltpu.SMEM(mol_group.shape, jnp.int32),
        edges_s=pltpu.SMEM(edge_counts.shape, jnp.int32),
        atoms_s=pltpu.SMEM(atom_counts.shape, jnp.int32),
        states_v=v((z.nodes, width), f32),
        state_grad_v=v((z.nodes, width), f32),
        out_rows_v=v((per, rows * width), f32),
        lsem=dma((len(operands),)),
        osem=dma((8,)),
        w2_send=dma((PARTS, n_mol)),
        w2_recv=dma((PARTS, n_mol)),
        w2_fsend=dma((PARTS, n_mol)),
        m_send=row_sems,
        m_recv=row_sems,
        rs_send=row_sems,
        rs_recv=row_sems,
        ag_send=row_sems,
        ag_recv=row_sems,
        dw_send=mol_sems,
        dw_recv=mol_sems,
        dw2_send=mol_sems,
        dw2_recv=mol_sems,
        sm_send=mol_sems,
        sm_recv=mol_sems,
        sa_send=mol_sems,
        sa_recv=mol_sems,
        wr_send=dma((n_row,)),
        wr_recv=dma((n_row,)),
        wm_send=mol_sems,
        wm_recv=mol_sems,
    )
    return pl.pallas_call(
        functools.partial(step_kernel, z),
        out_shape=outs,
        in_specs=[spec for _, spec in operands],
        out_specs=[any_spec] * len(outs),
        scratch_shapes=list(scratch),
        compiler_params=pltpu.CompilerParams(
            collective_id=0, has_side_effects=True, vmem_limit_bytes=VMEM_BYTES
        ),
        name="step",
    )(*[array for array, _ in operands])


def nesterov(state, grad, rate, out):
    scaled = rate * grad
    moment = momentum_coef * state[1] + scaled
    weight = state[0] - (scaled + momentum_coef * moment)
    out[0] = weight
    out[1] = moment
    out[2] = average_decay * state[2] + (1.0 - average_decay) * weight


def nesterov_line(state, grad, rate, out):
    scaled = rate * grad
    moment = momentum_coef * state[1:2, :] + scaled
    weight = state[0:1, :] - (scaled + momentum_coef * moment)
    out[0:1, :] = weight
    out[1:2, :] = moment
    out[2:3, :] = average_decay * state[2:3, :] + (1.0 - average_decay) * weight


class Update(NamedTuple):
    states: Any
    state_grad: Any
    out_rows: Any
    small: Any
    w1_sum: Any
    w1: Any
    b1: Any
    w2: Any
    b2: Any
    wi: Any
    wh: Any
    bg: Any


class Updated(NamedTuple):
    states: Any
    state_grad: Any
    w1_g: Any
    w1_n: Any
    b1_g: Any
    b1_n: Any
    w2_g: Any
    w2_n: Any
    b2_g: Any
    b2_n: Any
    wi_g: Any
    wi_n: Any
    wh_g: Any
    wh_n: Any
    bg_g: Any
    bg_n: Any


def update_kernel(z, rates, *refs):
    n_in, n_out = len(Update._fields), len(Updated._fields)
    given, out = Update(*refs[:n_in]), Updated(*refs[n_in : n_in + n_out])
    refs = refs[n_in + n_out :]
    here, new = Update(*refs[:n_in]), Updated(*refs[n_in : n_in + n_out])
    in_sem, out_sem = refs[n_in + n_out :]
    rate_in, rate_out, rate_gate = rates
    width = z.width
    sent = []

    def send(source, target):
        copy = pltpu.make_async_copy(source, target, out_sem.at[len(sent)])
        copy.start()
        sent.append(copy)

    fetched = Update(
        *[pltpu.make_async_copy(given[at], here[at], in_sem.at[at]) for at in range(n_in)]
    )
    order = (fetched.wi, fetched.small, fetched.wh, fetched.w2, fetched.out_rows)
    passed = (fetched.states, fetched.state_grad)
    rest = (fetched.bg, fetched.b2, fetched.w1, fetched.b1, fetched.w1_sum)
    for copy in order + passed + rest:
        copy.start()

    def thirds(at):
        parts = [here.small[(3 * at + t) * width : (3 * at + t + 1) * width, :] for t in range(3)]
        return jnp.concatenate(parts, axis=1).astype(f32)

    fetched.wi.wait()
    fetched.small.wait()
    total = thirds(0)
    new.wi_g[...] = total
    nesterov(here.wi, total, rate_gate, new.wi_n)
    send(new.wi_g, out.wi_g)
    send(new.wi_n, out.wi_n)
    fetched.wh.wait()
    total = thirds(1)
    new.wh_g[...] = total
    nesterov(here.wh, total, rate_gate, new.wh_n)
    send(new.wh_g, out.wh_g)
    send(new.wh_n, out.wh_n)
    fetched.w2.wait()
    fetched.out_rows.wait()
    send(here.out_rows, out.w2_g)
    nesterov(here.w2, here.out_rows[...], rate_out, new.w2_n)
    send(new.w2_n, out.w2_n)
    for copy in passed + rest:
        copy.wait()
    send(here.states, out.states)
    send(here.state_grad, out.state_grad)
    lines = here.small[z.gate_rows : z.gate_rows + 16, :].astype(f32)
    total = jnp.concatenate(
        [
            jnp.concatenate([lines[3 * side + t : 3 * side + t + 1, :] for t in range(3)], axis=1)
            for side in range(2)
        ],
        axis=0,
    )
    new.bg_g[...] = total
    nesterov(here.bg, total, rate_gate, new.bg_n)
    send(new.bg_g, out.bg_g)
    send(new.bg_n, out.bg_n)
    total = here.small[z.gate_rows + 16 : z.gate_rows + 16 + z.rows, :].astype(f32)
    new.b2_g[...] = total
    total = jnp.concatenate([total[i : i + 1, :] for i in range(z.rows)], axis=1)
    nesterov_line(here.b2, total, rate_out, new.b2_n)
    send(new.b2_g, out.b2_g)
    send(new.b2_n, out.b2_n)
    w1_sum = sum(here.w1_sum[at] for at in range(z.n_mol))
    total = w1_sum[: z.feats, :]
    new.w1_g[...] = total
    nesterov(here.w1, total, rate_in, new.w1_n)
    send(new.w1_g, out.w1_g)
    send(new.w1_n, out.w1_n)
    total = w1_sum[z.feats : z.feats + 1, :]
    new.b1_g[...] = total
    nesterov_line(here.b1, total, rate_in, new.b1_n)
    send(new.b1_g, out.b1_g)
    send(new.b1_n, out.b1_n)
    for copy in sent:
        copy.wait()


def per_device(mesh, *args):
    (node_states, edge_feats, edge_src, edge_dst, atom_counts, edge_counts, mol_group, col_mask,
     cotangent, edge_in_state, edge_in_bias_state, edge_out_state, edge_out_bias_state,
     gate_in_state, gate_hidden_state, gate_bias_state) = args
    z = Sizes(mesh, node_states, edge_feats, atom_counts, edge_in_state, edge_out_bias_state)
    w2_all = None
    if not z.fused:
        w2_all = lax.all_gather(low(edge_out_state[0]), "mol", axis=0, tiled=True)
        w2_all = w2_all.reshape(z.units, z.rows, z.width).swapaxes(0, 1)
    states, state_grad, out_rows, small, w1_sum = run_step(z, args, w2_all)
    if not z.fused:
        out_rows = out_rows.swapaxes(0, 1).reshape(z.units, z.rows * z.width)
        out_rows = lax.psum_scatter(out_rows, "mol", scatter_dimension=0, tiled=True).astype(f32)
    edges_all = edge_feats.shape[0] * z.n_mol
    nodes_all = z.nodes * z.n_mol
    rates = (
        z.feats ** (-0.5) / (0.2 * edges_all**0.5),
        (z.units * z.width * 8) ** (-0.5) / (0.4 * edges_all**0.5),
        z.width ** (-0.5) / (0.5 * nodes_all**0.5),
    )
    any_spec = pl.BlockSpec(memory_space=pl.ANY)
    operands = [
        states, state_grad, out_rows, small, w1_sum, edge_in_state, edge_in_bias_state,
        edge_out_state, edge_out_bias_state, gate_in_state, gate_hidden_state, gate_bias_state,
    ]
    outs = [
        states.shape, state_grad.shape, (z.feats, z.units), edge_in_state.shape,
        (1, z.units), edge_in_bias_state.shape, out_rows.shape, edge_out_state.shape,
        (z.rows, z.width), edge_out_bias_state.shape, (z.width, 3 * z.width), gate_in_state.shape,
        (z.width, 3 * z.width), gate_hidden_state.shape, (2, 3 * z.width), gate_bias_state.shape,
    ]
    results = pl.pallas_call(
        functools.partial(update_kernel, z, rates),
        out_shape=[jax.ShapeDtypeStruct(shape, f32) for shape in outs],
        in_specs=[any_spec] * len(operands),
        out_specs=[any_spec] * len(outs),
        scratch_shapes=[pltpu.VMEM(array.shape, array.dtype) for array in operands]
        + [pltpu.VMEM(shape, f32) for shape in outs]
        + [pltpu.SemaphoreType.DMA((len(operands),)), pltpu.SemaphoreType.DMA((len(outs),))],
        compiler_params=pltpu.CompilerParams(vmem_limit_bytes=VMEM_BYTES),
        name="update",
    )(*operands)
    results = list(results)
    results[4] = results[4].reshape(-1)
    results[8] = results[8].reshape(-1)
    return tuple(results)


def solution(mesh):
    return jax.shard_map(
        functools.partial(per_device, mesh),
        mesh=mesh,
        in_specs=(
            P(MOL, None),
            P(MOL, None),
            P(MOL),
            P(MOL),
            P(MOL),
            P(MOL),
            P(MOL),
            P(),
            P(MOL, None),
            P(),
            P(),
            P(None, MOL, ROW),
            P(None, ROW),
            P(),
            P(),
            P(),
        ),
        out_specs=(
            P(MOL, None),
            P(MOL, None),
            P(),
            P(),
            P(),
            P(),
            P(MOL, ROW),
            P(None, MOL, ROW),
            P(ROW),
            P(None, ROW),
            P(),
            P(),
            P(),
            P(),
            P(),
            P(),
        ),
        check_vma=False,
    )
```

```python
import functools
from typing import Any, NamedTuple

import jax
import jax.numpy as jnp
import numpy as np
from jax import lax
from jax.experimental import pallas as pl
from jax.experimental.pallas import tpu as pltpu
from jax.sharding import PartitionSpec as P

LAYERS = 2
HALF = 8
LANES = 128
PARTS = 1
MOL, ROW = "mol", "row"
MESH = pl.DeviceIdType.MESH
VMEM_BYTES = 58 * 1024 * 1024

momentum_coef = 0.9
average_decay = 0.9
f32 = jnp.float32
bf16 = jnp.bfloat16


def dot(left, right):
    return lax.dot_general(left, right, (((1,), (0,)), ((), ())), preferred_element_type=f32)


def dot_nt(left, right):
    return lax.dot_general(left, right, (((1,), (1,)), ((), ())), preferred_element_type=f32)


def dot_tn(left, right):
    return lax.dot_general(left, right, (((0,), (0,)), ((), ())), preferred_element_type=f32)


def low(value):
    return value.astype(bf16)


def iota(shape, axis):
    return lax.broadcasted_iota(jnp.int32, shape, axis)


def hot(mask):
    return low(jnp.where(mask, 1.0, 0.0))


class Sizes:
    def __init__(self, mesh, node_states, edge_feats, atom_counts, edge_in_state, edge_out_bias_state):
        self.n_mol, self.n_row = mesh.shape["mol"], mesh.shape["row"]
        self.mols = atom_counts.shape[0]
        self.nodes, self.width = node_states.shape
        self.cap = self.nodes // self.mols
        self.edges = edge_feats.shape[0] // self.mols
        self.feats = edge_feats.shape[1]
        self.units = edge_in_state.shape[2]
        self.rows = edge_out_bias_state.shape[1] // self.width
        self.per = self.units // self.n_mol
        self.halves = self.mols // HALF
        self.vpad = 32
        self.wpad = self.cap + self.cap % 2
        self.lanes = self.mols * self.vpad
        self.half_lanes = HALF * self.vpad
        self.half_rows = HALF * self.wpad
        self.span = self.wpad * self.units
        self.fused = self.per % 16 == 0
        self.gate_rows = 6 * self.width
        self.small_rows = self.gate_rows + 16 + self.rows
        self.chunk = -(-self.small_rows // (16 * self.n_mol)) * 16


class Operands(NamedTuple):
    nodes: Any
    feats_t: Any
    src: Any
    dst: Any
    atoms: Any
    edges: Any
    group: Any
    col_mask: Any
    cot: Any
    w1: Any
    b1: Any
    w2: Any
    b2: Any
    wi: Any
    wh: Any
    bg: Any
    perm_in_c: Any
    perm_c: Any


class Results(NamedTuple):
    states: Any
    state_grad: Any
    out_rows: Any
    small_out: Any
    w1_out: Any


class Scratch(NamedTuple):
    nodes_v: Any
    feats_v: Any
    src_v: Any
    dst_v: Any
    cot_v: Any
    w2_v: Any
    wi_v: Any
    wh_v: Any
    perm_in: Any
    perm: Any
    w2s: Any
    stage: Any
    hid: Any
    idx: Any
    s2: Any
    counts: Any
    cnt: Any
    t2: Any
    d2: Any
    e2: Any
    e_acc: Any
    dw_acc: Any
    ob_acc: Any
    gate_acc: Any
    gate_bias_acc: Any
    live: Any
    h: Any
    hb: Any
    hbw: Any
    hbw_t: Any
    gates: Any
    mt: Any
    dmt: Any
    dmn: Any
    dm: Any
    dgi: Any
    dgh: Any
    wib: Any
    whb: Any
    wit: Any
    wht: Any
    bcol: Any
    gt: Any
    spart: Any
    rs_in: Any
    sred: Any
    dwp: Any
    dw_in: Any
    dw_mid: Any
    dw_in2: Any
    sm_part: Any
    sm_in: Any
    sm_red: Any
    w1_part: Any
    w1_in: Any
    w1_mid: Any
    col_mask_v: Any
    w1_v: Any
    b1_v: Any
    bg_v: Any
    b2_v: Any
    group_s: Any
    edges_s: Any
    atoms_s: Any
    states_v: Any
    state_grad_v: Any
    out_rows_v: Any
    lsem: Any
    osem: Any
    w2_send: Any
    w2_recv: Any
    w2_fsend: Any
    m_send: Any
    m_recv: Any
    rs_send: Any
    rs_recv: Any
    ag_send: Any
    ag_recv: Any
    dw_send: Any
    dw_recv: Any
    dw2_send: Any
    dw2_recv: Any
    sm_send: Any
    sm_recv: Any
    sa_send: Any
    sa_recv: Any
    wr_send: Any
    wr_recv: Any
    wm_send: Any
    wm_recv: Any


def step_kernel(z, *refs):
    n_in, n_out = len(Operands._fields), len(Results._fields)
    a = Operands(*refs[:n_in])
    o = Results(*refs[n_in : n_in + n_out])
    r = Scratch(*refs[n_in + n_out :])
    atoms, edges, group = r.atoms_s, r.edges_s, r.group_s
    me, row = lax.axis_index(MOL), lax.axis_index(ROW)
    n_mol, n_row, rows, units, per = z.n_mol, z.n_row, z.rows, z.units, z.per
    width, halves = z.width, range(z.halves)
    row_at = pl.multiple_of(row * rows, rows)

    def others(index, count):
        return [lax.rem(index + step, count) for step in range(1, count)]

    def far_first(index, count):
        upper, mirror = lax.div(2 * index, count), count - 1 - index
        from_low = [at + lax.div(at + count - index, count) for at in range(count - 1)]
        from_high = [count - 1 - at - lax.div(at + count - mirror, count) for at in range(count - 1)]
        return [upper * low_at + (1 - upper) * high_at for low_at, high_at in zip(from_low, from_high)]

    def flipped(index, mask):
        bits = [1 << b for b in range(n_mol.bit_length() - 1)]
        return sum(bit * lax.rem(lax.div(index, bit) + (1 if mask & bit else 0), 2) for bit in bits)

    by_distance = sorted(range(1, n_mol), key=lambda mask: (-(mask // 2).bit_count(), -mask))
    mol_peers, row_peers = [flipped(me, mask) for mask in by_distance], far_first(row, n_row)

    def remote(source, target, send, recv, axis, device):
        return pltpu.make_async_remote_copy(
            src_ref=source,
            dst_ref=target,
            send_sem=send,
            recv_sem=recv,
            device_id={axis: device},
            device_id_type=MESH,
        )

    sent, stored = [], []

    def push(*args):
        remote(*args).start()
        sent.append(args)

    def store(source, target):
        pltpu.make_async_copy(source, target, r.osem.at[len(stored)]).start()
        stored.append((source, target))

    def arrived(there, send, recv, axis, device):
        remote(there, there, send, recv, axis, device).wait_recv()

    started = []

    def fetch(source, target):
        copy = pltpu.make_async_copy(source, target, r.lsem.at[len(started)])
        copy.start()
        started.append(copy)
        return copy

    barrier = pltpu.get_barrier_semaphore()
    for peer in mol_peers:
        pl.semaphore_signal(barrier, inc=1, device_id={MOL: peer}, device_id_type=MESH)
    for peer in row_peers:
        pl.semaphore_signal(barrier, inc=1, device_id={ROW: peer}, device_id_type=MESH)
    in_w2 = fetch(a.w2.at[0], r.w2_v) if z.fused else fetch(a.w2, r.w2s)
    in_small = (
        fetch(a.col_mask, r.col_mask_v),
        fetch(a.w1.at[0], r.w1_v),
        fetch(a.b1, r.b1_v),
        fetch(a.group, r.group_s),
        fetch(a.edges, r.edges_s),
        fetch(a.atoms, r.atoms_s),
    )
    in_src, in_dst = fetch(a.src, r.src_v), fetch(a.dst, r.dst_v)
    in_feats, in_nodes = fetch(a.feats_t, r.feats_v), fetch(a.nodes, r.nodes_v)
    in_perms = fetch(a.perm_in_c, r.perm_in), fetch(a.perm_c, r.perm)
    in_wi, in_wh = fetch(a.wi.at[0], r.wi_v), fetch(a.wh.at[0], r.wh_v)
    in_cot = fetch(a.cot, r.cot_v)
    in_bg, in_b2 = fetch(a.bg.at[0], r.bg_v), fetch(a.b2, r.b2_v)

    w2s, stage = r.w2s, r.stage
    partner = me + 1 - 2 * lax.rem(me, 2)
    same = [flipped(me, mask) for mask in by_distance if mask % 2 == 0]
    same_of_partner = [flipped(partner, mask) for mask in by_distance if mask % 2 == 0]

    some = rows // PARTS

    def block_of(ref, owner):
        return ref.at[:, pl.ds(pl.multiple_of(owner * per, 16), per), :]

    def part_of(owner, part):
        return w2s.at[pl.ds(part * some, some), pl.ds(pl.multiple_of(owner * per, 16), per), :]

    def forwards(part):
        copies = []
        for at, peer in enumerate(same):
            there, recv = part_of(peer, part), r.w2_recv.at[part, peer]
            copies.append(remote(there, there, r.w2_fsend.at[part, at], recv, MOL, partner))
        return copies

    def forward_part(part):
        for at, (peer, copy) in enumerate(zip(same, forwards(part))):
            there = part_of(peer, part)
            arrived(there, r.w2_send.at[part, at], r.w2_recv.at[part, peer], MOL, peer)
            copy.start()

    def whole_part(part):
        for peer in [partner] + same_of_partner:
            there = part_of(peer, part)
            arrived(there, r.w2_send.at[part, 0], r.w2_recv.at[part, peer], MOL, partner)

    for copy in in_small:
        copy.wait()
    lane_mol = iota((1, z.lanes), 1) // z.vpad
    lane_v = lax.rem(iota((1, z.lanes), 1), z.vpad)
    half_mol = iota((HALF, z.half_lanes), 1) // z.vpad == iota((HALF, z.half_lanes), 0)
    tile_v = hot(lax.rem(iota((z.vpad, z.half_lanes), 1), z.vpad) == iota((z.vpad, z.half_lanes), 0))
    live_to = jnp.zeros((1, z.lanes), jnp.int32)
    for m in range(z.mols):
        live_to = jnp.where(lane_mol == m, atoms[m], live_to)
    live_all = jnp.where(lane_v < live_to, 1.0, 0.0)
    for half in halves:
        lanes = slice(half * z.half_lanes, (half + 1) * z.half_lanes)
        r.live[half] = jnp.broadcast_to(live_all[:, lanes], (8, z.half_lanes))

    mask_cols = jnp.concatenate(
        [r.col_mask_v[...].astype(f32), jnp.zeros((8 - a.col_mask.shape[0], z.feats), f32)], axis=0
    )
    mask_cols = jnp.concatenate([mask_cols, jnp.zeros((8, LANES - z.feats), f32)], axis=1).T
    masks = [low(jnp.broadcast_to(mask_cols[: z.feats, g : g + 1], (z.feats, z.edges))) for g in (0, 1)]
    w1_low = low(r.w1_v[...])
    b1_row = r.b1_v[0:1, :]

    if z.fused:
        in_w2.wait()
        for i in range(rows):
            stage[i] = low(r.w2_v[:, i * LANES : (i + 1) * LANES])
        w2s[:, pl.ds(pl.multiple_of(me * per, 16), per), :] = stage[...]
    pl.semaphore_wait(barrier, n_mol - 1 + n_row - 1)
    if z.fused:
        for part in range(PARTS):
            for at, peer in enumerate(same + [partner]):
                push(
                    stage.at[pl.ds(part * some, some)],
                    part_of(me, part),
                    r.w2_send.at[part, at],
                    r.w2_recv.at[part, me],
                    MOL,
                    peer,
                )

    s2, hid, idx, counts = r.s2, r.hid, r.idx, r.counts
    for copy in (in_src, in_dst, in_feats):
        copy.wait()
    lines = z.edges // LANES
    edge_at = iota((1, z.edges), 1)
    v_id = low(iota((z.vpad, z.edges), 0).astype(f32))
    one, zero = jnp.ones((), bf16), jnp.zeros((), bf16)

    def pair_hots(ends, count):
        from_all = low(jnp.broadcast_to(ends[0:1], (z.vpad, z.edges)))
        to_all = low(jnp.broadcast_to(ends[1:2], (z.vpad, z.edges)))
        to_hot = jnp.where(to_all == v_id, one, zero)
        from_hot = jnp.where(from_all == v_id, one, zero)
        pair_hot = [
            jnp.where(from_all == jnp.full((), w, bf16), to_hot, zero) for w in range(count)
        ]
        return from_hot, to_hot, jnp.concatenate(pair_hot, axis=0)

    def one_molecule(half, m8):
        m = half * HALF + m8
        at = pl.multiple_of(m * z.edges, z.edges)
        base = (me * z.mols + m) * z.cap
        kept = jnp.where(group[m] == 1, masks[1], masks[0])
        feats_m = r.feats_v[:, pl.ds(at, z.edges)] * kept
        r.feats_v[:, pl.ds(at, z.edges)] = feats_m
        hidden = low(jnp.maximum(dot_tn(feats_m, w1_low) + b1_row, 0.0))
        hid[m] = hidden.T

        def line(ref):
            return jnp.concatenate(
                [ref[pl.ds(m * lines + t, 1), :] for t in range(lines)], axis=1
            )

        from_at = line(r.src_v) - base
        to_at = jnp.where(edge_at < edges[m], line(r.dst_v) - base, 2 * z.vpad)
        ends = jnp.concatenate([from_at, to_at, jnp.zeros((6, z.edges), jnp.int32)], axis=0)
        ends = ends.astype(f32)
        idx[m] = ends
        from_hot, to_hot, pair_hot = pair_hots(ends, z.cap)
        sums = low(dot(pair_hot, hidden))
        for w in range(z.cap):
            s2[half, m8 * z.vpad : (m8 + 1) * z.vpad, w * units : (w + 1) * units] = sums[
                w * z.vpad : (w + 1) * z.vpad
            ]
        found = dot(low(dot_nt(from_hot, to_hot)), tile_v)
        found = jnp.where(iota(found.shape, 1) // z.vpad == m8, found, 0.0)
        counts[half, :, m8 : m8 + 1, :] = found[: z.wpad].reshape(z.wpad, 1, z.half_lanes)

    def half_sums(half, carry):
        s2[half, :, z.cap * units :] = jnp.zeros((z.half_lanes, (z.wpad - z.cap) * units), bf16)
        for m8 in range(HALF):
            one_molecule(half, m8)
        r.cnt[half] = low(counts[half].reshape(z.half_rows, z.half_lanes))
        return carry

    lax.fori_loop(0, z.halves, half_sums, 0)
    if z.fused:
        for part in range(PARTS):
            forward_part(part)

    h, hb, hbw, hbw_t = r.h, r.hb, r.hbw, r.hbw_t
    for copy in (in_nodes, *in_perms):
        copy.wait()

    def set_rows(layer, half):
        hb[layer, half] = low(h[layer, half])
        hbw[layer, half] = low(dot_nt(r.perm[...], hb[layer, half]))
        hbw_t[layer, half] = low(dot_nt(hb[layer, half], r.perm[...]))

    def rows_in(value, target):
        moved = dot_tn(value, r.perm_in[...])
        for half in halves:
            target[half] = moved[:, half * z.half_lanes : (half + 1) * z.half_lanes]

    rows_in(r.nodes_v[...], h.at[0])
    for half in halves:
        set_rows(0, half)
    wib, whb, wit, wht, bcol = r.wib, r.whb, r.wit, r.wht, r.bcol
    in_b2.wait()
    b2_low = low(
        jnp.concatenate([r.b2_v[0:1, i * LANES : (i + 1) * LANES] for i in range(rows)], axis=0)
    )

    if not z.fused:
        in_w2.wait()

    t2, mt, gates = r.t2, r.mt, r.gates

    def two(at):
        return slice(at * 2 * units, (at + 1) * 2 * units)

    def wide(block):
        return jnp.concatenate([block] * (z.half_lanes // LANES), axis=1)

    def spread(layer, half, part):
        state = hbw[layer, half]

        def pair(at):
            ip = part * (some // 2) + at
            both = dot_nt(state, w2s[2 * ip : 2 * ip + 2].reshape(2 * units, width))
            at = ip * 2 * HALF
            for w in range(z.wpad):
                s = slice(w * HALF, (w + 1) * HALF)
                t2[layer, half, pl.ds(at, 2 * HALF), w * units : (w + 1) * units] = low(
                    jnp.concatenate([both[s, :units], both[s, units:]], axis=0)
                )

        for at in range(some // 2):
            pair(at)

    def messages(layer, half):
        state = hbw[layer, half]
        bias = dot(low(dot_nt(b2_low, state)), r.cnt[half])
        full = dot_nt(t2[layer, half], s2[half]).reshape(rows, HALF, z.half_lanes)
        full = jnp.where(half_mol[None], full + bias[:, None, :], 0.0)
        mt[layer, half, pl.ds(row_at, rows), :] = low(jnp.sum(full, axis=1))
        share(mt, r.m_send, r.m_recv, layer, half)

    def row_pushes(ref, send, recv, layer, half):
        mine = ref.at[layer, half, pl.ds(row_at, rows), :]
        return [
            remote(mine, mine, send.at[layer, half, at], recv.at[layer, half, row], ROW, peer)
            for at, peer in enumerate(row_peers)
        ]

    def share(*args):
        for copy in row_pushes(*args):
            copy.start()

    def collect(ref, send, recv, layer, half):
        for peer in row_peers:
            there = ref.at[layer, half, pl.ds(pl.multiple_of(peer * rows, rows), rows), :]
            arrived(there, send.at[layer, half, 0], recv.at[layer, half, peer], ROW, peer)

    def state_side(layer, half):
        gates[layer, half, 0] = dot(wht[...], hb[layer, half]) + wide(bcol[1])

    def gru(layer, half):
        collect(mt, r.m_send, r.m_recv, layer, half)
        from_msg = dot(wit[...], mt[layer, half]) + wide(bcol[0])
        from_state = gates[layer, half, 0]
        reset = jax.nn.sigmoid(from_msg[:width] + from_state[:width])
        update = jax.nn.sigmoid(from_msg[width : 2 * width] + from_state[width : 2 * width])
        new = jnp.tanh(from_msg[2 * width :] + reset * from_state[2 * width :])
        gates[layer, half, 1, :width] = reset
        gates[layer, half, 1, width : 2 * width] = update
        gates[layer, half, 1, 2 * width :] = new
        h[layer + 1, half] = r.live[half, 0:1] * ((1.0 - update) * new + update * h[layer, half])

    gt, dgi, dgh, dm, dmt, dmn = r.gt, r.dgi, r.dgh, r.dm, r.dmt, r.dmn
    d2, spart, sred = r.d2, r.spart, r.sred

    def gru_back(layer, half):
        up = gt[half] * r.live[half, 0:1]
        reset = gates[layer, half, 1, :width]
        update = gates[layer, half, 1, width : 2 * width]
        new = gates[layer, half, 1, 2 * width :]
        d_new = up * (1.0 - update) * (1.0 - new * new)
        d_update = up * (h[layer, half] - new) * update * (1.0 - update)
        d_reset = d_new * gates[layer, half, 0, 2 * width :] * reset * (1.0 - reset)
        msg_side = low(jnp.concatenate([d_reset, d_update, d_new], axis=0))
        dgi[layer, half] = msg_side
        dgh[layer, half, : 2 * width] = msg_side[: 2 * width]
        dgh[layer, half, 2 * width :] = low(d_new * reset)
        part = low(dot(wib[pl.ds(row_at, rows), :], msg_side))
        dm[layer, half] = part
        spread = jnp.where(half_mol[None], part.astype(f32)[:, None, :], 0.0)
        spread = spread.reshape(rows * HALF, z.half_lanes)
        dmt[layer, half] = low(spread)
        dmn[layer, half] = low(spread.T)
        gt[half] = up * update + dot(whb[...], dgh[layer, half])

    def gathered(layer, half):
        def pair(wp):
            lanes = two(wp)
            both = dot(dmt[layer, half], s2[half, :, lanes])
            at = wp * 2 * HALF
            for i in range(rows):
                part = both[i * HALF : (i + 1) * HALF]
                d2[pl.ds(at, 2 * HALF), i * units : (i + 1) * units] = low(
                    jnp.concatenate([part[:, :units], part[:, units:]], axis=0)
                )

        for wp in range(z.wpad // 2):
            pair(wp)

    def bias_rows(layer, half):
        return low(dot_nt(dm[layer, half], r.cnt[half]))

    def state_part(layer, half):
        biases = bias_rows(layer, half)
        r.ob_acc[...] += dot(biases, hbw[layer, half])
        back = dot(d2[...], w2s[...].reshape(rows * units, width)) + dot_tn(biases, b2_low)
        spart[layer, half] = low(dot_tn(low(back), r.perm[...]))
        for copy in part_pushes(layer, half):
            copy.start()

    def part_pushes(layer, half):
        return [
            remote(
                spart.at[layer, half, pl.ds(pl.multiple_of(peer * rows, rows), rows), :],
                r.rs_in.at[layer, half, row],
                r.rs_send.at[layer, half, at],
                r.rs_recv.at[layer, half, row],
                ROW,
                peer,
            )
            for at, peer in enumerate(row_peers)
        ]

    def state_sum(layer, half):
        total = spart[layer, half, pl.ds(row_at, rows), :].astype(f32)
        for peer in row_peers:
            there = r.rs_in.at[layer, half, peer]
            arrived(there, r.rs_send.at[layer, half, 0], r.rs_recv.at[layer, half, peer], ROW, peer)
            total = total + r.rs_in[layer, half, peer].astype(f32)
        sred[layer, half, pl.ds(row_at, rows), :] = low(total)
        share(sred, r.ag_send, r.ag_recv, layer, half)

    def settle():
        def one_step(t, carry):
            layer, half = lax.div(t, z.halves), lax.rem(t, z.halves)
            for copy in row_pushes(mt, r.m_send, r.m_recv, layer, half):
                copy.wait_send()
            for copy in part_pushes(layer, half):
                copy.wait_send()
            for copy in row_pushes(sred, r.ag_send, r.ag_recv, layer, half):
                copy.wait_send()
            return carry

        lax.fori_loop(0, LAYERS * z.halves, one_step, 0)
        for args in sent:
            remote(*args).wait_send()
        for copy in small_copies():
            copy.wait_send()
        if z.fused:
            for copy in pair_copies():
                copy.wait_send()
            for part in range(PARTS):
                for copy in forwards(part):
                    copy.wait_send()

    def rows_out(value):
        total = None
        for half in halves:
            rest = value(half)
            lanes = slice(half * z.half_lanes, (half + 1) * z.half_lanes)
            for _ in range(3):
                part = low(rest)
                rest = rest - part.astype(f32)
                moved = dot_nt(r.perm_in[:, lanes], part)
                total = moved if total is None else total + moved
        return total

    dwp, dw_acc, e2, e_acc = r.dwp, r.dw_acc, r.e2, r.e_acc

    def weight_grad(layer, half):
        for ip in range(rows // 2):
            at = two(ip)
            dw_acc[:, at] += dot(hbw_t[layer, half], d2[:, at])

    def pair_grad(layer, half):
        for wp in range(z.wpad // 2):
            at = two(wp)
            total = e_acc[half, :, at] + dot(dmn[layer, half], t2[layer, half, :, at])
            e_acc[half, :, at] = total
            e2[half, :, at] = low(total)

    def gate_weights():
        r.e_acc[...] = jnp.zeros(r.e_acc.shape, f32)
        r.dw_acc[...] = jnp.zeros(r.dw_acc.shape, f32)
        r.ob_acc[...] = jnp.zeros(r.ob_acc.shape, f32)
        in_wi.wait()
        in_wh.wait()
        wib[...] = low(r.wi_v[...])
        whb[...] = low(r.wh_v[...])
        wit[...] = low(r.wi_v[...].T)
        wht[...] = low(r.wh_v[...].T)
        in_cot.wait()
        in_bg.wait()
        bias_t = jnp.concatenate([r.bg_v[...], jnp.zeros((6, 3 * width), f32)], axis=0).T
        for side in range(2):
            bcol[side] = jnp.broadcast_to(bias_t[:, side : side + 1], (3 * width, LANES))
        rows_in(r.cot_v[...], r.gt)
        for half in halves:
            state_side(0, half)

    def forward_step(t, carry):
        layer, half = lax.div(t, z.halves), lax.rem(t, z.halves)

        @pl.when(layer > 0)
        def _():
            gru(layer - 1, half)
            set_rows(layer, half)

        for part in range(PARTS):
            if z.fused and part > 0:
                pl.when(t == 0)(functools.partial(whole_part, part))
            spread(layer, half, part)
        messages(layer, half)
        pl.when(t == z.halves - 1)(gate_weights)
        pl.when(layer > 0)(functools.partial(state_side, layer, half))
        return carry

    if z.fused:
        whole_part(0)
    lax.fori_loop(0, LAYERS * z.halves, forward_step, 0)

    last = LAYERS - 1

    ones = jnp.ones((8, z.lanes), bf16)

    def beside(ref, layer):
        return jnp.concatenate([ref[layer, half] for half in halves], axis=1)

    def gate_sums(layer):
        sums = []
        for at, (side, grads) in enumerate(((mt, dgi), (hb, dgh))):
            grads = beside(grads, layer)
            sums.append((dot_nt(beside(side, layer), grads), dot_nt(ones, grads)))
        return sums

    def back_half(layer, half):
        @pl.when(layer == last)
        def _():
            gru(last, half)

        @pl.when(layer < last)
        def _():
            collect(sred, r.ag_send, r.ag_recv, layer + 1, half)
            gt[half] += sred[layer + 1, half].astype(f32)

        gru_back(layer, half)
        gathered(layer, half)
        state_part(layer, half)
        weight_grad(layer, half)

    def pair_half(layer, half):
        pair_grad(layer, half)
        pl.when(layer == last)(functools.partial(state_sum, last, half))

    theirs, ours = [partner] + same_of_partner, [me] + same

    def pair_copies():
        return [
            remote(block_of(dwp, owner), r.dw_in.at[at], r.dw_send.at[at], r.dw_recv.at[at], MOL, partner)
            for at, owner in enumerate(theirs)
        ]

    def weight_out():
        for i in range(rows):
            dwp[i] = low(dw_acc[:, i * units : (i + 1) * units]).T
        if z.fused:
            for copy in pair_copies():
                copy.start()

    def backward_layer(t, carry):
        layer = last - t
        lax.fori_loop(0, z.halves, lambda half, c: back_half(layer, half) or c, 0)
        pl.when(layer == 0)(weight_out)
        lax.fori_loop(0, z.halves, lambda half, c: pair_half(layer, half) or c, 0)

        @pl.when(layer == last)
        def _():
            r.states_v[...] = rows_out(lambda half: h[LAYERS, half])
            store(r.states_v, o.states)
            for at, (weight, bias) in enumerate(gate_sums(last)):
                r.gate_acc[at], r.gate_bias_acc[at] = weight, bias

        return carry

    lax.fori_loop(0, LAYERS, backward_layer, 0)

    sm_part, sm_in = r.sm_part, r.sm_in
    bias_lines = []
    for at, (weight, bias) in enumerate(gate_sums(0)):
        weight, bias = weight + r.gate_acc[at], bias + r.gate_bias_acc[at]
        for third in range(3):
            first = (3 * at + third) * width
            sm_part[first : first + width, :] = low(weight[:, third * width : (third + 1) * width])
        bias_lines += [bias[0:1, third * width : (third + 1) * width] for third in range(3)]
    bias_lines.append(jnp.zeros((10, width), f32))
    sm_part[z.gate_rows : z.gate_rows + 16, :] = low(jnp.concatenate(bias_lines, axis=0))
    sm_part[z.gate_rows + 16 : z.small_rows, :] = low(r.ob_acc[...])
    if z.chunk * n_mol > z.small_rows:
        sm_part[z.small_rows :, :] = jnp.zeros((z.chunk * n_mol - z.small_rows, width), bf16)

    def chunk_of(ref, owner):
        return ref.at[pl.ds(pl.multiple_of(owner * z.chunk, 16), z.chunk), :]

    for at, peer in enumerate(mol_peers):
        push(chunk_of(sm_part, peer), sm_in.at[me], r.sm_send.at[at], r.sm_recv.at[me], MOL, peer)
    if z.fused:
        for at, owner in enumerate(ours):
            arrived(r.dw_in.at[at], r.dw_send.at[at], r.dw_recv.at[at], MOL, partner)
            own = dwp[:, pl.ds(pl.multiple_of(owner * per, 16), per), :].astype(f32)
            r.dw_mid[at] = low(own + r.dw_in[at].astype(f32))
            if at > 0:
                push(r.dw_mid.at[at], r.dw_in2.at[at], r.dw2_send.at[at], r.dw2_recv.at[at], MOL, owner)

    def small_copies():
        return [
            remote(r.sm_red, chunk_of(o.small_out, me), r.sa_send.at[at], r.sa_recv.at[me], MOL, peer)
            for at, peer in enumerate(mol_peers)
        ]

    def between():
        for half in halves:
            state_sum(0, half)

    def summed(pieces):
        return functools.reduce(jnp.add, pieces)

    def edge_grad(half, m8):
        m = half * HALF + m8
        at = pl.multiple_of(m * z.edges, z.edges)
        _, _, pair_hot = pair_hots(idx[m], z.wpad)
        slot = slice(m8 * z.vpad, (m8 + 1) * z.vpad)
        grads = [e2[half, slot, w * units : (w + 1) * units] for w in range(z.wpad)]
        d_hidden = dot_tn(jnp.concatenate(grads, axis=0), pair_hot)
        d_pre = low(jnp.where(hid[m].astype(f32) > 0.0, d_hidden, 0.0))
        feats_m = r.feats_v[:, pl.ds(at, z.edges)]
        feats_m = jnp.concatenate([feats_m, jnp.ones((16, z.edges), bf16)], axis=0)
        return dot_nt(d_pre, feats_m)

    def half_grad(half, total):
        total = total + summed([edge_grad(half, m8) for m8 in range(HALF)])
        pl.when(half == 0)(between)
        return total

    total = lax.fori_loop(0, z.halves, half_grad, jnp.zeros((units, z.feats + 16), f32))
    w1_part, w1_in, w1_mid = r.w1_part, r.w1_in, r.w1_mid
    total = jnp.concatenate([total, jnp.zeros((units, LANES - z.feats - 16), f32)], axis=1).T
    w1_part[...] = total[: z.feats + 8]
    for at, peer in enumerate(row_peers):
        push(w1_part, w1_in.at[row], r.wr_send.at[at], r.wr_recv.at[row], ROW, peer)
    w1_in[row] = w1_part[...]

    total = sm_part[pl.ds(pl.multiple_of(me * z.chunk, 16), z.chunk), :].astype(f32)
    for peer in mol_peers:
        arrived(sm_in.at[peer], r.sm_send.at[0], r.sm_recv.at[peer], MOL, peer)
        total = total + sm_in[peer].astype(f32)
    r.sm_red[...] = low(total)
    for copy in small_copies():
        copy.start()
    store(r.sm_red, chunk_of(o.small_out, me))
    for peer in row_peers:
        arrived(w1_in.at[peer], r.wr_send.at[0], r.wr_recv.at[peer], ROW, peer)
    total = w1_in[0]
    for at in range(1, n_row):
        total = total + w1_in[at]
    w1_mid[...] = total
    for at, peer in enumerate(mol_peers):
        push(w1_mid, o.w1_out.at[me], r.wm_send.at[at], r.wm_recv.at[me], MOL, peer)
    store(w1_mid, o.w1_out.at[me])

    for half in halves:
        collect(sred, r.ag_send, r.ag_recv, 0, half)
    r.state_grad_v[...] = rows_out(lambda half: gt[half] + sred[0, half].astype(f32))
    store(r.state_grad_v, o.state_grad)
    settle()
    if z.fused:
        total = r.dw_mid[0].astype(f32)
        for at in range(1, n_mol // 2):
            arrived(r.dw_in2.at[at], r.dw2_send.at[at], r.dw2_recv.at[at], MOL, partner)
            total = total + r.dw_in2[at].astype(f32)
        for i in range(rows):
            r.out_rows_v[:, i * LANES : (i + 1) * LANES] = total[i]
        store(r.out_rows_v, o.out_rows)
    else:
        store(dwp, o.out_rows)
    for peer in mol_peers:
        arrived(o.w1_out.at[peer], r.wm_send.at[0], r.wm_recv.at[peer], MOL, peer)
    for peer in mol_peers:
        arrived(chunk_of(o.small_out, peer), r.sa_send.at[0], r.sa_recv.at[peer], MOL, peer)
    for at, (source, target) in enumerate(stored):
        pltpu.make_async_copy(source, target, r.osem.at[at]).wait()


def run_step(z, args, w2_all):
    (node_states, edge_feats, edge_src, edge_dst, atom_counts, edge_counts, mol_group, col_mask,
     cotangent, edge_in_state, edge_in_bias_state, edge_out_state, edge_out_bias_state,
     gate_in_state, gate_hidden_state, gate_bias_state) = args
    any_spec = pl.BlockSpec(memory_space=pl.ANY)
    v = pltpu.VMEM
    dma = pltpu.SemaphoreType.DMA
    rows, width, units, per = z.rows, z.width, z.units, z.per
    n_mol, n_row, halves = z.n_mol, z.n_row, z.halves
    half_rows, half_lanes = z.half_rows, z.half_lanes
    both = (LAYERS, halves)
    full = rows * HALF
    lines = (z.mols * z.edges // LANES, LANES)
    step_in = (rows, per, LANES)
    lane = np.arange(z.lanes)
    lane_mol, lane_v = lane // z.vpad, lane % z.vpad
    node = np.where(lane_v < z.cap, lane_mol * z.cap + lane_v, -1)
    perm_in = (np.arange(z.nodes)[:, None] == node[None, :]).astype(np.float32)
    row_at = np.arange(half_rows)
    row_lane = (row_at % HALF) * z.vpad + row_at // HALF
    perm = (row_lane[:, None] == np.arange(half_lanes)[None, :]).astype(np.float32)
    operands = Operands(
        nodes=(node_states, any_spec),
        feats_t=(edge_feats.T, any_spec),
        src=(edge_src.reshape(lines), any_spec),
        dst=(edge_dst.reshape(lines), any_spec),
        atoms=(atom_counts, any_spec),
        edges=(edge_counts, any_spec),
        group=(mol_group, any_spec),
        col_mask=(col_mask, any_spec),
        cot=(cotangent, any_spec),
        w1=(edge_in_state, any_spec),
        b1=(edge_in_bias_state, any_spec),
        w2=(edge_out_state if z.fused else w2_all, any_spec),
        b2=(edge_out_bias_state, any_spec),
        wi=(gate_in_state, any_spec),
        wh=(gate_hidden_state, any_spec),
        bg=(gate_bias_state, any_spec),
        perm_in_c=(jnp.asarray(perm_in, bf16), any_spec),
        perm_c=(jnp.asarray(perm, bf16), any_spec),
    )
    outs = [
        jax.ShapeDtypeStruct((z.nodes, width), f32),
        jax.ShapeDtypeStruct((z.nodes, width), f32),
        jax.ShapeDtypeStruct((per, rows * width), f32)
        if z.fused
        else jax.ShapeDtypeStruct((rows, units, width), bf16),
        jax.ShapeDtypeStruct((n_mol * z.chunk, width), bf16),
        jax.ShapeDtypeStruct((n_mol, z.feats + 8, units), f32),
    ]
    row_sems = dma(both + (n_row,))
    mol_sems = dma((n_mol,))
    scratch = Scratch(
        nodes_v=v((z.nodes, width), bf16),
        feats_v=v((z.feats, z.mols * z.edges), bf16),
        src_v=v(lines, jnp.int32),
        dst_v=v(lines, jnp.int32),
        cot_v=v((z.nodes, width), bf16),
        w2_v=v((per, rows * width), f32),
        wi_v=v((width, 3 * width), f32),
        wh_v=v((width, 3 * width), f32),
        perm_in=v((z.nodes, z.lanes), bf16),
        perm=v((half_rows, half_lanes), bf16),
        w2s=v((rows, units, width), bf16),
        stage=v(step_in, bf16),
        hid=v((z.mols, units, z.edges), bf16),
        idx=v((z.mols, 8, z.edges), f32),
        s2=v((halves, half_lanes, z.span), bf16),
        counts=v((halves, z.wpad, HALF, half_lanes), f32),
        cnt=v((halves, half_rows, half_lanes), bf16),
        t2=v(both + (full, z.span), bf16),
        d2=v((half_rows, rows * units), bf16),
        e2=v((halves, half_lanes, z.span), bf16),
        e_acc=v((halves, half_lanes, z.span), f32),
        dw_acc=v((width, rows * units), f32),
        ob_acc=v((rows, width), f32),
        gate_acc=v((2, width, 3 * width), f32),
        gate_bias_acc=v((2, 8, 3 * width), f32),
        live=v((halves, 8, half_lanes), f32),
        h=v((LAYERS + 1, halves, width, half_lanes), f32),
        hb=v(both + (width, half_lanes), bf16),
        hbw=v(both + (half_rows, width), bf16),
        hbw_t=v(both + (width, half_rows), bf16),
        gates=v(both + (2, 3 * width, half_lanes), f32),
        mt=v(both + (width, half_lanes), bf16),
        dmt=v(both + (full, half_lanes), bf16),
        dmn=v(both + (half_lanes, full), bf16),
        dm=v(both + (rows, half_lanes), bf16),
        dgi=v(both + (3 * width, half_lanes), bf16),
        dgh=v(both + (3 * width, half_lanes), bf16),
        wib=v((width, 3 * width), bf16),
        whb=v((width, 3 * width), bf16),
        wit=v((3 * width, width), bf16),
        wht=v((3 * width, width), bf16),
        bcol=v((2, 3 * width, LANES), f32),
        gt=v((halves, width, half_lanes), f32),
        spart=v(both + (width, half_lanes), bf16),
        rs_in=v(both + (n_row, rows, half_lanes), bf16),
        sred=v(both + (width, half_lanes), bf16),
        dwp=v((rows, units, width), bf16),
        dw_in=v((n_mol // 2,) + step_in, bf16),
        dw_mid=v((n_mol // 2,) + step_in, bf16),
        dw_in2=v((n_mol // 2,) + step_in, bf16),
        sm_part=v((n_mol * z.chunk, width), bf16),
        sm_in=v((n_mol, z.chunk, width), bf16),
        sm_red=v((z.chunk, width), bf16),
        w1_part=v((z.feats + 8, units), f32),
        w1_in=v((n_row, z.feats + 8, units), f32),
        w1_mid=v((z.feats + 8, units), f32),
        col_mask_v=v(col_mask.shape, jnp.int32),
        w1_v=v(edge_in_state.shape[1:], f32),
        b1_v=v(edge_in_bias_state.shape, f32),
        bg_v=v(gate_bias_state.shape[1:], f32),
        b2_v=v(edge_out_bias_state.shape, f32),
        group_s=pltpu.SMEM(mol_group.shape, jnp.int32),
        edges_s=pltpu.SMEM(edge_counts.shape, jnp.int32),
        atoms_s=pltpu.SMEM(atom_counts.shape, jnp.int32),
        states_v=v((z.nodes, width), f32),
        state_grad_v=v((z.nodes, width), f32),
        out_rows_v=v((per, rows * width), f32),
        lsem=dma((len(operands),)),
        osem=dma((8,)),
        w2_send=dma((PARTS, n_mol)),
        w2_recv=dma((PARTS, n_mol)),
        w2_fsend=dma((PARTS, n_mol)),
        m_send=row_sems,
        m_recv=row_sems,
        rs_send=row_sems,
        rs_recv=row_sems,
        ag_send=row_sems,
        ag_recv=row_sems,
        dw_send=mol_sems,
        dw_recv=mol_sems,
        dw2_send=mol_sems,
        dw2_recv=mol_sems,
        sm_send=mol_sems,
        sm_recv=mol_sems,
        sa_send=mol_sems,
        sa_recv=mol_sems,
        wr_send=dma((n_row,)),
        wr_recv=dma((n_row,)),
        wm_send=mol_sems,
        wm_recv=mol_sems,
    )
    return pl.pallas_call(
        functools.partial(step_kernel, z),
        out_shape=outs,
        in_specs=[spec for _, spec in operands],
        out_specs=[any_spec] * len(outs),
        scratch_shapes=list(scratch),
        compiler_params=pltpu.CompilerParams(
            collective_id=0, has_side_effects=True, vmem_limit_bytes=VMEM_BYTES
        ),
        name="step",
    )(*[array for array, _ in operands])


def nesterov(state, grad, rate, out):
    scaled = rate * grad
    moment = momentum_coef * state[1] + scaled
    weight = state[0] - (scaled + momentum_coef * moment)
    out[0] = weight
    out[1] = moment
    out[2] = average_decay * state[2] + (1.0 - average_decay) * weight


def nesterov_line(state, grad, rate, out):
    scaled = rate * grad
    moment = momentum_coef * state[1:2, :] + scaled
    weight = state[0:1, :] - (scaled + momentum_coef * moment)
    out[0:1, :] = weight
    out[1:2, :] = moment
    out[2:3, :] = average_decay * state[2:3, :] + (1.0 - average_decay) * weight


class Update(NamedTuple):
    states: Any
    state_grad: Any
    out_rows: Any
    small: Any
    w1_sum: Any
    w1: Any
    b1: Any
    w2: Any
    b2: Any
    wi: Any
    wh: Any
    bg: Any


class Updated(NamedTuple):
    states: Any
    state_grad: Any
    w1_g: Any
    w1_n: Any
    b1_g: Any
    b1_n: Any
    w2_g: Any
    w2_n: Any
    b2_g: Any
    b2_n: Any
    wi_g: Any
    wi_n: Any
    wh_g: Any
    wh_n: Any
    bg_g: Any
    bg_n: Any


def update_kernel(z, rates, *refs):
    n_in, n_out = len(Update._fields), len(Updated._fields)
    given, out = Update(*refs[:n_in]), Updated(*refs[n_in : n_in + n_out])
    refs = refs[n_in + n_out :]
    here, new = Update(*refs[:n_in]), Updated(*refs[n_in : n_in + n_out])
    in_sem, out_sem = refs[n_in + n_out :]
    rate_in, rate_out, rate_gate = rates
    width = z.width
    sent = []

    def send(source, target):
        copy = pltpu.make_async_copy(source, target, out_sem.at[len(sent)])
        copy.start()
        sent.append(copy)

    fetched = Update(
        *[pltpu.make_async_copy(given[at], here[at], in_sem.at[at]) for at in range(n_in)]
    )
    order = (fetched.wi, fetched.small, fetched.wh, fetched.w2, fetched.out_rows)
    passed = (fetched.states, fetched.state_grad)
    rest = (fetched.bg, fetched.b2, fetched.w1, fetched.b1, fetched.w1_sum)
    for copy in order + passed + rest:
        copy.start()

    def thirds(at):
        parts = [here.small[(3 * at + t) * width : (3 * at + t + 1) * width, :] for t in range(3)]
        return jnp.concatenate(parts, axis=1).astype(f32)

    fetched.wi.wait()
    fetched.small.wait()
    total = thirds(0)
    new.wi_g[...] = total
    nesterov(here.wi, total, rate_gate, new.wi_n)
    send(new.wi_g, out.wi_g)
    send(new.wi_n, out.wi_n)
    fetched.wh.wait()
    total = thirds(1)
    new.wh_g[...] = total
    nesterov(here.wh, total, rate_gate, new.wh_n)
    send(new.wh_g, out.wh_g)
    send(new.wh_n, out.wh_n)
    fetched.w2.wait()
    fetched.out_rows.wait()
    send(here.out_rows, out.w2_g)
    nesterov(here.w2, here.out_rows[...], rate_out, new.w2_n)
    send(new.w2_n, out.w2_n)
    for copy in passed + rest:
        copy.wait()
    send(here.states, out.states)
    send(here.state_grad, out.state_grad)
    lines = here.small[z.gate_rows : z.gate_rows + 16, :].astype(f32)
    total = jnp.concatenate(
        [
            jnp.concatenate([lines[3 * side + t : 3 * side + t + 1, :] for t in range(3)], axis=1)
            for side in range(2)
        ],
        axis=0,
    )
    new.bg_g[...] = total
    nesterov(here.bg, total, rate_gate, new.bg_n)
    send(new.bg_g, out.bg_g)
    send(new.bg_n, out.bg_n)
    total = here.small[z.gate_rows + 16 : z.gate_rows + 16 + z.rows, :].astype(f32)
    new.b2_g[...] = total
    total = jnp.concatenate([total[i : i + 1, :] for i in range(z.rows)], axis=1)
    nesterov_line(here.b2, total, rate_out, new.b2_n)
    send(new.b2_g, out.b2_g)
    send(new.b2_n, out.b2_n)
    w1_sum = sum(here.w1_sum[at] for at in range(z.n_mol))
    total = w1_sum[: z.feats, :]
    new.w1_g[...] = total
    nesterov(here.w1, total, rate_in, new.w1_n)
    send(new.w1_g, out.w1_g)
    send(new.w1_n, out.w1_n)
    total = w1_sum[z.feats : z.feats + 1, :]
    new.b1_g[...] = total
    nesterov_line(here.b1, total, rate_in, new.b1_n)
    send(new.b1_g, out.b1_g)
    send(new.b1_n, out.b1_n)
    for copy in sent:
        copy.wait()


def per_device(mesh, *args):
    (node_states, edge_feats, edge_src, edge_dst, atom_counts, edge_counts, mol_group, col_mask,
     cotangent, edge_in_state, edge_in_bias_state, edge_out_state, edge_out_bias_state,
     gate_in_state, gate_hidden_state, gate_bias_state) = args
    z = Sizes(mesh, node_states, edge_feats, atom_counts, edge_in_state, edge_out_bias_state)
    w2_all = None
    if not z.fused:
        w2_all = lax.all_gather(low(edge_out_state[0]), "mol", axis=0, tiled=True)
        w2_all = w2_all.reshape(z.units, z.rows, z.width).swapaxes(0, 1)
    states, state_grad, out_rows, small, w1_sum = run_step(z, args, w2_all)
    if not z.fused:
        out_rows = out_rows.swapaxes(0, 1).reshape(z.units, z.rows * z.width)
        out_rows = lax.psum_scatter(out_rows, "mol", scatter_dimension=0, tiled=True).astype(f32)
    edges_all = edge_feats.shape[0] * z.n_mol
    nodes_all = z.nodes * z.n_mol
    rates = (
        z.feats ** (-0.5) / (0.2 * edges_all**0.5),
        (z.units * z.width * 8) ** (-0.5) / (0.4 * edges_all**0.5),
        z.width ** (-0.5) / (0.5 * nodes_all**0.5),
    )
    any_spec = pl.BlockSpec(memory_space=pl.ANY)
    operands = [
        states, state_grad, out_rows, small, w1_sum, edge_in_state, edge_in_bias_state,
        edge_out_state, edge_out_bias_state, gate_in_state, gate_hidden_state, gate_bias_state,
    ]
    outs = [
        states.shape, state_grad.shape, (z.feats, z.units), edge_in_state.shape,
        (1, z.units), edge_in_bias_state.shape, out_rows.shape, edge_out_state.shape,
        (z.rows, z.width), edge_out_bias_state.shape, (z.width, 3 * z.width), gate_in_state.shape,
        (z.width, 3 * z.width), gate_hidden_state.shape, (2, 3 * z.width), gate_bias_state.shape,
    ]
    results = pl.pallas_call(
        functools.partial(update_kernel, z, rates),
        out_shape=[jax.ShapeDtypeStruct(shape, f32) for shape in outs],
        in_specs=[any_spec] * len(operands),
        out_specs=[any_spec] * len(outs),
        scratch_shapes=[pltpu.VMEM(array.shape, array.dtype) for array in operands]
        + [pltpu.VMEM(shape, f32) for shape in outs]
        + [pltpu.SemaphoreType.DMA((len(operands),)), pltpu.SemaphoreType.DMA((len(outs),))],
        compiler_params=pltpu.CompilerParams(vmem_limit_bytes=VMEM_BYTES),
        name="update",
    )(*operands)
    results = list(results)
    results[4] = results[4].reshape(-1)
    results[8] = results[8].reshape(-1)
    return tuple(results)


def solution(mesh):
    return jax.shard_map(
        functools.partial(per_device, mesh),
        mesh=mesh,
        in_specs=(
            P(MOL, None),
            P(MOL, None),
            P(MOL),
            P(MOL),
            P(MOL),
            P(MOL),
            P(MOL),
            P(),
            P(MOL, None),
            P(),
            P(),
            P(None, MOL, ROW),
            P(None, ROW),
            P(),
            P(),
            P(),
        ),
        out_specs=(
            P(MOL, None),
            P(MOL, None),
            P(),
            P(),
            P(),
            P(),
            P(MOL, ROW),
            P(None, MOL, ROW),
            P(ROW),
            P(None, ROW),
            P(),
            P(),
            P(),
            P(),
            P(),
            P(),
        ),
        check_vma=False,
    )
```
